512 devices in a mesh: samp: 32 (over z_hi, y, core), pen: 16 (over x, z_lo).
Axes of the slice: x: 4, y: 8, z: 8 (z_hi: 2, z_lo: 4; z = z_hi * 4 + z_lo), core: 2. Of those that a mesh axis runs over, the one named last changes fastest.
Arguments:
- activations: bfloat16 [32, 96, 32, 1024], P('samp', None, 'pen'), may hold values from -6 to 6
- cotangent: bfloat16 [32, 96, 32, 1024], P('samp', None, 'pen'), may hold values from -6 to 6
- depth_kernels: float32 [3, 96, 9], replicated, may hold values from -5 to 5
- dilations: int32 [3], replicated, may hold values from 1 to 3
- expand_weight: bfloat16 [96, 384], replicated, may hold values from -0.625 to 0.625
- reduce_weight: bfloat16 [384, 96], replicated, may hold values from -0.3125 to 0.3125
Outputs:
- grad_input: bfloat16 [32, 96, 32, 1024], P('samp', None, 'pen')
- grad_expand: float32 [96, 384], P(None, 'pen')
- grad_reduce: float32 [384, 96], P('pen')
- grad_kernels: float32 [3, 96, 9], replicated
The draws below stay inside these ranges and needn't reach their ends.
All inputs are finite; a program needn't handle non-finite values.
Results may differ from the reference program's by a relative error of at most 0.0085.
Values may be sent and summed in bfloat16 or wider, within the bound.
No kernel may reach another device: no remote copies, remote signals or barrier semaphores. Data moves between devices by JAX's collectives and lax.ppermute only.
A program may use at most 64 MiB of HBM per device.

```python
import math
import jax
import jax.numpy as jnp
from jax import lax

C = 96
H = 384
L = 32
TAPS = 9
SAMPLES = 32


def block_scale(key, dims, shards, low, high):
    def one(axis_at, parts):
        steps = jax.random.uniform(jax.random.fold_in(jax.random.fold_in(key, 6), axis_at), (parts,), jnp.float32, low / len(shards), high / len(shards))
        return jnp.repeat(jnp.exp(steps), dims[axis_at] // parts).reshape((-1,) + (1,) * (len(dims) - axis_at - 1))

    gain = one(*shards[0])
    for cut in shards[1:]:
        gain = gain * one(*cut)
    return gain


def scatter_about(own_key, dims, spread, limit, cuts=(), dtype=jnp.bfloat16):
    values = jax.random.normal(own_key, dims, jnp.float32) * spread
    if len(cuts) > 0:
        values = block_scale(own_key, dims, cuts, -0.22, 0.18) * values
    return jnp.clip(values, min=-limit, max=limit).astype(dtype)


def setup_inputs(seed: int = 0) -> dict:
    key_of = jax.random.split(jax.random.key(seed), 7)
    activations = scatter_about(key_of[0], (SAMPLES, C, L, L * L), 1.0, 6.0, ((0, 32), (2, 16)))
    cotangent = scatter_about(key_of[1], (SAMPLES, C, L, L * L), 1.0, 6.0, ((0, 32), (2, 16)))
    depth_kernels = scatter_about(key_of[2], (3, C, TAPS), 0.35, 5.0, (), jnp.float32)
    dilations = jax.random.randint(key_of[3], (3,), 1, 4).astype(jnp.int32)
    expand_weight = scatter_about(key_of[4], (C, H), C ** -0.5, 0.625)
    reduce_weight = scatter_about(key_of[5], (H, C), H ** -0.5, 0.3125)
    return dict(activations=activations, cotangent=cotangent, depth_kernels=depth_kernels, dilations=dilations, expand_weight=expand_weight, reduce_weight=reduce_weight)


def settle(values):
    return lax.optimization_barrier(values.astype(jnp.bfloat16)).astype(jnp.float32)

def taps_apply(field, kernel_rows, spacing, direction, sign):
    shape = [1] * field.ndim
    shape[0] = kernel_rows.shape[0]
    total = jnp.zeros(field.shape, jnp.float32)
    for tap_index in range(TAPS):
        weight_col = kernel_rows[:, tap_index].reshape(shape)
        total = total + weight_col * jnp.roll(field, sign * (tap_index - 4) * spacing, direction)
    return total

def taps_grad(upstream, field, spacing, direction):
    columns = []
    for tap_index in range(TAPS):
        moved = jnp.roll(field, -(tap_index - 4) * spacing, direction)
        columns.append(lax.optimization_barrier(jnp.sum(upstream * moved, axis=(1, 2, 3))))
    return jnp.stack(columns, axis=-1)

def reference(activations, cotangent, depth_kernels, dilations, expand_weight, reduce_weight):

    def per_sample(carry, pair):
        sum_expand, sum_reduce, sum_kernels = carry
        sample_in, sample_cot = pair
        lattice = sample_in.reshape(C, L, L, L).astype(jnp.float32)
        first = settle(taps_apply(lattice, depth_kernels[0], dilations[0], 1, -1))
        second = settle(taps_apply(first, depth_kernels[1], dilations[1], 2, -1))
        mixed = taps_apply(second, depth_kernels[2], dilations[2], 3, -1).astype(jnp.bfloat16)
        mixed_flat = mixed.reshape(C, L * L * L)
        cot_flat = sample_cot.reshape(C, L * L * L)
        pre = jnp.dot(expand_weight.T, mixed_flat, preferred_element_type=jnp.float32)
        hidden = jax.nn.gelu(pre, approximate=True).astype(jnp.bfloat16)
        d_hidden = jnp.dot(reduce_weight, cot_flat, preferred_element_type=jnp.float32)
        pullback = jax.vjp(lambda values: jax.nn.gelu(values, approximate=True), pre)[1]
        d_pre = pullback(d_hidden)[0].astype(jnp.bfloat16)
        sum_reduce = sum_reduce + jnp.dot(hidden, cot_flat.T, preferred_element_type=jnp.float32)
        sum_expand = sum_expand + jnp.dot(mixed_flat, d_pre.T, preferred_element_type=jnp.float32)
        d_mixed = jnp.dot(expand_weight, d_pre, preferred_element_type=jnp.float32)
        d_mixed = settle(d_mixed).reshape(C, L, L, L)
        d_second = settle(taps_apply(d_mixed, depth_kernels[2], dilations[2], 3, 1))
        d_first = settle(taps_apply(d_second, depth_kernels[1], dilations[1], 2, 1))
        d_conv = settle(taps_apply(d_first, depth_kernels[0], dilations[0], 1, 1))
        kernel_terms = jnp.stack([taps_grad(d_first, lattice, dilations[0], 1), taps_grad(d_second, first, dilations[1], 2), taps_grad(d_mixed, second, dilations[2], 3)])
        sum_kernels = sum_kernels + kernel_terms
        result = (sample_cot.astype(jnp.float32) + d_conv.reshape(C, L, L * L)).astype(jnp.bfloat16)
        return ((sum_expand, sum_reduce, sum_kernels), result)
    start = (jnp.zeros((C, H), jnp.float32), jnp.zeros((H, C), jnp.float32), jnp.zeros((3, C, TAPS), jnp.float32))
    totals, grad_input = lax.scan(per_sample, start, (activations, cotangent))
    norm_scale = 1.0 / math.sqrt(SAMPLES * L * L * L)
    return (grad_input, totals[0] * norm_scale, totals[1] * norm_scale, totals[2] * norm_scale)
```

```python
import math

import jax
import jax.numpy as jnp
import numpy as np
from jax import lax
from jax.experimental import pallas as pl
from jax.experimental.pallas import tpu as pltpu
from jax.sharding import Mesh
from jax.sharding import PartitionSpec as P

C = 96
H = 384
L = 32
TAPS = 9
GROUPS = 16
CH = C // GROUPS
ROWS = C * L * L * 2 // 128
STRIDE = 16
HALO = 16
F32 = jnp.float32
BF16 = jnp.bfloat16
SAMP = ("zh", "y", "core")


def delta_table():
    r = np.arange(256)
    plane, rest = r // 128, r % 128
    x, c = 2 * (rest // CH) + plane, rest % CH
    valid = rest < C
    delta = (x[:, None] - x[None, :]) % L
    same = (c[:, None] == c[None, :]) & valid[:, None] & valid[None, :]
    return np.where(same, delta, -1).astype(np.int32)


def channel_table():
    r = np.arange(256) % 128
    out = np.zeros((8, 256), np.float32)
    for c in range(CH):
        out[c] = (r % CH == c) & (r < C)
    return out


def contract(a, b, da, db):
    return lax.dot_general(a, b, (((da,), (db,)), ((), ())), preferred_element_type=F32)


def pieces(stage, j, p):
    return stage[pl.ds(2 * j + p, C, stride=STRIDE), :]


def for_each_dilation(spacing):
    def run(body):
        for d in (1, 2, 3):
            @pl.when(spacing == d)
            def _():
                @pl.loop(0, L)
                def _(y):
                    body(d, y)
    return run


def conv_fwd(dil, a_ref, coef, delta, mixed_ref, first_ref, second_ref, field_ref, hi_ref, lo_ref,
             stage, fir, sec, mix):
    d0, d1, d2 = dil[0], dil[1], dil[2]
    stage[...] = a_ref[...].astype(F32)
    m = jnp.zeros((256, 256), F32)
    for t in range(TAPS):
        m = m + jnp.where(delta[...] == (((t - 4) * d0) & (L - 1)), coef[t:t + 1, :], 0.0)
    hi = m.astype(BF16)
    lo = (m - hi.astype(F32)).astype(BF16)
    hi_ref[...] = hi
    lo_ref[...] = lo
    eye = jnp.where(delta[...] == 0, 1.0, 0.0).astype(BF16)
    gap = jnp.zeros((32, 128), F32)
    for j in range(8):
        parts = []
        for p in range(2):
            parts += [pieces(stage, j, p), gap]
        f = jnp.concatenate(parts, axis=0).astype(BF16)
        field_ref[:, j * 128:(j + 1) * 128] = f
        out = contract(f, hi, 0, 0) + contract(f, lo, 0, 0)
        out = out.astype(BF16)
        first_ref[j * 128:(j + 1) * 128, :] = out
        fir[4 * j:4 * j + 4] = out.astype(F32).reshape(4, L, 256)

    @pl.loop(0, L)
    def _(y):
        acc = jnp.zeros((L, 256), F32)
        for t in range(TAPS):
            acc = acc + coef[16 + t:17 + t, :] * fir[(y + (t - 4) * d1) & (L - 1)]
        acc = acc.astype(BF16)
        second_ref[pl.ds(pl.multiple_of(y * L, L), L), :] = acc
        acc = acc.astype(F32)
        sec[y, HALO:HALO + L, :] = acc
        sec[y, 0:HALO, :] = acc[L - HALO:, :]
        sec[y, HALO + L:, :] = acc[:HALO, :]

    @for_each_dilation(d2)
    def _(d, y):
        acc = jnp.zeros((L, 256), F32)
        for t in range(TAPS):
            at = HALO + (t - 4) * d
            acc = acc + coef[32 + t:33 + t, :] * sec[y, at:at + L, :]
        mix[pl.ds(pl.multiple_of(y * L, L), L), :] = acc.astype(BF16)

    for j in range(8):
        turned = contract(eye, mix[j * 128:(j + 1) * 128, :], 1, 1)
        for p in range(2):
            stage[pl.ds(2 * j + p, C, stride=STRIDE), :] = turned[p * 128:p * 128 + C, :]
    mixed_ref[...] = stage[...].astype(BF16)


def conv_bwd(dil, d_ref, coef, delta, table, first_ref, second_ref, field_ref, hi_ref, lo_ref,
             out_ref, kern_ref, stage, dmh, dse, dfi, acc_ref):
    d0, d1, d2 = dil[0], dil[1], dil[2]
    stage[...] = d_ref[...].astype(F32)
    acc_ref[...] = jnp.zeros_like(acc_ref)
    eye = jnp.where(delta[...] == 0, 1.0, 0.0).astype(BF16)
    gap = jnp.zeros((32, 128), F32)
    for j in range(8):
        parts = []
        for p in range(2):
            parts += [pieces(stage, j, p), gap]
        f = jnp.concatenate(parts, axis=0).astype(BF16)
        out = contract(f, eye, 0, 0).reshape(4, L, 256)
        dmh[4 * j:4 * j + 4, HALO:HALO + L, :] = out
        dmh[4 * j:4 * j + 4, 0:HALO, :] = out[:, L - HALO:, :]
        dmh[4 * j:4 * j + 4, HALO + L:, :] = out[:, :HALO, :]

    def fold(v):
        return v[0:8] + v[8:16] + v[16:24] + v[24:32]

    @for_each_dilation(d2)
    def _(d, y):
        row = pl.ds(pl.multiple_of(y * L, L), L)
        field = second_ref[row, :].astype(F32)
        acc = jnp.zeros((L, 256), F32)
        for t in range(TAPS):
            at = HALO - (t - 4) * d
            moved = dmh[y, at:at + L, :]
            acc = acc + coef[32 + t:33 + t, :] * moved
            acc_ref[18 + t] += fold(moved * field)
        dse[y] = acc.astype(BF16).astype(F32)

    @pl.loop(0, L)
    def _(y):
        row = pl.ds(pl.multiple_of(y * L, L), L)
        field = first_ref[row, :].astype(F32)
        acc = jnp.zeros((L, 256), F32)
        for t in range(TAPS):
            moved = dse[(y - (t - 4) * d1) & (L - 1)]
            acc = acc + coef[16 + t:17 + t, :] * moved
            acc_ref[9 + t] += fold(moved * field)
        dfi[row, :] = acc.astype(BF16)

    hi, lo = hi_ref[...], lo_ref[...]
    for j in range(8):
        block = dfi[j * 128:(j + 1) * 128, :]
        out = contract(hi, block, 1, 1) + contract(lo, block, 1, 1)
        for p in range(2):
            stage[pl.ds(2 * j + p, C, stride=STRIDE), :] = out[p * 128:p * 128 + C, :]
    out_ref[...] = stage[...].astype(BF16)
    cross = contract(field_ref[...], dfi[...], 1, 0)
    for t in range(TAPS):
        keep = jnp.where(delta[...] == (((t - 4) * d0) & (L - 1)), cross, 0.0)
        acc_ref[t] = jnp.sum(keep.reshape(32, 8, 256), axis=0)
    sums = jnp.sum(acc_ref[...], axis=1)
    kern_ref[...] = jnp.zeros_like(kern_ref)
    kern_ref[:, 0:32] = lax.dot_general(
        table[...], sums, (((1,), (1,)), ((), ())),
        precision=lax.Precision.HIGHEST, preferred_element_type=F32)


BLOCK = 256


def middle(m_ref, c_ref, we, wr, out_ref, expand_ref, reduce_ref, stage, stage_c, mix, cot):
    stage[...] = m_ref[...].astype(F32)
    stage_c[...] = c_ref[...].astype(F32)
    for j in range(8):
        for p in range(2):
            k = 2 * j + p
            mix[:, k * 128:(k + 1) * 128] = pieces(stage, j, p).astype(BF16)
            cot[:, k * 128:(k + 1) * 128] = pieces(stage_c, j, p).astype(BF16)
    expand_ref[...] = jnp.zeros_like(expand_ref)
    reduce_ref[...] = jnp.zeros_like(reduce_ref)
    root = math.sqrt(2.0 / math.pi)

    for b in range(2 * L * L // BLOCK):
        cols = slice(b * BLOCK, (b + 1) * BLOCK)
        mb, cb = mix[:, cols], cot[:, cols]
        pre = contract(we[...], mb, 0, 0)
        d_hidden = contract(wr[...], cb, 1, 0)
        square = pre * pre
        inner = root * pre * (1.0 + 0.044715 * square)
        half = 0.5 + 0.5 * jnp.tanh(inner)
        hidden = (pre * half).astype(BF16)
        slope = half + pre * (2.0 * half * (1.0 - half)) * (root * (1.0 + 3.0 * 0.044715 * square))
        d_pre = (d_hidden * slope).astype(BF16)
        reduce_ref[...] += contract(hidden, cb, 1, 1)
        expand_ref[...] += contract(d_pre, mb, 1, 1)
        out = contract(we[...], d_pre, 1, 0)
        for i in range(BLOCK // 128):
            k = b * (BLOCK // 128) + i
            stage[pl.ds(k, C, stride=STRIDE), :] = out[:, i * 128:(i + 1) * 128]
    out_ref[...] = stage[...].astype(BF16)


VMEM = pl.BlockSpec(memory_space=pltpu.VMEM)
SMEM = pl.BlockSpec(memory_space=pltpu.SMEM)
PARAMS = pltpu.CompilerParams(vmem_limit_bytes=28 * 1024 * 1024)


def shape(*dims, dtype=BF16):
    return jax.ShapeDtypeStruct(dims, dtype)


def run_conv_fwd(dilations, rows, coef, delta):
    return pl.pallas_call(
        conv_fwd,
        out_shape=(shape(ROWS, 128), shape(1024, 256), shape(1024, 256), shape(256, 1024),
                   shape(256, 256), shape(256, 256)),
        in_specs=[SMEM, VMEM, VMEM, VMEM],
        out_specs=(VMEM,) * 6,
        scratch_shapes=[pltpu.VMEM((ROWS, 128), F32), pltpu.VMEM((L, L, 256), F32),
                        pltpu.VMEM((L, L + 2 * HALO, 256), F32), pltpu.VMEM((1024, 256), BF16)],
        compiler_params=PARAMS,
        cost_estimate=pl.CostEstimate(flops=10**9, bytes_accessed=4 * 10**6, transcendentals=0),
        name="conv_fwd",
    )(dilations, rows, coef, delta)


def run_conv_bwd(dilations, rows, coef, delta, table, first, second, field, hi, lo):
    return pl.pallas_call(
        conv_bwd,
        out_shape=(shape(ROWS, 128), shape(8, 128, dtype=F32)),
        in_specs=[SMEM] + [VMEM] * 9,
        out_specs=(VMEM,) * 2,
        scratch_shapes=[pltpu.VMEM((ROWS, 128), F32), pltpu.VMEM((L, L + 2 * HALO, 256), F32),
                        pltpu.VMEM((L, L, 256), F32), pltpu.VMEM((1024, 256), BF16),
                        pltpu.VMEM((32, 8, 256), F32)],
        compiler_params=PARAMS,
        cost_estimate=pl.CostEstimate(flops=10**9, bytes_accessed=4 * 10**6, transcendentals=0),
        name="conv_bwd",
    )(dilations, rows, coef, delta, table, first, second, field, hi, lo)


def run_middle(rows, cot_rows, expand_weight, reduce_weight):
    return pl.pallas_call(
        middle,
        out_shape=(shape(ROWS, 128), shape(H, C, dtype=F32), shape(H, C, dtype=F32)),
        in_specs=[VMEM] * 4,
        out_specs=(VMEM,) * 3,
        scratch_shapes=[pltpu.VMEM((ROWS, 128), F32), pltpu.VMEM((ROWS, 128), F32),
                        pltpu.VMEM((C, 2048), BF16), pltpu.VMEM((C, 2048), BF16)],
        compiler_params=PARAMS,
        cost_estimate=pl.CostEstimate(flops=10**9, bytes_accessed=4 * 10**6, transcendentals=10**6),
        name="middle",
    )(rows, cot_rows, expand_weight, reduce_weight)


def to_rows(field):
    return field.reshape(C, 2, 8, 128).transpose(0, 2, 1, 3).reshape(ROWS, 128)


def from_rows(rows):
    return rows.reshape(C, 8, 2, 128).transpose(0, 2, 1, 3).reshape(1, C, 2, 1024)


def swap(rows):
    parts = rows.reshape(GROUPS, ROWS // GROUPS, 128)
    return lax.all_to_all(parts, "pen", 0, 0, tiled=True).reshape(ROWS, 128)


def sum_over(values, axes, size):
    copies = jnp.broadcast_to(values[None], (size,) + values.shape)
    return jnp.sum(lax.all_to_all(copies, axes, 0, 0, tiled=True), axis=0)


def per_device(activations, cotangent, depth_kernels, dilations, expand_weight, reduce_weight):
    delta = jnp.asarray(delta_table())
    table = jnp.asarray(channel_table())
    own = lax.dynamic_slice_in_dim(depth_kernels, lax.axis_index("pen") * CH, CH, 1)
    coef = jnp.tile(own.transpose(0, 2, 1), (1, 1, GROUPS))
    coef = jnp.pad(coef, ((0, 0), (0, 16 - TAPS), (0, 128 - C)))
    coef = jnp.concatenate([coef, coef], axis=2).reshape(48, 256)

    lines = swap(to_rows(activations))
    mixed, first, second, field, hi, lo = run_conv_fwd(dilations, lines, coef, delta)
    cot_rows = to_rows(cotangent)
    d_mixed, part_expand, part_reduce = run_middle(
        swap(mixed), cot_rows, expand_weight, reduce_weight)
    d_lines = swap(d_mixed)
    weights = jnp.concatenate(
        [part_expand.reshape(GROUPS, 24, C), part_reduce.reshape(GROUPS, 24, C)], axis=1)
    weights = lax.all_to_all(weights.astype(BF16), "pen", 0, 0, tiled=True)
    weights = jnp.sum(weights.astype(F32), axis=0)
    d_conv, kern = run_conv_bwd(
        dilations, d_lines, coef, delta, table, first, second, field, hi, lo)
    total = jnp.concatenate([jnp.pad(weights, ((0, 0), (0, 128 - C))), kern], axis=0)
    total = sum_over(total, "y", lax.axis_size("y"))
    total = sum_over(total, ("zh", "core"), lax.axis_size("zh") * lax.axis_size("core"))
    d_input = swap(d_conv)
    grad_input = from_rows((cot_rows.astype(F32) + d_input.astype(F32)).astype(BF16))

    samples = lax.axis_size("zh") * lax.axis_size("y") * lax.axis_size("core")
    total = total * (1.0 / math.sqrt(samples * L * L * L))
    own_expand = total[0:24, 0:C].T
    own_reduce = total[24:48, 0:C]
    kern = jnp.broadcast_to(total[None, 48:56, :], (GROUPS, 8, 128))
    kern = lax.all_to_all(kern, "pen", 0, 0, tiled=True)
    kern = kern[:, :CH, :3 * TAPS].reshape(C, 3, TAPS).transpose(1, 0, 2)
    return grad_input, own_expand, own_reduce, kern


def solution(mesh):
    samp = mesh.devices.shape[0]
    split = (2, samp // 4, 2) if samp % 4 == 0 else (1, samp, 1)
    fine = Mesh(mesh.devices.reshape(*split, GROUPS), (*SAMP, "pen"))
    field = P(SAMP, None, "pen", None)
    return jax.shard_map(
        per_device,
        mesh=fine,
        in_specs=(field, field, P(), P(), P(), P()),
        out_specs=(field, P(None, "pen"), P("pen", None), P()),
        check_vma=False,
    )
```

```python
import math

import jax
import jax.numpy as jnp
import numpy as np
from jax import lax
from jax.experimental import pallas as pl
from jax.experimental.pallas import tpu as pltpu
from jax.sharding import Mesh
from jax.sharding import PartitionSpec as P

C = 96
H = 384
L = 32
TAPS = 9
GROUPS = 16
CH = C // GROUPS
ROWS = C * L * L * 2 // 128
STRIDE = 16
PIECE = ROWS // GROUPS
BH = H // GROUPS
EXTRA_W = 2 * BH
EXTRA_K = 16
HALO = 16
F32 = jnp.float32
BF16 = jnp.bfloat16
SAMP = ("zh", "y", "core")


def delta_table():
    r = np.arange(256)
    plane, rest = r // 128, r % 128
    x, c = 2 * (rest // CH) + plane, rest % CH
    valid = rest < C
    delta = (x[:, None] - x[None, :]) % L
    same = (c[:, None] == c[None, :]) & valid[:, None] & valid[None, :]
    return np.where(same, delta, -1).astype(np.int32)


def channel_table():
    r = np.arange(256) % 128
    out = np.zeros((8, 256), np.float32)
    for c in range(CH):
        out[c] = (r % CH == c) & (r < C)
    return out


def contract(a, b, da, db):
    return lax.dot_general(a, b, (((da,), (db,)), ((), ())), preferred_element_type=F32)


def pieces(stage, j, p):
    return stage[pl.ds(2 * j + p, C, stride=STRIDE), :]


def for_each_dilation(spacing):
    def run(body):
        for d in (1, 2, 3):
            @pl.when(spacing == d)
            def _():
                @pl.loop(0, L)
                def _(y):
                    body(d, y)
    return run


def conv_fwd(dil, a_ref, coef, delta, mixed_ref, first_ref, second_ref, field_ref, hi_ref, lo_ref,
             stage, fir, sec, mix):
    d0, d1, d2 = dil[0], dil[1], dil[2]
    stage[...] = a_ref[...].astype(F32)
    m = jnp.zeros((256, 256), F32)
    for t in range(TAPS):
        m = m + jnp.where(delta[...] == (((t - 4) * d0) & (L - 1)), coef[t:t + 1, :], 0.0)
    hi = m.astype(BF16)
    lo = (m - hi.astype(F32)).astype(BF16)
    hi_ref[...] = hi
    lo_ref[...] = lo
    eye = jnp.where(delta[...] == 0, 1.0, 0.0).astype(BF16)
    gap = jnp.zeros((32, 128), F32)
    for j in range(8):
        parts = []
        for p in range(2):
            parts += [pieces(stage, j, p), gap]
        f = jnp.concatenate(parts, axis=0).astype(BF16)
        field_ref[:, j * 128:(j + 1) * 128] = f
        out = contract(f, hi, 0, 0) + contract(f, lo, 0, 0)
        out = out.astype(BF16)
        first_ref[j * 128:(j + 1) * 128, :] = out
        fir[4 * j:4 * j + 4] = out.astype(F32).reshape(4, L, 256)

    @pl.loop(0, L)
    def _(y):
        acc = jnp.zeros((L, 256), F32)
        for t in range(TAPS):
            acc = acc + coef[16 + t:17 + t, :] * fir[(y + (t - 4) * d1) & (L - 1)]
        acc = acc.astype(BF16)
        second_ref[pl.ds(pl.multiple_of(y * L, L), L), :] = acc
        acc = acc.astype(F32)
        sec[y, HALO:HALO + L, :] = acc
        sec[y, 0:HALO, :] = acc[L - HALO:, :]
        sec[y, HALO + L:, :] = acc[:HALO, :]

    @for_each_dilation(d2)
    def _(d, y):
        acc = jnp.zeros((L, 256), F32)
        for t in range(TAPS):
            at = HALO + (t - 4) * d
            acc = acc + coef[32 + t:33 + t, :] * sec[y, at:at + L, :]
        mix[pl.ds(pl.multiple_of(y * L, L), L), :] = acc.astype(BF16)

    for j in range(8):
        turned = contract(eye, mix[j * 128:(j + 1) * 128, :], 1, 1)
        for p in range(2):
            stage[pl.ds(2 * j + p, C, stride=STRIDE), :] = turned[p * 128:p * 128 + C, :]
    mixed_ref[...] = stage[...].astype(BF16)


def conv_bwd(dil, d_ref, coef, delta, table, first_ref, second_ref, field_ref, hi_ref, lo_ref,
             out_ref, weight_ref, stage, dmh, dse, dfi, acc_ref):
    d0, d1, d2 = dil[0], dil[1], dil[2]
    weights = jnp.zeros((EXTRA_W, 128), F32)
    for g in range(GROUPS):
        stage[g * PIECE:(g + 1) * PIECE, :] = d_ref[g, 0:PIECE, :].astype(F32)
        weights = weights + d_ref[g, PIECE:PIECE + EXTRA_W, :].astype(F32)
    weight_ref[...] = weights
    acc_ref[...] = jnp.zeros_like(acc_ref)
    eye = jnp.where(delta[...] == 0, 1.0, 0.0).astype(BF16)
    gap = jnp.zeros((32, 128), F32)
    for j in range(8):
        parts = []
        for p in range(2):
            parts += [pieces(stage, j, p), gap]
        f = jnp.concatenate(parts, axis=0).astype(BF16)
        out = contract(f, eye, 0, 0).reshape(4, L, 256)
        dmh[4 * j:4 * j + 4, HALO:HALO + L, :] = out
        dmh[4 * j:4 * j + 4, 0:HALO, :] = out[:, L - HALO:, :]
        dmh[4 * j:4 * j + 4, HALO + L:, :] = out[:, :HALO, :]

    def fold(v):
        return v[0:8] + v[8:16] + v[16:24] + v[24:32]

    @for_each_dilation(d2)
    def _(d, y):
        row = pl.ds(pl.multiple_of(y * L, L), L)
        field = second_ref[row, :].astype(F32)
        acc = jnp.zeros((L, 256), F32)
        for t in range(TAPS):
            at = HALO - (t - 4) * d
            moved = dmh[y, at:at + L, :]
            acc = acc + coef[32 + t:33 + t, :] * moved
            acc_ref[18 + t] += fold(moved * field)
        dse[y] = acc.astype(BF16).astype(F32)

    @pl.loop(0, L)
    def _(y):
        row = pl.ds(pl.multiple_of(y * L, L), L)
        field = first_ref[row, :].astype(F32)
        acc = jnp.zeros((L, 256), F32)
        for t in range(TAPS):
            moved = dse[(y - (t - 4) * d1) & (L - 1)]
            acc = acc + coef[16 + t:17 + t, :] * moved
            acc_ref[9 + t] += fold(moved * field)
        dfi[row, :] = acc.astype(BF16)

    hi, lo = hi_ref[...], lo_ref[...]
    for j in range(8):
        block = dfi[j * 128:(j + 1) * 128, :]
        out = contract(hi, block, 1, 1) + contract(lo, block, 1, 1)
        for p in range(2):
            stage[pl.ds(2 * j + p, C, stride=STRIDE), :] = out[p * 128:p * 128 + C, :]
    cross = contract(field_ref[...], dfi[...], 1, 0)
    for t in range(TAPS):
        keep = jnp.where(delta[...] == (((t - 4) * d0) & (L - 1)), cross, 0.0)
        acc_ref[t] = jnp.sum(keep.reshape(32, 8, 256), axis=0)
    sums = jnp.sum(acc_ref[...], axis=1)
    kern = lax.dot_general(
        table[...], sums, (((1,), (1,)), ((), ())),
        precision=lax.Precision.HIGHEST, preferred_element_type=F32)
    lane = lax.broadcasted_iota(jnp.int32, (8, 128), 1)
    kern = jnp.concatenate([kern] * 4, axis=1)
    kern = jnp.where(lane // 32 == dil[3], kern, 0.0)
    high = kern.astype(BF16).astype(F32)
    extra = jnp.concatenate([high, kern - high], axis=0).astype(BF16)
    for g in range(GROUPS):
        out_ref[g, 0:PIECE, :] = stage[g * PIECE:(g + 1) * PIECE, :].astype(BF16)
        out_ref[g, PIECE:PIECE + EXTRA_K, :] = extra


BLOCK = 256


def middle(m_ref, c_ref, we, wr, out_ref, stage, stage_c, mix, cot, expand_ref, reduce_ref):
    stage[...] = m_ref[...].astype(F32)
    stage_c[...] = c_ref[...].astype(F32)
    for j in range(8):
        for p in range(2):
            k = 2 * j + p
            mix[:, k * 128:(k + 1) * 128] = pieces(stage, j, p).astype(BF16)
            cot[:, k * 128:(k + 1) * 128] = pieces(stage_c, j, p).astype(BF16)
    expand_ref[...] = jnp.zeros_like(expand_ref)
    reduce_ref[...] = jnp.zeros_like(reduce_ref)
    root = math.sqrt(2.0 / math.pi)

    for b in range(2 * L * L // BLOCK):
        cols = slice(b * BLOCK, (b + 1) * BLOCK)
        mb, cb = mix[:, cols], cot[:, cols]
        pre = contract(we[...], mb, 0, 0)
        d_hidden = contract(wr[...], cb, 1, 0)
        square = pre * pre
        inner = root * pre * (1.0 + 0.044715 * square)
        half = 0.5 + 0.5 * jnp.tanh(inner)
        hidden = (pre * half).astype(BF16)
        slope = half + pre * (2.0 * half * (1.0 - half)) * (root * (1.0 + 3.0 * 0.044715 * square))
        d_pre = (d_hidden * slope).astype(BF16)
        reduce_ref[...] += contract(hidden, cb, 1, 1)
        expand_ref[...] += contract(d_pre, mb, 1, 1)
        out = contract(we[...], d_pre, 1, 0)
        for i in range(BLOCK // 128):
            k = b * (BLOCK // 128) + i
            stage[pl.ds(k, C, stride=STRIDE), :] = out[:, i * 128:(i + 1) * 128]
    gap = jnp.zeros((EXTRA_W, 128 - C), F32)
    for g in range(GROUPS):
        own = slice(g * BH, (g + 1) * BH)
        terms = jnp.concatenate([expand_ref[own, :], reduce_ref[own, :]], axis=0)
        out_ref[g, 0:PIECE, :] = stage[g * PIECE:(g + 1) * PIECE, :].astype(BF16)
        out_ref[g, PIECE:PIECE + EXTRA_W, :] = jnp.concatenate([terms, gap], axis=1).astype(BF16)


VMEM = pl.BlockSpec(memory_space=pltpu.VMEM)
SMEM = pl.BlockSpec(memory_space=pltpu.SMEM)
PARAMS = pltpu.CompilerParams(vmem_limit_bytes=28 * 1024 * 1024)


def shape(*dims, dtype=BF16):
    return jax.ShapeDtypeStruct(dims, dtype)


def run_conv_fwd(dilations, rows, coef, delta):
    return pl.pallas_call(
        conv_fwd,
        out_shape=(shape(ROWS, 128), shape(1024, 256), shape(1024, 256), shape(256, 1024),
                   shape(256, 256), shape(256, 256)),
        in_specs=[SMEM, VMEM, VMEM, VMEM],
        out_specs=(VMEM,) * 6,
        scratch_shapes=[pltpu.VMEM((ROWS, 128), F32), pltpu.VMEM((L, L, 256), F32),
                        pltpu.VMEM((L, L + 2 * HALO, 256), F32), pltpu.VMEM((1024, 256), BF16)],
        compiler_params=PARAMS,
        cost_estimate=pl.CostEstimate(flops=10**9, bytes_accessed=4 * 10**6, transcendentals=0),
        name="conv_fwd",
    )(dilations, rows, coef, delta)


def run_conv_bwd(dilations, rows, coef, delta, table, first, second, field, hi, lo):
    return pl.pallas_call(
        conv_bwd,
        out_shape=(shape(GROUPS, PIECE + EXTRA_K, 128), shape(EXTRA_W, 128, dtype=F32)),
        in_specs=[SMEM] + [VMEM] * 9,
        out_specs=(VMEM,) * 2,
        scratch_shapes=[pltpu.VMEM((ROWS, 128), F32), pltpu.VMEM((L, L + 2 * HALO, 256), F32),
                        pltpu.VMEM((L, L, 256), F32), pltpu.VMEM((1024, 256), BF16),
                        pltpu.VMEM((32, 8, 256), F32)],
        compiler_params=PARAMS,
        cost_estimate=pl.CostEstimate(flops=10**9, bytes_accessed=4 * 10**6, transcendentals=0),
        name="conv_bwd",
    )(dilations, rows, coef, delta, table, first, second, field, hi, lo)


def run_middle(rows, cot_rows, expand_weight, reduce_weight):
    return pl.pallas_call(
        middle,
        out_shape=shape(GROUPS, PIECE + EXTRA_W, 128),
        in_specs=[VMEM] * 4,
        out_specs=VMEM,
        scratch_shapes=[pltpu.VMEM((ROWS, 128), F32), pltpu.VMEM((ROWS, 128), F32),
                        pltpu.VMEM((C, 2048), BF16), pltpu.VMEM((C, 2048), BF16),
                        pltpu.VMEM((H, C), F32), pltpu.VMEM((H, C), F32)],
        compiler_params=PARAMS,
        cost_estimate=pl.CostEstimate(flops=10**9, bytes_accessed=4 * 10**6, transcendentals=10**6),
        name="middle",
    )(rows, cot_rows, expand_weight, reduce_weight)


def to_rows(field):
    return field.reshape(C, 2, 8, 128).transpose(0, 2, 1, 3).reshape(ROWS, 128)


def from_rows(rows):
    return rows.reshape(C, 8, 2, 128).transpose(0, 2, 1, 3).reshape(1, C, 2, 1024)


def swap(parts):
    return lax.all_to_all(parts, "pen", 0, 0, tiled=True)


def sum_over_samples(terms):
    half = terms.shape[0] // 2
    zh, y = lax.axis_size("zh"), lax.axis_size("y")
    cores = lax.axis_size("core")
    if cores == 1:
        parts = jnp.broadcast_to(terms.astype(BF16)[None], (zh * y,) + terms.shape)
        return jnp.sum(lax.all_to_all(parts, SAMP, 0, 0, tiled=True).astype(F32), axis=0)
    parts = terms.astype(BF16).reshape(1, 2, half, 128)
    parts = jnp.broadcast_to(parts, (zh * y, 2, half, 128)).reshape(zh * y * 2, half, 128)
    mine = jnp.sum(lax.all_to_all(parts, SAMP, 0, 0, tiled=True).astype(F32), axis=0)
    other = lax.ppermute(mine, "core", [(0, 1), (1, 0)])
    first = lax.axis_index("core") == 0
    return jnp.concatenate([jnp.where(first, mine, other), jnp.where(first, other, mine)], axis=0)


def per_device(activations, cotangent, depth_kernels, dilations, expand_weight, reduce_weight):
    delta = jnp.asarray(delta_table())
    table = jnp.asarray(channel_table())
    own = lax.dynamic_slice_in_dim(depth_kernels, lax.axis_index("pen") * CH, CH, 1)
    coef = jnp.tile(own.transpose(0, 2, 1), (1, 1, GROUPS))
    coef = jnp.pad(coef, ((0, 0), (0, 16 - TAPS), (0, 128 - C)))
    coef = jnp.concatenate([coef, coef], axis=2).reshape(48, 256)

    group = lax.axis_index("pen").astype(jnp.int32)
    scalars = jnp.concatenate([dilations, jnp.mod(group, 4)[None]])
    lines = swap(to_rows(activations).reshape(GROUPS, PIECE, 128)).reshape(ROWS, 128)
    mixed, first, second, field, hi, lo = run_conv_fwd(scalars, lines, coef, delta)
    cot_rows = to_rows(cotangent)
    mixed = swap(mixed.reshape(GROUPS, PIECE, 128)).reshape(ROWS, 128)
    d_lines = swap(run_middle(mixed, cot_rows, expand_weight, reduce_weight))
    d_conv, weights = run_conv_bwd(
        scalars, d_lines, coef, delta, table, first, second, field, hi, lo)
    arrived = swap(d_conv)

    kern = arrived[:, PIECE:, :].astype(F32).reshape(4, 4, 2, 8, 128)
    kern = jnp.sum(kern, axis=(1, 2)).reshape(32, 128)
    total = sum_over_samples(jnp.concatenate([weights, kern], axis=0))
    d_input = arrived[:, :PIECE, :].reshape(ROWS, 128)
    grad_input = from_rows((cot_rows.astype(F32) + d_input.astype(F32)).astype(BF16))

    samples = lax.axis_size("zh") * lax.axis_size("y") * lax.axis_size("core")
    total = total * (1.0 / math.sqrt(samples * L * L * L))
    own_expand = total[0:BH, 0:C].T
    own_reduce = total[BH:EXTRA_W, 0:C]
    kern = total[EXTRA_W:].reshape(4, 8, 4, 32)[:, :CH, :, :3 * TAPS]
    kern = kern.transpose(0, 2, 1, 3).reshape(C, 3, TAPS).transpose(1, 0, 2)
    return grad_input, own_expand, own_reduce, kern


def solution(mesh):
    samp = mesh.devices.shape[0]
    split = (2, samp // 4, 2) if samp % 4 == 0 else (1, samp, 1)
    fine = Mesh(mesh.devices.reshape(*split, GROUPS), (*SAMP, "pen"))
    field = P(SAMP, None, "pen", None)
    return jax.shard_map(
        per_device,
        mesh=fine,
        in_specs=(field, field, P(), P(), P(), P()),
        out_specs=(field, P(None, "pen"), P("pen", None), P()),
        check_vma=False,
    )
```

```python
import math

import jax
import jax.numpy as jnp
import numpy as np
from jax import lax
from jax.experimental import pallas as pl
from jax.experimental.pallas import tpu as pltpu
from jax.sharding import Mesh
from jax.sharding import PartitionSpec as P

C = 96
H = 384
L = 32
TAPS = 9
GROUPS = 16
CH = C // GROUPS
ROWS = C * L * L * 2 // 128
STRIDE = 16
PIECE = ROWS // GROUPS
BH = H // GROUPS
EXTRA_W = 2 * BH
HALO = 16
F32 = jnp.float32
BF16 = jnp.bfloat16
SAMP = ("zh", "y", "core")


def delta_table():
    r = np.arange(256)
    plane, rest = r // 128, r % 128
    x, c = 2 * (rest // CH) + plane, rest % CH
    valid = rest < C
    delta = (x[:, None] - x[None, :]) % L
    same = (c[:, None] == c[None, :]) & valid[:, None] & valid[None, :]
    return np.where(same, delta, -1).astype(np.int32)


def channel_table():
    r = np.arange(128)
    out = np.zeros((8, 128), np.float32)
    for c in range(CH):
        out[c] = (r % CH == c) & (r < C)
    return out


def contract(a, b, da, db):
    return lax.dot_general(a, b, (((da,), (db,)), ((), ())), preferred_element_type=F32)


def pieces(stage, j, p):
    return stage[pl.ds(2 * j + p, C, stride=STRIDE), :]


def spread(coef, base):
    return [jnp.broadcast_to(coef[base + t:base + t + 1, :], (8, 128)) for t in range(TAPS)]


def tiles(v):
    return v.reshape(4, 8, 128)


def load_field(stage, j):
    gap = jnp.zeros((128 - C, 128), F32)
    parts = []
    for p in range(2):
        parts += [pieces(stage, j, p), gap]
    return jnp.concatenate(parts, axis=0).astype(BF16)


def put_halo(ref, p, y, v):
    ref[p, y, HALO:HALO + L, :] = v
    ref[p, y, 0:HALO, :] = v[L - HALO:, :]
    ref[p, y, HALO + L:, :] = v[:HALO, :]


def conv_fwd(dil, a_ref, coef, delta, wide, mixed_ref, first_ref, second_ref, field_ref, hi_ref,
             lo_ref, stage, fir, sec, mix):
    d0, d1, d2 = dil[0], dil[1], dil[2]
    stage[...] = a_ref[...].astype(F32)
    m = jnp.zeros((256, 256), F32)
    for t in range(TAPS):
        m = m + jnp.where(delta[...] == (((t - 4) * d0) & (L - 1)), wide[t:t + 1, :], 0.0)
    hi = m.astype(BF16)
    lo = (m - hi.astype(F32)).astype(BF16)
    hi_ref[...] = hi
    lo_ref[...] = lo
    eye = jnp.where(delta[...] == 0, 1.0, 0.0).astype(BF16)
    for j in range(8):
        f = load_field(stage, j)
        field_ref[:, j * 128:(j + 1) * 128] = f
        out = (contract(f, hi, 0, 0) + contract(f, lo, 0, 0)).astype(BF16)
        for p in range(2):
            half = out[:, p * 128:(p + 1) * 128]
            first_ref[p, j * 128:(j + 1) * 128, :] = half
            fir[p, 4 * j:4 * j + 4] = half.astype(F32).reshape(4, L, 128)

    taps = spread(coef, 16)

    @pl.loop(0, L)
    def _(y):
        row = pl.ds(pl.multiple_of(y * L, L), L)
        for p in range(2):
            acc = jnp.zeros((4, 8, 128), F32)
            for t in range(TAPS):
                acc = acc + taps[t] * tiles(fir[p, (y + (t - 4) * d1) & (L - 1)])
            acc = acc.reshape(L, 128).astype(BF16)
            second_ref[p, row, :] = acc
            put_halo(sec, p, y, acc.astype(F32))

    taps_z = spread(coef, 32)

    @pl.loop(0, L)
    def _(y):
        row = pl.ds(pl.multiple_of(y * L, L), L)
        for p in range(2):
            acc = jnp.zeros((4, 8, 128), F32)
            for t in range(TAPS):
                acc = acc + taps_z[t] * tiles(sec[p, y, pl.ds(HALO + (t - 4) * d2, L), :])
            mix[row, p * 128:(p + 1) * 128] = acc.reshape(L, 128).astype(BF16)

    for j in range(8):
        turned = contract(eye, mix[j * 128:(j + 1) * 128, :], 1, 1)
        for p in range(2):
            stage[pl.ds(2 * j + p, C, stride=STRIDE), :] = turned[p * 128:p * 128 + C, :]
    mixed_ref[...] = stage[...].astype(BF16)


def conv_bwd(dil, d_ref, coef, delta, table, first_ref, second_ref, field_ref, hi_ref, lo_ref,
             out_ref, sums_ref, stage, dmh, dse, dfi, acc_ref):
    d0, d1, d2 = dil[0], dil[1], dil[2]
    weights = jnp.zeros((EXTRA_W, 128), F32)
    for g in range(GROUPS):
        stage[g * PIECE:(g + 1) * PIECE, :] = d_ref[g, 0:PIECE, :].astype(F32)
        weights = weights + d_ref[g, PIECE:PIECE + EXTRA_W, :].astype(F32)
    sums_ref[0:EXTRA_W, :] = weights
    eye = jnp.where(delta[...] == 0, 1.0, 0.0).astype(BF16)
    for j in range(8):
        out = contract(load_field(stage, j), eye, 0, 0)
        for p in range(2):
            for i in range(4):
                put_halo(dmh, p, 4 * j + i, out[i * L:(i + 1) * L, p * 128:(p + 1) * 128])

    def fold(v):
        return (v[0] + v[1]) + (v[2] + v[3])

    taps_z = spread(coef, 32)
    empty = (jnp.zeros((8, 128), F32),) * TAPS

    def along_z(y, sums):
        row = pl.ds(pl.multiple_of(y * L, L), L)
        sums = list(sums)
        for p in range(2):
            field = tiles(second_ref[p, row, :].astype(F32))
            acc = jnp.zeros((4, 8, 128), F32)
            for t in range(TAPS):
                moved = tiles(dmh[p, y, pl.ds(HALO - (t - 4) * d2, L), :])
                acc = acc + taps_z[t] * moved
                sums[t] = sums[t] + fold(moved * field)
            dse[p, y] = acc.reshape(L, 128).astype(BF16).astype(F32)
        return tuple(sums)

    sums = lax.fori_loop(0, L, along_z, empty)
    for t in range(TAPS):
        acc_ref[18 + t] = sums[t]
    taps = spread(coef, 16)

    def along_y(y, sums):
        row = pl.ds(pl.multiple_of(y * L, L), L)
        sums = list(sums)
        for p in range(2):
            field = tiles(first_ref[p, row, :].astype(F32))
            acc = jnp.zeros((4, 8, 128), F32)
            for t in range(TAPS):
                moved = tiles(dse[p, (y - (t - 4) * d1) & (L - 1)])
                acc = acc + taps[t] * moved
                sums[t] = sums[t] + fold(moved * field)
            dfi[row, p * 128:(p + 1) * 128] = acc.reshape(L, 128).astype(BF16)
        return tuple(sums)

    sums = lax.fori_loop(0, L, along_y, empty)
    for t in range(TAPS):
        acc_ref[9 + t] = sums[t]
    for t in range(27, 32):
        acc_ref[t] = jnp.zeros((8, 128), F32)

    hi, lo = hi_ref[...], lo_ref[...]
    for j in range(8):
        block = dfi[j * 128:(j + 1) * 128, :]
        out = contract(hi, block, 1, 1) + contract(lo, block, 1, 1)
        for p in range(2):
            stage[pl.ds(2 * j + p, C, stride=STRIDE), :] = out[p * 128:p * 128 + C, :]
    cross = contract(field_ref[...], dfi[...], 1, 0)
    for t in range(TAPS):
        keep = jnp.where(delta[...] == (((t - 4) * d0) & (L - 1)), cross, 0.0)
        keep = jnp.sum(keep.reshape(32, 8, 256), axis=0)
        acc_ref[t] = keep[:, :128] + keep[:, 128:]
    sums_ref[EXTRA_W:EXTRA_W + 8, :] = jnp.zeros((8, 128), F32)
    sums_ref[EXTRA_W:EXTRA_W + 8, 0:32] = lax.dot_general(
        table[...], jnp.sum(acc_ref[...], axis=1), (((1,), (1,)), ((), ())),
        precision=lax.Precision.HIGHEST, preferred_element_type=F32)
    out_ref[...] = stage[...].astype(BF16)


BLOCK = 256


def middle(m_ref, c_ref, we, wr, out_ref, stage, stage_c, mix, cot, expand_ref, reduce_ref):
    stage[...] = m_ref[...].astype(F32)
    stage_c[...] = c_ref[...].astype(F32)
    for j in range(8):
        for p in range(2):
            k = 2 * j + p
            mix[:, k * 128:(k + 1) * 128] = pieces(stage, j, p).astype(BF16)
            cot[:, k * 128:(k + 1) * 128] = pieces(stage_c, j, p).astype(BF16)
    expand_ref[...] = jnp.zeros_like(expand_ref)
    reduce_ref[...] = jnp.zeros_like(reduce_ref)
    root = math.sqrt(2.0 / math.pi)

    for b in range(2 * L * L // BLOCK):
        cols = slice(b * BLOCK, (b + 1) * BLOCK)
        mb, cb = mix[:, cols], cot[:, cols]
        pre = contract(we[...], mb, 0, 0)
        d_hidden = contract(wr[...], cb, 1, 0)
        square = pre * pre
        inner = root * pre * (1.0 + 0.044715 * square)
        half = 0.5 + 0.5 * jnp.tanh(inner)
        hidden = (pre * half).astype(BF16)
        slope = half + pre * (2.0 * half * (1.0 - half)) * (root * (1.0 + 3.0 * 0.044715 * square))
        d_pre = (d_hidden * slope).astype(BF16)
        reduce_ref[...] += contract(hidden, cb, 1, 1)
        expand_ref[...] += contract(d_pre, mb, 1, 1)
        out = contract(we[...], d_pre, 1, 0)
        for i in range(BLOCK // 128):
            k = b * (BLOCK // 128) + i
            stage[pl.ds(k, C, stride=STRIDE), :] = out[:, i * 128:(i + 1) * 128]
    gap = jnp.zeros((EXTRA_W, 128 - C), F32)
    for g in range(GROUPS):
        own = slice(g * BH, (g + 1) * BH)
        terms = jnp.concatenate([expand_ref[own, :], reduce_ref[own, :]], axis=0)
        out_ref[g, 0:PIECE, :] = stage[g * PIECE:(g + 1) * PIECE, :].astype(BF16)
        out_ref[g, PIECE:PIECE + EXTRA_W, :] = jnp.concatenate([terms, gap], axis=1).astype(BF16)


VMEM = pl.BlockSpec(memory_space=pltpu.VMEM)
SMEM = pl.BlockSpec(memory_space=pltpu.SMEM)
PARAMS = pltpu.CompilerParams(vmem_limit_bytes=28 * 1024 * 1024)


def shape(*dims, dtype=BF16):
    return jax.ShapeDtypeStruct(dims, dtype)


def run_conv_fwd(dilations, rows, coef, delta, wide):
    return pl.pallas_call(
        conv_fwd,
        out_shape=(shape(ROWS, 128), shape(2, 1024, 128), shape(2, 1024, 128), shape(256, 1024),
                   shape(256, 256), shape(256, 256)),
        in_specs=[SMEM] + [VMEM] * 4,
        out_specs=(VMEM,) * 6,
        scratch_shapes=[pltpu.VMEM((ROWS, 128), F32), pltpu.VMEM((2, L, L, 128), F32),
                        pltpu.VMEM((2, L, L + 2 * HALO, 128), F32), pltpu.VMEM((1024, 256), BF16)],
        compiler_params=PARAMS,
        cost_estimate=pl.CostEstimate(flops=10**9, bytes_accessed=4 * 10**6, transcendentals=0),
        name="conv_fwd",
    )(dilations, rows, coef, delta, wide)


def run_conv_bwd(dilations, rows, coef, delta, table, first, second, field, hi, lo):
    return pl.pallas_call(
        conv_bwd,
        out_shape=(shape(ROWS, 128), shape(EXTRA_W + 8, 128, dtype=F32)),
        in_specs=[SMEM] + [VMEM] * 9,
        out_specs=(VMEM,) * 2,
        scratch_shapes=[pltpu.VMEM((ROWS, 128), F32),
                        pltpu.VMEM((2, L, L + 2 * HALO, 128), F32),
                        pltpu.VMEM((2, L, L, 128), F32), pltpu.VMEM((1024, 256), BF16),
                        pltpu.VMEM((32, 8, 128), F32)],
        compiler_params=PARAMS,
        cost_estimate=pl.CostEstimate(flops=10**9, bytes_accessed=4 * 10**6, transcendentals=0),
        name="conv_bwd",
    )(dilations, rows, coef, delta, table, first, second, field, hi, lo)


def run_middle(rows, cot_rows, expand_weight, reduce_weight):
    return pl.pallas_call(
        middle,
        out_shape=shape(GROUPS, PIECE + EXTRA_W, 128),
        in_specs=[VMEM] * 4,
        out_specs=VMEM,
        scratch_shapes=[pltpu.VMEM((ROWS, 128), F32), pltpu.VMEM((ROWS, 128), F32),
                        pltpu.VMEM((C, 2048), BF16), pltpu.VMEM((C, 2048), BF16),
                        pltpu.VMEM((H, C), F32), pltpu.VMEM((H, C), F32)],
        compiler_params=PARAMS,
        cost_estimate=pl.CostEstimate(flops=10**9, bytes_accessed=4 * 10**6, transcendentals=10**6),
        name="middle",
    )(rows, cot_rows, expand_weight, reduce_weight)


def to_rows(field):
    return field.reshape(C, 2, 8, 128).transpose(0, 2, 1, 3).reshape(ROWS, 128)


def from_rows(rows):
    return rows.reshape(C, 8, 2, 128).transpose(0, 2, 1, 3).reshape(1, C, 2, 1024)


def swap(parts):
    return lax.all_to_all(parts, "pen", 0, 0, tiled=True)


def sum_over_partners(terms):
    total = terms
    if lax.axis_size("zh") == 2:
        flips = [[(0, 2), (1, 3), (2, 0), (3, 1)], [(0, 3), (1, 2), (2, 1), (3, 0)],
                 [(0, 1), (1, 0), (2, 3), (3, 2)]]
        for flip in flips:
            total = total + lax.ppermute(terms, ("zh", "core"), flip)
    return total


def sum_over_y(terms):
    size = lax.axis_size("y")
    parts = jnp.broadcast_to(terms.astype(BF16)[None], (size,) + terms.shape)
    return jnp.sum(lax.all_to_all(parts, "y", 0, 0, tiled=True).astype(F32), axis=0)


def per_device(activations, cotangent, depth_kernels, dilations, expand_weight, reduce_weight):
    delta = jnp.asarray(delta_table())
    table = jnp.asarray(channel_table())
    own = lax.dynamic_slice_in_dim(depth_kernels, lax.axis_index("pen") * CH, CH, 1)
    coef = jnp.tile(own.transpose(0, 2, 1), (1, 1, GROUPS))
    coef = jnp.pad(coef, ((0, 0), (0, 16 - TAPS), (0, 128 - C))).reshape(48, 128)
    wide = jnp.concatenate([coef[0:16], coef[0:16]], axis=1)

    lines = swap(to_rows(activations).reshape(GROUPS, PIECE, 128)).reshape(ROWS, 128)
    mixed, first, second, field, hi, lo = run_conv_fwd(dilations, lines, coef, delta, wide)
    cot_rows = to_rows(cotangent)
    mixed = swap(mixed.reshape(GROUPS, PIECE, 128)).reshape(ROWS, 128)
    d_lines = swap(run_middle(mixed, cot_rows, expand_weight, reduce_weight))
    d_conv, sums = run_conv_bwd(
        dilations, d_lines, coef, delta, table, first, second, field, hi, lo)
    d_input = swap(d_conv.reshape(GROUPS, PIECE, 128)).reshape(ROWS, 128)
    sums = sum_over_partners(sums)
    sums, d_input = lax.optimization_barrier((sums, d_input))
    sums = sum_over_y(sums)
    grad_input = from_rows((cot_rows.astype(F32) + d_input.astype(F32)).astype(BF16))

    samples = lax.axis_size("zh") * lax.axis_size("y") * lax.axis_size("core")
    sums = sums * (1.0 / math.sqrt(samples * L * L * L))
    kern = jnp.broadcast_to(sums[None, EXTRA_W:, :], (GROUPS, 8, 128))
    kern = swap(kern)[:, :CH, :3 * TAPS].reshape(C, 3, TAPS).transpose(1, 0, 2)
    own_expand = sums[0:BH, 0:C].T
    own_reduce = sums[BH:EXTRA_W, 0:C]
    return grad_input, own_expand, own_reduce, kern


def solution(mesh):
    samp = mesh.devices.shape[0]
    split = (2, samp // 4, 2) if samp % 4 == 0 else (1, samp, 1)
    fine = Mesh(mesh.devices.reshape(*split, GROUPS), (*SAMP, "pen"))
    field = P(SAMP, None, "pen", None)
    return jax.shard_map(
        per_device,
        mesh=fine,
        in_specs=(field, field, P(), P(), P(), P()),
        out_specs=(field, P(None, "pen"), P("pen", None), P()),
        check_vma=False,
    )
```

```python
import math

import jax
import jax.numpy as jnp
import numpy as np
from jax import lax
from jax.experimental import pallas as pl
from jax.experimental.pallas import tpu as pltpu
from jax.sharding import Mesh
from jax.sharding import PartitionSpec as P

C = 96
H = 384
L = 32
TAPS = 9
GROUPS = 16
CH = C // GROUPS
ROWS = C * L * L * 2 // 128
STRIDE = 16
PIECE = ROWS // GROUPS
BH = H // GROUPS
EXTRA_W = 2 * BH
EXTRA_K = 16
HALO = 16
F32 = jnp.float32
BF16 = jnp.bfloat16
SAMP = ("zh", "y", "core")


def delta_table():
    r = np.arange(256)
    plane, rest = r // 128, r % 128
    x, c = 2 * (rest // CH) + plane, rest % CH
    valid = rest < C
    delta = (x[:, None] - x[None, :]) % L
    same = (c[:, None] == c[None, :]) & valid[:, None] & valid[None, :]
    return np.where(same, delta, -1).astype(np.int32)


def contract(a, b, da, db):
    return lax.dot_general(a, b, (((da,), (db,)), ((), ())), preferred_element_type=F32)


def pieces(stage, j, p):
    return stage[pl.ds(2 * j + p, C, stride=STRIDE), :]


def spread(coef, base):
    return [jnp.broadcast_to(coef[base + t:base + t + 1, :], (8, 128)) for t in range(TAPS)]


def tiles(v):
    return v.reshape(4, 8, 128)


def load_field(stage, j):
    gap = jnp.zeros((128 - C, 128), F32)
    parts = []
    for p in range(2):
        parts += [pieces(stage, j, p), gap]
    return jnp.concatenate(parts, axis=0).astype(BF16)


def put_halo(ref, p, y, v):
    ref[p, y, HALO:HALO + L, :] = v
    ref[p, y, 0:HALO, :] = v[L - HALO:, :]
    ref[p, y, HALO + L:, :] = v[:HALO, :]


def prepare(dil, coef, delta, hi_ref, lo_ref, eye_ref):
    spacing = dil[0]
    for half in range(2):
        cols = slice(half * 128, (half + 1) * 128)
        table = delta[:, cols]
        m = jnp.zeros((256, 128), F32)
        for t in range(TAPS):
            m = m + jnp.where(table == (((t - 4) * spacing) & (L - 1)), coef[t:t + 1, :], 0.0)
        hi = m.astype(BF16)
        hi_ref[:, cols] = hi
        lo_ref[:, cols] = (m - hi.astype(F32)).astype(BF16)
        eye_ref[:, cols] = jnp.where(table == 0, 1.0, 0.0).astype(BF16)


def conv_fwd(dil, a_ref, coef, hi_ref, lo_ref, eye_ref, mixed_ref, first_ref, second_ref,
             field_ref, stage, fir, sec, mix):
    d1, d2 = dil[1], dil[2]
    stage[...] = a_ref[...].astype(F32)
    hi, lo, eye = hi_ref[...], lo_ref[...], eye_ref[...]
    for j in range(8):
        f = load_field(stage, j)
        field_ref[:, j * 128:(j + 1) * 128] = f
        out = (contract(f, hi, 0, 0) + contract(f, lo, 0, 0)).astype(BF16)
        for p in range(2):
            half = out[:, p * 128:(p + 1) * 128]
            first_ref[p, j * 128:(j + 1) * 128, :] = half
            fir[p, 4 * j:4 * j + 4] = half.astype(F32).reshape(4, L, 128)

    taps = spread(coef, 16)

    @pl.loop(0, L)
    def _(y):
        row = pl.ds(pl.multiple_of(y * L, L), L)
        for p in range(2):
            acc = jnp.zeros((4, 8, 128), F32)
            for t in range(TAPS):
                acc = acc + taps[t] * tiles(fir[p, (y + (t - 4) * d1) & (L - 1)])
            acc = acc.reshape(L, 128).astype(BF16)
            second_ref[p, row, :] = acc
            put_halo(sec, p, y, acc.astype(F32))

    taps_z = spread(coef, 32)

    @pl.loop(0, L)
    def _(y):
        row = pl.ds(pl.multiple_of(y * L, L), L)
        for p in range(2):
            acc = jnp.zeros((4, 8, 128), F32)
            for t in range(TAPS):
                acc = acc + taps_z[t] * tiles(sec[p, y, pl.ds(HALO + (t - 4) * d2, L), :])
            mix[row, p * 128:(p + 1) * 128] = acc.reshape(L, 128).astype(BF16)

    for j in range(8):
        turned = contract(eye, mix[j * 128:(j + 1) * 128, :], 1, 1)
        for p in range(2):
            stage[pl.ds(2 * j + p, C, stride=STRIDE), :] = turned[p * 128:p * 128 + C, :]
    mixed_ref[...] = stage[...].astype(BF16)


def conv_bwd(dil, d_ref, coef, which, eye_ref, first_ref, second_ref, field_ref,
             dfi, sums_ref, stage, dmh, dse, acc_ref):
    d1, d2 = dil[1], dil[2]
    weights = jnp.zeros((EXTRA_W, 128), F32)
    for g in range(GROUPS):
        stage[g * PIECE:(g + 1) * PIECE, :] = d_ref[g, 0:PIECE, :].astype(F32)
        weights = weights + d_ref[g, PIECE:PIECE + EXTRA_W, :].astype(F32)
    sums_ref[0:EXTRA_W, :] = weights
    eye = eye_ref[...]
    for j in range(8):
        out = contract(load_field(stage, j), eye, 0, 0)
        for p in range(2):
            for i in range(4):
                put_halo(dmh, p, 4 * j + i, out[i * L:(i + 1) * L, p * 128:(p + 1) * 128])

    def fold(v):
        return (v[0] + v[1]) + (v[2] + v[3])

    taps_z = spread(coef, 32)
    empty = (jnp.zeros((8, 128), F32),) * TAPS

    def along_z(y, sums):
        row = pl.ds(pl.multiple_of(y * L, L), L)
        sums = list(sums)
        for p in range(2):
            field = tiles(second_ref[p, row, :].astype(F32))
            acc = jnp.zeros((4, 8, 128), F32)
            for t in range(TAPS):
                moved = tiles(dmh[p, y, pl.ds(HALO - (t - 4) * d2, L), :])
                acc = acc + taps_z[t] * moved
                sums[t] = sums[t] + fold(moved * field)
            dse[p, y] = acc.reshape(L, 128).astype(BF16).astype(F32)
        return tuple(sums)

    sums = lax.fori_loop(0, L, along_z, empty)
    for t in range(TAPS):
        acc_ref[18 + t] = sums[t]
    taps = spread(coef, 16)

    def along_y(y, sums):
        row = pl.ds(pl.multiple_of(y * L, L), L)
        sums = list(sums)
        for p in range(2):
            field = tiles(first_ref[p, row, :].astype(F32))
            acc = jnp.zeros((4, 8, 128), F32)
            for t in range(TAPS):
                moved = tiles(dse[p, (y - (t - 4) * d1) & (L - 1)])
                acc = acc + taps[t] * moved
                sums[t] = sums[t] + fold(moved * field)
            dfi[row, p * 128:(p + 1) * 128] = acc.reshape(L, 128).astype(BF16)
        return tuple(sums)

    sums = lax.fori_loop(0, L, along_y, empty)
    for t in range(TAPS):
        acc_ref[9 + t] = sums[t]
    for t in range(27, 32):
        acc_ref[t] = jnp.zeros((8, 128), F32)

    cross = contract(field_ref[...], dfi[...], 1, 0)
    for t in range(TAPS):
        keep = jnp.where(which[...] == t, cross, 0.0)
        keep = jnp.sum(keep.reshape(32, 8, 256), axis=0)
        acc_ref[t] = keep[:, :128] + keep[:, 128:]
    lane = lax.broadcasted_iota(jnp.int32, (8, 128), 1)
    channel = lax.broadcasted_iota(jnp.int32, (8, 128), 0)
    table = jnp.where((lax.rem(lane, CH) == channel) & (lane < C), 1.0, 0.0)
    kern = lax.dot_general(
        table, jnp.sum(acc_ref[...], axis=1), (((1,), (1,)), ((), ())),
        precision=lax.Precision.HIGHEST, preferred_element_type=F32)
    kern = jnp.concatenate([kern] * 4, axis=1)
    sums_ref[EXTRA_W:EXTRA_W + 8, :] = jnp.where(lane // 32 == dil[3], kern, 0.0)


def pack_out(dfi, hi_ref, lo_ref, mine, other, out_ref, weight_ref, stage):
    hi, lo = hi_ref[...], lo_ref[...]
    for j in range(8):
        block = dfi[j * 128:(j + 1) * 128, :]
        out = contract(hi, block, 1, 1) + contract(lo, block, 1, 1)
        for p in range(2):
            stage[pl.ds(2 * j + p, C, stride=STRIDE), :] = out[p * 128:p * 128 + C, :]
    weight_ref[...] = mine[0:EXTRA_W, :] + other[0:EXTRA_W, :]
    kern = mine[EXTRA_W:, :] + other[EXTRA_W:, :]
    high = kern.astype(BF16).astype(F32)
    extra = jnp.concatenate([high, kern - high], axis=0).astype(BF16)
    for g in range(GROUPS):
        out_ref[g, 0:PIECE, :] = stage[g * PIECE:(g + 1) * PIECE, :].astype(BF16)
        out_ref[g, PIECE:PIECE + EXTRA_K, :] = extra


BLOCK = 256


def middle(m_ref, c_ref, we, wr, out_ref, stage, stage_c, mix, cot, expand_ref, reduce_ref):
    stage[...] = m_ref[...].astype(F32)
    stage_c[...] = c_ref[...].astype(F32)
    for j in range(8):
        for p in range(2):
            k = 2 * j + p
            mix[:, k * 128:(k + 1) * 128] = pieces(stage, j, p).astype(BF16)
            cot[:, k * 128:(k + 1) * 128] = pieces(stage_c, j, p).astype(BF16)
    expand_ref[...] = jnp.zeros_like(expand_ref)
    reduce_ref[...] = jnp.zeros_like(reduce_ref)
    root = math.sqrt(2.0 / math.pi)

    for b in range(2 * L * L // BLOCK):
        cols = slice(b * BLOCK, (b + 1) * BLOCK)
        mb, cb = mix[:, cols], cot[:, cols]
        pre = contract(we[...], mb, 0, 0)
        d_hidden = contract(wr[...], cb, 1, 0)
        square = pre * pre
        inner = root * pre * (1.0 + 0.044715 * square)
        half = 0.5 + 0.5 * jnp.tanh(inner)
        hidden = (pre * half).astype(BF16)
        slope = half + pre * (2.0 * half * (1.0 - half)) * (root * (1.0 + 3.0 * 0.044715 * square))
        d_pre = (d_hidden * slope).astype(BF16)
        reduce_ref[...] += contract(hidden, cb, 1, 1)
        expand_ref[...] += contract(d_pre, mb, 1, 1)
        out = contract(we[...], d_pre, 1, 0)
        for i in range(BLOCK // 128):
            k = b * (BLOCK // 128) + i
            stage[pl.ds(k, C, stride=STRIDE), :] = out[:, i * 128:(i + 1) * 128]
    gap = jnp.zeros((EXTRA_W, 128 - C), F32)
    for g in range(GROUPS):
        own = slice(g * BH, (g + 1) * BH)
        terms = jnp.concatenate([expand_ref[own, :], reduce_ref[own, :]], axis=0)
        out_ref[g, 0:PIECE, :] = stage[g * PIECE:(g + 1) * PIECE, :].astype(BF16)
        out_ref[g, PIECE:PIECE + EXTRA_W, :] = jnp.concatenate([terms, gap], axis=1).astype(BF16)


VMEM = pl.BlockSpec(memory_space=pltpu.VMEM)
SMEM = pl.BlockSpec(memory_space=pltpu.SMEM)
PARAMS = pltpu.CompilerParams(vmem_limit_bytes=28 * 1024 * 1024)


def shape(*dims, dtype=BF16):
    return jax.ShapeDtypeStruct(dims, dtype)


def estimate(flops):
    return pl.CostEstimate(flops=flops, bytes_accessed=4 * 10**6, transcendentals=0)


def run_prepare(scalars, coef, delta):
    return pl.pallas_call(
        prepare,
        out_shape=(shape(256, 256),) * 3,
        in_specs=[SMEM] + [VMEM] * 2,
        out_specs=(VMEM,) * 3,
        compiler_params=PARAMS,
        cost_estimate=estimate(10**8),
        name="prepare",
    )(scalars, coef, delta)


def run_conv_fwd(scalars, rows, coef, hi, lo, eye):
    return pl.pallas_call(
        conv_fwd,
        out_shape=(shape(ROWS, 128), shape(2, 1024, 128), shape(2, 1024, 128), shape(256, 1024)),
        in_specs=[SMEM] + [VMEM] * 5,
        out_specs=(VMEM,) * 4,
        scratch_shapes=[pltpu.VMEM((ROWS, 128), F32), pltpu.VMEM((2, L, L, 128), F32),
                        pltpu.VMEM((2, L, L + 2 * HALO, 128), F32), pltpu.VMEM((1024, 256), BF16)],
        compiler_params=PARAMS,
        cost_estimate=estimate(10**9),
        name="conv_fwd",
    )(scalars, rows, coef, hi, lo, eye)


def run_conv_bwd(scalars, rows, coef, which, eye, first, second, field):
    return pl.pallas_call(
        conv_bwd,
        out_shape=(shape(1024, 256), shape(EXTRA_W + 8, 128, dtype=F32)),
        in_specs=[SMEM] + [VMEM] * 7,
        out_specs=(VMEM,) * 2,
        scratch_shapes=[pltpu.VMEM((ROWS, 128), F32),
                        pltpu.VMEM((2, L, L + 2 * HALO, 128), F32),
                        pltpu.VMEM((2, L, L, 128), F32), pltpu.VMEM((32, 8, 128), F32)],
        compiler_params=PARAMS,
        cost_estimate=estimate(10**9),
        name="conv_bwd",
    )(scalars, rows, coef, which, eye, first, second, field)


def run_pack_out(d_first, hi, lo, mine, other):
    return pl.pallas_call(
        pack_out,
        out_shape=(shape(GROUPS, PIECE + EXTRA_K, 128), shape(EXTRA_W, 128, dtype=F32)),
        in_specs=[VMEM] * 5,
        out_specs=(VMEM,) * 2,
        scratch_shapes=[pltpu.VMEM((ROWS, 128), F32)],
        compiler_params=PARAMS,
        cost_estimate=estimate(10**9),
        name="pack_out",
    )(d_first, hi, lo, mine, other)


def run_middle(rows, cot_rows, expand_weight, reduce_weight):
    return pl.pallas_call(
        middle,
        out_shape=shape(GROUPS, PIECE + EXTRA_W, 128),
        in_specs=[VMEM] * 4,
        out_specs=VMEM,
        scratch_shapes=[pltpu.VMEM((ROWS, 128), F32), pltpu.VMEM((ROWS, 128), F32),
                        pltpu.VMEM((C, 2048), BF16), pltpu.VMEM((C, 2048), BF16),
                        pltpu.VMEM((H, C), F32), pltpu.VMEM((H, C), F32)],
        compiler_params=PARAMS,
        cost_estimate=pl.CostEstimate(flops=10**9, bytes_accessed=4 * 10**6, transcendentals=10**6),
        name="middle",
    )(rows, cot_rows, expand_weight, reduce_weight)


def to_rows(field):
    return field.reshape(C, 2, 8, 128).transpose(0, 2, 1, 3).reshape(ROWS, 128)


def from_rows(rows):
    return rows.reshape(C, 8, 2, 128).transpose(0, 2, 1, 3).reshape(1, C, 2, 1024)


def swap(parts):
    return lax.all_to_all(parts, "pen", 0, 0, tiled=True)


def from_other_core(terms):
    if lax.axis_size("core") == 1:
        return jnp.zeros_like(terms)
    return lax.ppermute(terms, "core", [(0, 1), (1, 0)])


def sum_over_chips(terms):
    size = lax.axis_size("zh") * lax.axis_size("y")
    parts = jnp.broadcast_to(terms.astype(BF16)[None], (size,) + terms.shape)
    return jnp.sum(lax.all_to_all(parts, ("zh", "y"), 0, 0, tiled=True).astype(F32), axis=0)


def per_device(activations, cotangent, depth_kernels, dilations, expand_weight, reduce_weight):
    delta = jnp.asarray(delta_table())
    own = lax.dynamic_slice_in_dim(depth_kernels, lax.axis_index("pen") * CH, CH, 1)
    coef = jnp.tile(own.transpose(0, 2, 1), (1, 1, GROUPS))
    coef = jnp.pad(coef, ((0, 0), (0, 16 - TAPS), (0, 128 - C))).reshape(48, 128)
    group = lax.axis_index("pen").astype(jnp.int32)
    scalars = jnp.concatenate([dilations, jnp.mod(group, 4)[None]])
    steps = ((jnp.arange(TAPS, dtype=jnp.int32) - 4) * dilations[0]) % L
    which = jnp.full((256, 256), -1, jnp.int32)
    for t in range(TAPS):
        which = jnp.where(delta == steps[t], t, which)

    start = activations.reshape(GROUPS, CH, 2, 8, 128).transpose(0, 1, 3, 2, 4)
    lines = swap(start).reshape(ROWS, 128)
    hi, lo, eye = run_prepare(scalars, coef, delta)
    mixed, first, second, field = run_conv_fwd(scalars, lines, coef, hi, lo, eye)
    cot_rows = to_rows(cotangent)
    mixed = swap(mixed.reshape(GROUPS, PIECE, 128)).reshape(ROWS, 128)
    d_lines = swap(run_middle(mixed, cot_rows, expand_weight, reduce_weight))
    d_first, mine = run_conv_bwd(scalars, d_lines, coef, which, eye, first, second, field)
    d_conv, weights = run_pack_out(d_first, hi, lo, mine, from_other_core(mine))
    arrived = swap(d_conv)

    kern = arrived[:, PIECE:, :].astype(F32).reshape(4, 4, 2, 8, 128)
    kern = jnp.sum(kern, axis=(1, 2)).reshape(32, 128)
    sums = sum_over_chips(jnp.concatenate([weights, kern], axis=0))
    d_input = arrived[:, :PIECE, :].reshape(ROWS, 128)
    grad_input = from_rows((cot_rows.astype(F32) + d_input.astype(F32)).astype(BF16))

    samples = lax.axis_size("zh") * lax.axis_size("y") * lax.axis_size("core")
    sums = sums * (1.0 / math.sqrt(samples * L * L * L))
    own_expand = sums[0:BH, 0:C].T
    own_reduce = sums[BH:EXTRA_W, 0:C]
    kern = sums[EXTRA_W:].reshape(4, 8, 4, 32)[:, :CH, :, :3 * TAPS]
    kern = kern.transpose(0, 2, 1, 3).reshape(C, 3, TAPS).transpose(1, 0, 2)
    return grad_input, own_expand, own_reduce, kern


def solution(mesh):
    samp = mesh.devices.shape[0]
    split = (2, samp // 4, 2) if samp % 4 == 0 else (1, samp, 1)
    fine = Mesh(mesh.devices.reshape(*split, GROUPS), (*SAMP, "pen"))
    field = P(SAMP, None, "pen", None)
    return jax.shard_map(
        per_device,
        mesh=fine,
        in_specs=(field, field, P(), P(), P(), P()),
        out_specs=(field, P(None, "pen"), P("pen", None), P()),
        check_vma=False,
    )
```

```python
import math

import jax
import jax.numpy as jnp
import numpy as np
from jax import lax
from jax.experimental import pallas as pl
from jax.experimental.pallas import tpu as pltpu
from jax.sharding import Mesh
from jax.sharding import PartitionSpec as P

C = 96
H = 384
L = 32
TAPS = 9
GROUPS = 16
CH = C // GROUPS
ROWS = C * L * L * 2 // 128
STRIDE = 16
PIECE = ROWS // GROUPS
BH = H // GROUPS
EXTRA_W = 2 * BH
HALO = 16
F32 = jnp.float32
BF16 = jnp.bfloat16
SAMP = ("zh", "y", "core")


def delta_table():
    r = np.arange(256)
    plane, rest = r // 128, r % 128
    x, c = 2 * (rest // CH) + plane, rest % CH
    valid = rest < C
    delta = (x[:, None] - x[None, :]) % L
    same = (c[:, None] == c[None, :]) & valid[:, None] & valid[None, :]
    return np.where(same, delta, -1).astype(np.int32)


def contract(a, b, da, db):
    return lax.dot_general(a, b, (((da,), (db,)), ((), ())), preferred_element_type=F32)


def pieces(stage, j, p):
    return stage[pl.ds(2 * j + p, C, stride=STRIDE), :]


def spread(coef, base):
    return [jnp.broadcast_to(coef[base + t:base + t + 1, :], (8, 128)) for t in range(TAPS)]


def tiles(v):
    return v.reshape(4, 8, 128)


def load_field(stage, j):
    gap = jnp.zeros((128 - C, 128), F32)
    parts = []
    for p in range(2):
        parts += [pieces(stage, j, p), gap]
    return jnp.concatenate(parts, axis=0).astype(BF16)


def put_halo(ref, p, y, v):
    ref[p, y, HALO:HALO + L, :] = v
    ref[p, y, 0:HALO, :] = v[L - HALO:, :]
    ref[p, y, HALO + L:, :] = v[:HALO, :]


def prepare(dil, coef, delta, hi_ref, lo_ref, eye_ref):
    spacing = dil[0]
    for half in range(2):
        cols = slice(half * 128, (half + 1) * 128)
        table = delta[:, cols]
        m = jnp.zeros((256, 128), F32)
        for t in range(TAPS):
            m = m + jnp.where(table == (((t - 4) * spacing) & (L - 1)), coef[t:t + 1, :], 0.0)
        hi = m.astype(BF16)
        hi_ref[:, cols] = hi
        lo_ref[:, cols] = (m - hi.astype(F32)).astype(BF16)
        eye_ref[:, cols] = jnp.where(table == 0, 1.0, 0.0).astype(BF16)


def conv_fwd(dil, a_ref, coef, hi_ref, lo_ref, eye_ref, mixed_ref, first_ref, second_ref,
             field_ref, stage, fir, sec, mix):
    d1, d2 = dil[1], dil[2]
    stage[...] = a_ref[...].astype(F32)
    hi, lo, eye = hi_ref[...], lo_ref[...], eye_ref[...]
    for j in range(8):
        f = load_field(stage, j)
        field_ref[:, j * 128:(j + 1) * 128] = f
        out = (contract(f, hi, 0, 0) + contract(f, lo, 0, 0)).astype(BF16)
        for p in range(2):
            half = out[:, p * 128:(p + 1) * 128]
            first_ref[p, j * 128:(j + 1) * 128, :] = half
            fir[p, 4 * j:4 * j + 4] = half.astype(F32).reshape(4, L, 128)

    taps = spread(coef, 16)

    @pl.loop(0, L, unroll=2)
    def _(y):
        row = pl.ds(pl.multiple_of(y * L, L), L)
        for p in range(2):
            acc = jnp.zeros((4, 8, 128), F32)
            for t in range(TAPS):
                acc = acc + taps[t] * tiles(fir[p, (y + (t - 4) * d1) & (L - 1)])
            acc = acc.reshape(L, 128).astype(BF16)
            second_ref[p, row, :] = acc
            put_halo(sec, p, y, acc.astype(F32))

    taps_z = spread(coef, 32)

    @pl.loop(0, L, unroll=2)
    def _(y):
        row = pl.ds(pl.multiple_of(y * L, L), L)
        for p in range(2):
            acc = jnp.zeros((4, 8, 128), F32)
            for t in range(TAPS):
                acc = acc + taps_z[t] * tiles(sec[p, y, pl.ds(HALO + (t - 4) * d2, L), :])
            mix[row, p * 128:(p + 1) * 128] = acc.reshape(L, 128).astype(BF16)

    for j in range(8):
        turned = contract(eye, mix[j * 128:(j + 1) * 128, :], 1, 1)
        for p in range(2):
            stage[pl.ds(2 * j + p, C, stride=STRIDE), :] = turned[p * 128:p * 128 + C, :]
    mixed_ref[...] = stage[...].astype(BF16)


def conv_bwd(dil, d_ref, coef, which, eye_ref, first_ref, second_ref, field_ref,
             dfi, sums_ref, stage, dmh, dse, acc_ref):
    d1, d2 = dil[1], dil[2]
    weights = jnp.zeros((EXTRA_W, 128), F32)
    for g in range(GROUPS):
        stage[g * PIECE:(g + 1) * PIECE, :] = d_ref[g, 0:PIECE, :].astype(F32)
        weights = weights + d_ref[g, PIECE:PIECE + EXTRA_W, :].astype(F32)
    sums_ref[0:EXTRA_W, :] = weights
    eye = eye_ref[...]
    for j in range(8):
        out = contract(load_field(stage, j), eye, 0, 0)
        for p in range(2):
            for i in range(4):
                put_halo(dmh, p, 4 * j + i, out[i * L:(i + 1) * L, p * 128:(p + 1) * 128])

    def fold(v):
        return (v[0] + v[1]) + (v[2] + v[3])

    taps_z = spread(coef, 32)
    empty = (jnp.zeros((8, 128), F32),) * TAPS

    def along_z(y, sums):
        row = pl.ds(pl.multiple_of(y * L, L), L)
        sums = list(sums)
        for p in range(2):
            field = tiles(second_ref[p, row, :].astype(F32))
            acc = jnp.zeros((4, 8, 128), F32)
            for t in range(TAPS):
                moved = tiles(dmh[p, y, pl.ds(HALO - (t - 4) * d2, L), :])
                acc = acc + taps_z[t] * moved
                sums[t] = sums[t] + fold(moved * field)
            dse[p, y] = acc.reshape(L, 128).astype(BF16).astype(F32)
        return tuple(sums)

    sums = lax.fori_loop(0, L, along_z, empty, unroll=2)
    for t in range(TAPS):
        acc_ref[18 + t] = sums[t]
    taps = spread(coef, 16)

    def along_y(y, sums):
        row = pl.ds(pl.multiple_of(y * L, L), L)
        sums = list(sums)
        for p in range(2):
            field = tiles(first_ref[p, row, :].astype(F32))
            acc = jnp.zeros((4, 8, 128), F32)
            for t in range(TAPS):
                moved = tiles(dse[p, (y - (t - 4) * d1) & (L - 1)])
                acc = acc + taps[t] * moved
                sums[t] = sums[t] + fold(moved * field)
            dfi[row, p * 128:(p + 1) * 128] = acc.reshape(L, 128).astype(BF16)
        return tuple(sums)

    sums = lax.fori_loop(0, L, along_y, empty, unroll=2)
    for t in range(TAPS):
        acc_ref[9 + t] = sums[t]
    for t in range(27, 32):
        acc_ref[t] = jnp.zeros((8, 128), F32)

    cross = contract(field_ref[...], dfi[...], 1, 0)
    for t in range(TAPS):
        keep = jnp.where(which[...] == t, cross, 0.0)
        keep = jnp.sum(keep.reshape(32, 8, 256), axis=0)
        acc_ref[t] = keep[:, :128] + keep[:, 128:]
    lane = lax.broadcasted_iota(jnp.int32, (8, 128), 1)
    channel = lax.broadcasted_iota(jnp.int32, (8, 128), 0)
    table = jnp.where((lax.rem(lane, CH) == channel) & (lane < C), 1.0, 0.0)
    kern = lax.dot_general(
        table, jnp.sum(acc_ref[...], axis=1), (((1,), (1,)), ((), ())),
        precision=lax.Precision.HIGHEST, preferred_element_type=F32)
    sums_ref[EXTRA_W:, :] = jnp.zeros((8, 128), F32)
    sums_ref[EXTRA_W:, 0:32] = kern


def pack_out(dfi, hi_ref, lo_ref, out_ref, stage):
    hi, lo = hi_ref[...], lo_ref[...]
    for j in range(8):
        block = dfi[j * 128:(j + 1) * 128, :]
        out = contract(hi, block, 1, 1) + contract(lo, block, 1, 1)
        for p in range(2):
            stage[pl.ds(2 * j + p, C, stride=STRIDE), :] = out[p * 128:p * 128 + C, :]
    out_ref[...] = stage[...].astype(BF16)


BLOCK = 256


def middle(m_ref, c_ref, we, wr, out_ref, stage, stage_c, mix, cot, expand_ref, reduce_ref):
    stage[...] = m_ref[...].astype(F32)
    stage_c[...] = c_ref[...].astype(F32)
    for j in range(8):
        for p in range(2):
            k = 2 * j + p
            mix[:, k * 128:(k + 1) * 128] = pieces(stage, j, p).astype(BF16)
            cot[:, k * 128:(k + 1) * 128] = pieces(stage_c, j, p).astype(BF16)
    expand_ref[...] = jnp.zeros_like(expand_ref)
    reduce_ref[...] = jnp.zeros_like(reduce_ref)
    root = math.sqrt(2.0 / math.pi)

    for b in range(2 * L * L // BLOCK):
        cols = slice(b * BLOCK, (b + 1) * BLOCK)
        mb, cb = mix[:, cols], cot[:, cols]
        pre = contract(we[...], mb, 0, 0)
        d_hidden = contract(wr[...], cb, 1, 0)
        square = pre * pre
        inner = root * pre * (1.0 + 0.044715 * square)
        half = 0.5 + 0.5 * jnp.tanh(inner)
        hidden = (pre * half).astype(BF16)
        slope = half + pre * (2.0 * half * (1.0 - half)) * (root * (1.0 + 3.0 * 0.044715 * square))
        d_pre = (d_hidden * slope).astype(BF16)
        reduce_ref[...] += contract(hidden, cb, 1, 1)
        expand_ref[...] += contract(d_pre, mb, 1, 1)
        out = contract(we[...], d_pre, 1, 0)
        for i in range(BLOCK // 128):
            k = b * (BLOCK // 128) + i
            stage[pl.ds(k, C, stride=STRIDE), :] = out[:, i * 128:(i + 1) * 128]
    gap = jnp.zeros((EXTRA_W, 128 - C), F32)
    for g in range(GROUPS):
        own = slice(g * BH, (g + 1) * BH)
        terms = jnp.concatenate([expand_ref[own, :], reduce_ref[own, :]], axis=0)
        out_ref[g, 0:PIECE, :] = stage[g * PIECE:(g + 1) * PIECE, :].astype(BF16)
        out_ref[g, PIECE:PIECE + EXTRA_W, :] = jnp.concatenate([terms, gap], axis=1).astype(BF16)


VMEM = pl.BlockSpec(memory_space=pltpu.VMEM)
SMEM = pl.BlockSpec(memory_space=pltpu.SMEM)
PARAMS = pltpu.CompilerParams(vmem_limit_bytes=28 * 1024 * 1024)


def shape(*dims, dtype=BF16):
    return jax.ShapeDtypeStruct(dims, dtype)


def estimate(flops):
    return pl.CostEstimate(flops=flops, bytes_accessed=4 * 10**6, transcendentals=0)


def run_prepare(scalars, coef, delta):
    return pl.pallas_call(
        prepare,
        out_shape=(shape(256, 256),) * 3,
        in_specs=[SMEM] + [VMEM] * 2,
        out_specs=(VMEM,) * 3,
        compiler_params=PARAMS,
        cost_estimate=estimate(10**8),
        name="prepare",
    )(scalars, coef, delta)


def run_conv_fwd(scalars, rows, coef, hi, lo, eye):
    return pl.pallas_call(
        conv_fwd,
        out_shape=(shape(ROWS, 128), shape(2, 1024, 128), shape(2, 1024, 128), shape(256, 1024)),
        in_specs=[SMEM] + [VMEM] * 5,
        out_specs=(VMEM,) * 4,
        scratch_shapes=[pltpu.VMEM((ROWS, 128), F32), pltpu.VMEM((2, L, L, 128), F32),
                        pltpu.VMEM((2, L, L + 2 * HALO, 128), F32), pltpu.VMEM((1024, 256), BF16)],
        compiler_params=PARAMS,
        cost_estimate=estimate(10**9),
        name="conv_fwd",
    )(scalars, rows, coef, hi, lo, eye)


def run_conv_bwd(scalars, rows, coef, which, eye, first, second, field):
    return pl.pallas_call(
        conv_bwd,
        out_shape=(shape(1024, 256), shape(EXTRA_W + 8, 128, dtype=F32)),
        in_specs=[SMEM] + [VMEM] * 7,
        out_specs=(VMEM,) * 2,
        scratch_shapes=[pltpu.VMEM((ROWS, 128), F32),
                        pltpu.VMEM((2, L, L + 2 * HALO, 128), F32),
                        pltpu.VMEM((2, L, L, 128), F32), pltpu.VMEM((32, 8, 128), F32)],
        compiler_params=PARAMS,
        cost_estimate=estimate(10**9),
        name="conv_bwd",
    )(scalars, rows, coef, which, eye, first, second, field)


def run_pack_out(d_first, hi, lo):
    return pl.pallas_call(
        pack_out,
        out_shape=shape(ROWS, 128),
        in_specs=[VMEM] * 3,
        out_specs=VMEM,
        scratch_shapes=[pltpu.VMEM((ROWS, 128), F32)],
        compiler_params=PARAMS,
        cost_estimate=estimate(10**9),
        name="pack_out",
    )(d_first, hi, lo)


def run_middle(rows, cot_rows, expand_weight, reduce_weight):
    return pl.pallas_call(
        middle,
        out_shape=shape(GROUPS, PIECE + EXTRA_W, 128),
        in_specs=[VMEM] * 4,
        out_specs=VMEM,
        scratch_shapes=[pltpu.VMEM((ROWS, 128), F32), pltpu.VMEM((ROWS, 128), F32),
                        pltpu.VMEM((C, 2048), BF16), pltpu.VMEM((C, 2048), BF16),
                        pltpu.VMEM((H, C), F32), pltpu.VMEM((H, C), F32)],
        compiler_params=PARAMS,
        cost_estimate=pl.CostEstimate(flops=10**9, bytes_accessed=4 * 10**6, transcendentals=10**6),
        name="middle",
    )(rows, cot_rows, expand_weight, reduce_weight)


def to_rows(field):
    return field.reshape(C, 2, 8, 128).transpose(0, 2, 1, 3).reshape(ROWS, 128)


def from_rows(rows):
    return rows.reshape(C, 8, 2, 128).transpose(0, 2, 1, 3).reshape(1, C, 2, 1024)


def swap(parts):
    return lax.all_to_all(parts, "pen", 0, 0, tiled=True)


def shifted(terms, axis, by):
    size = lax.axis_size(axis)
    return lax.ppermute(terms, axis, [(i, (i + by) % size) for i in range(size)])


def sum_over_core_and_y(terms):
    if lax.axis_size("core") == 2:
        terms = terms + shifted(terms, "core", 1)
    if lax.axis_size("y") == 8:
        terms = terms + shifted(terms, "y", 4)
        return terms + shifted(terms, "y", 1) + shifted(terms, "y", -1) + shifted(terms, "y", 2)
    total = terms
    for by in range(1, lax.axis_size("y")):
        total = total + shifted(terms, "y", by)
    return total


def per_device(activations, cotangent, depth_kernels, dilations, expand_weight, reduce_weight):
    delta = jnp.asarray(delta_table())
    own = lax.dynamic_slice_in_dim(depth_kernels, lax.axis_index("pen") * CH, CH, 1)
    coef = jnp.tile(own.transpose(0, 2, 1), (1, 1, GROUPS))
    coef = jnp.pad(coef, ((0, 0), (0, 16 - TAPS), (0, 128 - C))).reshape(48, 128)
    scalars = jnp.concatenate([dilations, jnp.zeros((1,), jnp.int32)])
    steps = ((jnp.arange(TAPS, dtype=jnp.int32) - 4) * dilations[0]) % L
    which = jnp.full((256, 256), -1, jnp.int32)
    for t in range(TAPS):
        which = jnp.where(delta == steps[t], t, which)

    start = activations.reshape(GROUPS, CH, 2, 8, 128).transpose(0, 1, 3, 2, 4)
    lines = swap(start).reshape(ROWS, 128)
    hi, lo, eye = run_prepare(scalars, coef, delta)
    mixed, first, second, field = run_conv_fwd(scalars, lines, coef, hi, lo, eye)
    cot_rows = to_rows(cotangent)
    mixed = swap(mixed.reshape(GROUPS, PIECE, 128)).reshape(ROWS, 128)
    d_lines = swap(run_middle(mixed, cot_rows, expand_weight, reduce_weight))
    d_first, mine = run_conv_bwd(scalars, d_lines, coef, which, eye, first, second, field)
    d_conv = run_pack_out(d_first, hi, lo)
    d_input = swap(d_conv.reshape(GROUPS, PIECE, 128)).reshape(ROWS, 128)
    sums = sum_over_core_and_y(mine)
    sums, d_input = lax.optimization_barrier((sums, d_input))

    halves = lax.axis_size("zh")
    kern = jnp.broadcast_to(sums[None, EXTRA_W:], (halves * GROUPS, 8, 128))
    kern = lax.all_to_all(kern, ("zh", "pen"), 0, 0, tiled=True)
    weights = sums[:EXTRA_W]
    if halves == 2:
        weights = weights + shifted(weights, "zh", 1)
    grad_input = from_rows((cot_rows.astype(F32) + d_input.astype(F32)).astype(BF16))

    samples = halves * lax.axis_size("y") * lax.axis_size("core")
    scale = 1.0 / math.sqrt(samples * L * L * L)
    own_expand = weights[0:BH, 0:C].T * scale
    own_reduce = weights[BH:EXTRA_W, 0:C] * scale
    kern = jnp.sum(kern.reshape(halves, GROUPS, 8, 128), axis=0) * scale
    kern = kern[:, :CH, :3 * TAPS].reshape(C, 3, TAPS).transpose(1, 0, 2)
    return grad_input, own_expand, own_reduce, kern


def solution(mesh):
    samp = mesh.devices.shape[0]
    split = (2, samp // 4, 2) if samp % 4 == 0 else (1, samp, 1)
    fine = Mesh(mesh.devices.reshape(*split, GROUPS), (*SAMP, "pen"))
    field = P(SAMP, None, "pen", None)
    return jax.shard_map(
        per_device,
        mesh=fine,
        in_specs=(field, field, P(), P(), P(), P()),
        out_specs=(field, P(None, "pen"), P("pen", None), P()),
        check_vma=False,
    )
```

```python
import math

import jax
import jax.numpy as jnp
import numpy as np
from jax import lax
from jax.experimental import pallas as pl
from jax.experimental.pallas import tpu as pltpu
from jax.sharding import Mesh
from jax.sharding import PartitionSpec as P

C = 96
H = 384
L = 32
TAPS = 9
GROUPS = 16
CH = C // GROUPS
ROWS = C * L * L * 2 // 128
STRIDE = 16
PIECE = ROWS // GROUPS
BH = H // GROUPS
HALO = 16
F32 = jnp.float32
BF16 = jnp.bfloat16
SAMP = ("zh", "y", "core")


def delta_table():
    r = np.arange(256)
    plane, rest = r // 128, r % 128
    x, c = 2 * (rest // CH) + plane, rest % CH
    valid = rest < C
    delta = (x[:, None] - x[None, :]) % L
    same = (c[:, None] == c[None, :]) & valid[:, None] & valid[None, :]
    return np.where(same, delta, -1).astype(np.int32)


def contract(a, b, da, db):
    return lax.dot_general(a, b, (((da,), (db,)), ((), ())), preferred_element_type=F32)


def pieces(stage, j, p):
    return stage[pl.ds(2 * j + p, C, stride=STRIDE), :]


def spread(coef, base):
    return [jnp.broadcast_to(coef[base + t:base + t + 1, :], (8, 128)) for t in range(TAPS)]


def tiles(v):
    return v.reshape(4, 8, 128)


def load_field(stage, j):
    gap = jnp.zeros((128 - C, 128), F32)
    parts = []
    for p in range(2):
        parts += [pieces(stage, j, p), gap]
    return jnp.concatenate(parts, axis=0).astype(BF16)


def put_halo(ref, p, y, v):
    ref[p, y, HALO:HALO + L, :] = v
    ref[p, y, 0:HALO, :] = v[L - HALO:, :]
    ref[p, y, HALO + L:, :] = v[:HALO, :]


def prepare(dil, coef, delta, hi_ref, lo_ref, eye_ref, which_ref):
    spacing = dil[0]
    for half in range(2):
        cols = slice(half * 128, (half + 1) * 128)
        table = delta[:, cols]
        m = jnp.zeros((256, 128), F32)
        which = jnp.full((256, 128), -1, jnp.int32)
        for t in range(TAPS):
            here = table == (((t - 4) * spacing) & (L - 1))
            m = m + jnp.where(here, coef[t:t + 1, :], 0.0)
            which = jnp.where(here, t, which)
        which_ref[:, cols] = which
        hi = m.astype(BF16)
        hi_ref[:, cols] = hi
        lo_ref[:, cols] = (m - hi.astype(F32)).astype(BF16)
        eye_ref[:, cols] = jnp.where(table == 0, 1.0, 0.0).astype(BF16)


def conv_fwd(dil, a_ref, coef, hi_ref, lo_ref, eye_ref, mixed_ref, first_ref, second_ref,
             field_ref, stage, fir, sec, mix):
    d1, d2 = dil[1], dil[2]
    stage[...] = a_ref[...].astype(F32)
    hi, lo, eye = hi_ref[...], lo_ref[...], eye_ref[...]
    for j in range(8):
        f = load_field(stage, j)
        field_ref[:, j * 128:(j + 1) * 128] = f
        out = (contract(f, hi, 0, 0) + contract(f, lo, 0, 0)).astype(BF16)
        for p in range(2):
            half = out[:, p * 128:(p + 1) * 128]
            first_ref[p, j * 128:(j + 1) * 128, :] = half
            fir[p, 4 * j:4 * j + 4] = half.astype(F32).reshape(4, L, 128)

    taps = spread(coef, 16)

    @pl.loop(0, L, unroll=2)
    def _(y):
        row = pl.ds(pl.multiple_of(y * L, L), L)
        for p in range(2):
            acc = jnp.zeros((4, 8, 128), F32)
            for t in range(TAPS):
                acc = acc + taps[t] * tiles(fir[p, (y + (t - 4) * d1) & (L - 1)])
            acc = acc.reshape(L, 128).astype(BF16)
            second_ref[p, row, :] = acc
            put_halo(sec, p, y, acc.astype(F32))

    taps_z = spread(coef, 32)

    @pl.loop(0, L, unroll=2)
    def _(y):
        row = pl.ds(pl.multiple_of(y * L, L), L)
        for p in range(2):
            acc = jnp.zeros((4, 8, 128), F32)
            for t in range(TAPS):
                acc = acc + taps_z[t] * tiles(sec[p, y, pl.ds(HALO + (t - 4) * d2, L), :])
            mix[row, p * 128:(p + 1) * 128] = acc.reshape(L, 128).astype(BF16)

    for j in range(8):
        turned = contract(eye, mix[j * 128:(j + 1) * 128, :], 1, 1)
        for p in range(2):
            stage[pl.ds(2 * j + p, C, stride=STRIDE), :] = turned[p * 128:p * 128 + C, :]
    mixed_ref[...] = stage[...].astype(BF16)


def conv_bwd(dil, d_ref, coef, hi_ref, lo_ref, which, eye_ref, first_ref, second_ref, field_ref,
             kept, other, out_ref, stage, dmh, dse, dfi, acc_ref):
    d1, d2 = dil[1], dil[2]
    stage[...] = d_ref[...].astype(F32)
    eye = eye_ref[...]
    for j in range(8):
        out = contract(load_field(stage, j), eye, 0, 0)
        for p in range(2):
            for i in range(4):
                put_halo(dmh, p, 4 * j + i, out[i * L:(i + 1) * L, p * 128:(p + 1) * 128])

    def fold(v):
        return (v[0] + v[1]) + (v[2] + v[3])

    taps_z = spread(coef, 32)
    empty = (jnp.zeros((8, 128), F32),) * TAPS

    def along_z(y, sums):
        row = pl.ds(pl.multiple_of(y * L, L), L)
        sums = list(sums)
        for p in range(2):
            field = tiles(second_ref[p, row, :].astype(F32))
            acc = jnp.zeros((4, 8, 128), F32)
            for t in range(TAPS):
                moved = tiles(dmh[p, y, pl.ds(HALO - (t - 4) * d2, L), :])
                acc = acc + taps_z[t] * moved
                sums[t] = sums[t] + fold(moved * field)
            dse[p, y] = acc.reshape(L, 128).astype(BF16).astype(F32)
        return tuple(sums)

    sums = lax.fori_loop(0, L, along_z, empty, unroll=2)
    for t in range(TAPS):
        acc_ref[18 + t] = sums[t]
    taps = spread(coef, 16)

    def along_y(y, sums):
        row = pl.ds(pl.multiple_of(y * L, L), L)
        sums = list(sums)
        for p in range(2):
            field = tiles(first_ref[p, row, :].astype(F32))
            acc = jnp.zeros((4, 8, 128), F32)
            for t in range(TAPS):
                moved = tiles(dse[p, (y - (t - 4) * d1) & (L - 1)])
                acc = acc + taps[t] * moved
                sums[t] = sums[t] + fold(moved * field)
            dfi[row, p * 128:(p + 1) * 128] = acc.reshape(L, 128).astype(BF16)
        return tuple(sums)

    sums = lax.fori_loop(0, L, along_y, empty, unroll=2)
    for t in range(TAPS):
        acc_ref[9 + t] = sums[t]
    for t in range(27, 32):
        acc_ref[t] = jnp.zeros((8, 128), F32)

    cross = contract(field_ref[...], dfi[...], 1, 0)
    for t in range(TAPS):
        keep = jnp.where(which[...] == t, cross, 0.0)
        keep = jnp.sum(keep.reshape(32, 8, 256), axis=0)
        acc_ref[t] = keep[:, :128] + keep[:, 128:]
    lane = lax.broadcasted_iota(jnp.int32, (8, 128), 1)
    channel = lax.broadcasted_iota(jnp.int32, (8, 128), 0)
    table = jnp.where((lax.rem(lane, CH) == channel) & (lane < C), 1.0, 0.0)
    kern = lax.dot_general(
        table, jnp.sum(acc_ref[...], axis=1), (((1,), (1,)), ((), ())),
        precision=lax.Precision.HIGHEST, preferred_element_type=F32)
    kern = jnp.concatenate([kern] * 4, axis=1)
    kern = jnp.where(lane // 32 == dil[3], kern, 0.0)
    hi, lo = hi_ref[...], lo_ref[...]
    for j in range(8):
        block = dfi[j * 128:(j + 1) * 128, :]
        out = contract(hi, block, 1, 1) + contract(lo, block, 1, 1)
        for p in range(2):
            stage[pl.ds(2 * j + p, C, stride=STRIDE), :] = out[p * 128:p * 128 + C, :]
    gap = jnp.zeros((BH, 128 - C), F32)
    for g in range(GROUPS):
        out_ref[g, 0:PIECE, :] = stage[g * PIECE:(g + 1) * PIECE, :].astype(BF16)
        own = slice(g * BH, (g + 1) * BH)
        weights = jnp.concatenate([kept[own, :] + other[own, :], gap], axis=1)
        out_ref[g, PIECE:, :] = jnp.concatenate([weights, kern], axis=0).astype(BF16)


BLOCK = 256


def load_sites(m_ref, c_ref, stage, stage_c, mix, cot):
    stage[...] = m_ref[...].astype(F32)
    stage_c[...] = c_ref[...].astype(F32)
    for j in range(8):
        for p in range(2):
            cols = slice((2 * j + p) * 128, (2 * j + p + 1) * 128)
            mix[:, cols] = pieces(stage, j, p).astype(BF16)
            cot[:, cols] = pieces(stage_c, j, p).astype(BF16)


def activation(mb, cb, we, wr):
    root = math.sqrt(2.0 / math.pi)
    pre = contract(we[...], mb, 0, 0)
    d_hidden = contract(wr[...], cb, 1, 0)
    square = pre * pre
    inner = pre * (root + (root * 0.044715) * square)
    half = 0.5 + 0.5 * jnp.tanh(inner)
    hidden = pre * half
    slope = half + hidden * (1.0 - half) * (2.0 * root + (6.0 * root * 0.044715) * square)
    return hidden, (d_hidden * slope).astype(BF16)


def middle(m_ref, c_ref, we, wr, out_ref, stage, stage_c, mix, cot):
    load_sites(m_ref, c_ref, stage, stage_c, mix, cot)
    for b in range(2 * L * L // BLOCK):
        cols = slice(b * BLOCK, (b + 1) * BLOCK)
        _, d_pre = activation(mix[:, cols], cot[:, cols], we, wr)
        out = contract(we[...], d_pre, 1, 0)
        for i in range(BLOCK // 128):
            k = b * (BLOCK // 128) + i
            stage[pl.ds(k, C, stride=STRIDE), :] = out[:, i * 128:(i + 1) * 128]
    out_ref[...] = stage[...].astype(BF16)


def weight_terms(core, m_ref, c_ref, we, wr, keep_ref, send_ref, stage, stage_c, mix, cot,
                 expand_ref, reduce_ref):
    load_sites(m_ref, c_ref, stage, stage_c, mix, cot)
    expand_ref[...] = jnp.zeros_like(expand_ref)
    reduce_ref[...] = jnp.zeros_like(reduce_ref)
    for b in range(2 * L * L // BLOCK):
        cols = slice(b * BLOCK, (b + 1) * BLOCK)
        mb, cb = mix[:, cols], cot[:, cols]
        hidden, d_pre = activation(mb, cb, we, wr)
        reduce_ref[...] += contract(hidden.astype(BF16), cb, 1, 1)
        expand_ref[...] += contract(d_pre, mb, 1, 1)
    expand, reduce = expand_ref[...], reduce_ref[...]
    keep_ref[...] = jnp.where(core[0] == 0, expand, reduce)
    send_ref[...] = jnp.where(core[0] == 0, reduce, expand)


VMEM = pl.BlockSpec(memory_space=pltpu.VMEM)
SMEM = pl.BlockSpec(memory_space=pltpu.SMEM)
PARAMS = pltpu.CompilerParams(vmem_limit_bytes=28 * 1024 * 1024)


def shape(*dims, dtype=BF16):
    return jax.ShapeDtypeStruct(dims, dtype)


def estimate(flops):
    return pl.CostEstimate(flops=flops, bytes_accessed=4 * 10**6, transcendentals=0)


def run_prepare(scalars, coef, delta):
    return pl.pallas_call(
        prepare,
        out_shape=(shape(256, 256),) * 3 + (shape(256, 256, dtype=jnp.int32),),
        in_specs=[SMEM] + [VMEM] * 2,
        out_specs=(VMEM,) * 4,
        compiler_params=PARAMS,
        cost_estimate=estimate(10**8),
        name="prepare",
    )(scalars, coef, delta)


def run_conv_fwd(scalars, rows, coef, hi, lo, eye):
    return pl.pallas_call(
        conv_fwd,
        out_shape=(shape(ROWS, 128), shape(2, 1024, 128), shape(2, 1024, 128), shape(256, 1024)),
        in_specs=[SMEM] + [VMEM] * 5,
        out_specs=(VMEM,) * 4,
        scratch_shapes=[pltpu.VMEM((ROWS, 128), F32), pltpu.VMEM((2, L, L, 128), F32),
                        pltpu.VMEM((2, L, L + 2 * HALO, 128), F32), pltpu.VMEM((1024, 256), BF16)],
        compiler_params=PARAMS,
        cost_estimate=estimate(10**9),
        name="conv_fwd",
    )(scalars, rows, coef, hi, lo, eye)


def run_conv_bwd(scalars, *arrays):
    return pl.pallas_call(
        conv_bwd,
        out_shape=shape(GROUPS, PIECE + BH + 8, 128),
        in_specs=[SMEM] + [VMEM] * len(arrays),
        out_specs=VMEM,
        scratch_shapes=[pltpu.VMEM((ROWS, 128), F32),
                        pltpu.VMEM((2, L, L + 2 * HALO, 128), F32),
                        pltpu.VMEM((2, L, L, 128), F32), pltpu.VMEM((1024, 256), BF16),
                        pltpu.VMEM((32, 8, 128), F32)],
        compiler_params=PARAMS,
        cost_estimate=estimate(10**9),
        name="conv_bwd",
    )(scalars, *arrays)


def site_scratch():
    return [pltpu.VMEM((ROWS, 128), F32), pltpu.VMEM((ROWS, 128), F32),
            pltpu.VMEM((C, 2048), BF16), pltpu.VMEM((C, 2048), BF16)]


def run_middle(*arrays):
    return pl.pallas_call(
        middle,
        out_shape=shape(ROWS, 128),
        in_specs=[VMEM] * 4,
        out_specs=VMEM,
        scratch_shapes=site_scratch(),
        compiler_params=PARAMS,
        cost_estimate=estimate(10**9),
        name="middle",
    )(*arrays)


def run_weight_terms(core, *arrays):
    return pl.pallas_call(
        weight_terms,
        out_shape=(shape(H, C, dtype=F32),) * 2,
        in_specs=[SMEM] + [VMEM] * 4,
        out_specs=(VMEM,) * 2,
        scratch_shapes=site_scratch() + [pltpu.VMEM((H, C), F32)] * 2,
        compiler_params=PARAMS,
        cost_estimate=estimate(10**9),
        name="weight_terms",
    )(core, *arrays)


def to_rows(field):
    return field.reshape(C, 2, 8, 128).transpose(0, 2, 1, 3).reshape(ROWS, 128)


def from_rows(rows):
    return rows.reshape(C, 8, 2, 128).transpose(0, 2, 1, 3).reshape(1, C, 2, 1024)


def swap(parts):
    return lax.all_to_all(parts, "pen", 0, 0, tiled=True)


def from_other_core(terms):
    return lax.ppermute(terms, "core", [(0, 1), (1, 0)])


def sum_over_chips(terms):
    size = lax.axis_size("zh") * lax.axis_size("y")
    parts = jnp.broadcast_to(terms.astype(BF16)[None], (size,) + terms.shape)
    return jnp.sum(lax.all_to_all(parts, ("zh", "y"), 0, 0, tiled=True).astype(F32), axis=0)


def per_device(activations, cotangent, depth_kernels, dilations, expand_weight, reduce_weight):
    delta = jnp.asarray(delta_table())
    own = lax.dynamic_slice_in_dim(depth_kernels, lax.axis_index("pen") * CH, CH, 1)
    coef = jnp.tile(own.transpose(0, 2, 1), (1, 1, GROUPS))
    coef = jnp.pad(coef, ((0, 0), (0, 16 - TAPS), (0, 128 - C))).reshape(48, 128)
    group = lax.axis_index("pen").astype(jnp.int32)
    core = lax.axis_index("core").astype(jnp.int32)
    scalars = jnp.concatenate([dilations, jnp.mod(group, 4)[None]])

    start = activations.reshape(GROUPS, CH, 2, 8, 128).transpose(0, 1, 3, 2, 4)
    lines = swap(start).reshape(ROWS, 128)
    hi, lo, eye, which = run_prepare(scalars, coef, delta)
    mixed, first, second, field = run_conv_fwd(scalars, lines, coef, hi, lo, eye)
    cot_rows = to_rows(cotangent)
    mixed = swap(mixed.reshape(GROUPS, PIECE, 128)).reshape(ROWS, 128)
    d_mixed = run_middle(mixed, cot_rows, expand_weight, reduce_weight)
    d_lines = swap(d_mixed.reshape(GROUPS, PIECE, 128)).reshape(ROWS, 128)
    keep, send = run_weight_terms(core[None], mixed, cot_rows, expand_weight, reduce_weight)
    d_conv = run_conv_bwd(scalars, d_lines, coef, hi, lo, which, eye, first, second, field,
                          keep, from_other_core(send))
    arrived = swap(d_conv)

    weights = jnp.sum(arrived[:, PIECE:PIECE + BH, :].astype(F32), axis=0)
    kern = arrived[:, PIECE + BH:, :].astype(F32).reshape(4, 4, 8, 128)
    kern = jnp.sum(kern, axis=1)[:, :CH, :].reshape(4 * CH, 128)
    mine = sum_over_chips(jnp.concatenate([weights, kern], axis=0))
    d_input = arrived[:, :PIECE, :].reshape(ROWS, 128)
    grad_input = from_rows((cot_rows.astype(F32) + d_input.astype(F32)).astype(BF16))

    samples = lax.axis_size("zh") * lax.axis_size("y") * lax.axis_size("core")
    mine = mine * (1.0 / math.sqrt(samples * L * L * L))
    other = from_other_core(mine)
    own_expand = jnp.where(core == 0, mine, other)[0:BH, 0:C].T
    own_reduce = jnp.where(core == 0, other, mine)[0:BH, 0:C]
    kern = (mine + other)[BH:].reshape(4, CH, 4, 32)[:, :, :, :3 * TAPS]
    kern = kern.transpose(0, 2, 1, 3).reshape(C, 3, TAPS).transpose(1, 0, 2)
    return grad_input, own_expand, own_reduce, kern


def solution(mesh):
    samp = mesh.devices.shape[0]
    split = (2, samp // 4, 2)
    fine = Mesh(mesh.devices.reshape(*split, GROUPS), (*SAMP, "pen"))
    field = P(SAMP, None, "pen", None)
    return jax.shard_map(
        per_device,
        mesh=fine,
        in_specs=(field, field, P(), P(), P(), P()),
        out_specs=(field, P(None, "pen"), P("pen", None), P()),
        check_vma=False,
    )
```

```python
import math

import jax
import jax.numpy as jnp
import numpy as np
from jax import lax
from jax.experimental import pallas as pl
from jax.experimental.pallas import tpu as pltpu
from jax.sharding import Mesh
from jax.sharding import PartitionSpec as P

C = 96
H = 384
L = 32
TAPS = 9
GROUPS = 16
CH = C // GROUPS
ROWS = C * L * L * 2 // 128
STRIDE = 16
PIECE = ROWS // GROUPS
BH = H // GROUPS
HALO = 16
F32 = jnp.float32
BF16 = jnp.bfloat16
SAMP = ("zh", "y", "core")


def delta_table():
    r = np.arange(256)
    plane, rest = r // 128, r % 128
    x, c = 2 * (rest // CH) + plane, rest % CH
    valid = rest < C
    delta = (x[:, None] - x[None, :]) % L
    same = (c[:, None] == c[None, :]) & valid[:, None] & valid[None, :]
    return np.where(same, delta, -1).astype(np.int32)


def contract(a, b, da, db):
    return lax.dot_general(a, b, (((da,), (db,)), ((), ())), preferred_element_type=F32)


def pieces(stage, j, p):
    return stage[pl.ds(2 * j + p, C, stride=STRIDE), :]


def spread(coef, base):
    return [jnp.broadcast_to(coef[base + t:base + t + 1, :], (8, 128)) for t in range(TAPS)]


def tiles(v):
    return v.reshape(4, 8, 128)


def load_field(stage, j):
    gap = jnp.zeros((128 - C, 128), F32)
    parts = []
    for p in range(2):
        parts += [pieces(stage, j, p), gap]
    return jnp.concatenate(parts, axis=0).astype(BF16)


def put_halo(ref, p, y, v):
    ref[p, y, HALO:HALO + L, :] = v
    ref[p, y, 0:HALO, :] = v[L - HALO:, :]
    ref[p, y, HALO + L:, :] = v[:HALO, :]


def prepare(dil, coef, delta, hi_ref, lo_ref, eye_ref, which_ref):
    spacing = dil[0]
    for half in range(2):
        cols = slice(half * 128, (half + 1) * 128)
        table = delta[:, cols]
        m = jnp.zeros((256, 128), F32)
        which = jnp.full((256, 128), -1.0, F32)
        for t in range(TAPS):
            here = table == (((t - 4) * spacing) & (L - 1))
            m = m + jnp.where(here, coef[t:t + 1, :], 0.0)
            which = jnp.where(here, float(t), which)
        which_ref[:, cols] = which.astype(BF16)
        hi = m.astype(BF16)
        hi_ref[:, cols] = hi
        lo_ref[:, cols] = (m - hi.astype(F32)).astype(BF16)
        eye_ref[:, cols] = jnp.where(table == 0, 1.0, 0.0).astype(BF16)


def conv_fwd(dil, a_ref, coef, hi_ref, lo_ref, eye_ref, mixed_ref, first_ref, second_ref,
             field_ref, stage, fir, sec, mix):
    d1, d2 = dil[1], dil[2]
    stage[...] = a_ref[...].astype(F32)
    hi, lo, eye = hi_ref[...], lo_ref[...], eye_ref[...]
    for j in range(8):
        f = load_field(stage, j)
        field_ref[:, j * 128:(j + 1) * 128] = f
        out = (contract(f, hi, 0, 0) + contract(f, lo, 0, 0)).astype(BF16)
        for p in range(2):
            half = out[:, p * 128:(p + 1) * 128]
            first_ref[p, j * 128:(j + 1) * 128, :] = half
            fir[p, 4 * j:4 * j + 4] = half.astype(F32).reshape(4, L, 128)

    taps = spread(coef, 16)

    @pl.loop(0, L, unroll=4)
    def _(y):
        row = pl.ds(pl.multiple_of(y * L, L), L)
        for p in range(2):
            acc = jnp.zeros((4, 8, 128), F32)
            for t in range(TAPS):
                acc = acc + taps[t] * tiles(fir[p, (y + (t - 4) * d1) & (L - 1)])
            acc = acc.reshape(L, 128).astype(BF16)
            second_ref[p, row, :] = acc
            put_halo(sec, p, y, acc.astype(F32))

    taps_z = spread(coef, 32)

    @pl.loop(0, L, unroll=4)
    def _(y):
        row = pl.ds(pl.multiple_of(y * L, L), L)
        for p in range(2):
            acc = jnp.zeros((4, 8, 128), F32)
            for t in range(TAPS):
                acc = acc + taps_z[t] * tiles(sec[p, y, pl.ds(HALO + (t - 4) * d2, L), :])
            mix[row, p * 128:(p + 1) * 128] = acc.reshape(L, 128).astype(BF16)

    for j in range(8):
        turned = contract(eye, mix[j * 128:(j + 1) * 128, :], 1, 1)
        for p in range(2):
            stage[pl.ds(2 * j + p, C, stride=STRIDE), :] = turned[p * 128:p * 128 + C, :]
    mixed_ref[...] = stage[...].astype(BF16)


def conv_bwd(dil, d_ref, coef, hi_ref, lo_ref, which, first_ref, second_ref, field_ref,
             terms, out_ref, stage, dmh, dse, dfi, acc_ref):
    d1, d2 = dil[1], dil[2]
    stage[...] = d_ref[...].astype(F32)
    eye = jnp.where(which[...].astype(F32) == 4.0, 1.0, 0.0).astype(BF16)
    for j in range(8):
        out = contract(load_field(stage, j), eye, 0, 0)
        for p in range(2):
            for i in range(4):
                put_halo(dmh, p, 4 * j + i, out[i * L:(i + 1) * L, p * 128:(p + 1) * 128])

    def fold(v):
        return (v[0] + v[1]) + (v[2] + v[3])

    taps_z = spread(coef, 32)
    empty = (jnp.zeros((8, 128), F32),) * TAPS

    def along_z(y, sums):
        row = pl.ds(pl.multiple_of(y * L, L), L)
        sums = list(sums)
        for p in range(2):
            field = tiles(second_ref[p, row, :].astype(F32))
            acc = jnp.zeros((4, 8, 128), F32)
            for t in range(TAPS):
                moved = tiles(dmh[p, y, pl.ds(HALO - (t - 4) * d2, L), :])
                acc = acc + taps_z[t] * moved
                sums[t] = sums[t] + fold(moved * field)
            dse[p, y] = acc.reshape(L, 128).astype(BF16).astype(F32)
        return tuple(sums)

    sums = lax.fori_loop(0, L, along_z, empty, unroll=4)
    for t in range(TAPS):
        acc_ref[18 + t] = sums[t]
    taps = spread(coef, 16)

    def along_y(y, sums):
        row = pl.ds(pl.multiple_of(y * L, L), L)
        sums = list(sums)
        for p in range(2):
            field = tiles(first_ref[p, row, :].astype(F32))
            acc = jnp.zeros((4, 8, 128), F32)
            for t in range(TAPS):
                moved = tiles(dse[p, (y - (t - 4) * d1) & (L - 1)])
                acc = acc + taps[t] * moved
                sums[t] = sums[t] + fold(moved * field)
            dfi[row, p * 128:(p + 1) * 128] = acc.reshape(L, 128).astype(BF16)
        return tuple(sums)

    sums = lax.fori_loop(0, L, along_y, empty, unroll=4)
    for t in range(TAPS):
        acc_ref[9 + t] = sums[t]
    for t in range(27, 32):
        acc_ref[t] = jnp.zeros((8, 128), F32)

    cross = contract(field_ref[...], dfi[...], 1, 0)
    tap_of = which[...].astype(F32)
    for t in range(TAPS):
        keep = jnp.where(tap_of == float(t), cross, 0.0)
        keep = jnp.sum(keep.reshape(32, 8, 256), axis=0)
        acc_ref[t] = keep[:, :128] + keep[:, 128:]
    lane = lax.broadcasted_iota(jnp.int32, (8, 128), 1)
    channel = lax.broadcasted_iota(jnp.int32, (8, 128), 0)
    table = jnp.where((lax.rem(lane, CH) == channel) & (lane < C), 1.0, 0.0)
    kern = lax.dot_general(
        table, jnp.sum(acc_ref[...], axis=1), (((1,), (1,)), ((), ())),
        precision=lax.Precision.HIGHEST, preferred_element_type=F32)
    kern = jnp.concatenate([kern] * 4, axis=1)
    kern = jnp.where(lane // 32 == dil[3], kern, 0.0)
    hi, lo = hi_ref[...], lo_ref[...]
    for j in range(8):
        block = dfi[j * 128:(j + 1) * 128, :]
        out = contract(hi, block, 1, 1) + contract(lo, block, 1, 1)
        for p in range(2):
            stage[pl.ds(2 * j + p, C, stride=STRIDE), :] = out[p * 128:p * 128 + C, :]
    gap = jnp.zeros((BH, 128 - C), F32)
    for g in range(GROUPS):
        out_ref[g, 0:PIECE, :] = stage[g * PIECE:(g + 1) * PIECE, :].astype(BF16)
        own = slice(g * BH, (g + 1) * BH)
        weights = jnp.concatenate([terms[own, :], gap], axis=1)
        out_ref[g, PIECE:, :] = jnp.concatenate([weights, kern], axis=0).astype(BF16)


BLOCK = 512


def by_site(rows_ref, stage, out):
    stage[...] = rows_ref[...].astype(F32)
    for j in range(8):
        for p in range(2):
            cols = slice((2 * j + p) * 128, (2 * j + p + 1) * 128)
            out[:, cols] = pieces(stage, j, p).astype(BF16)


def activation(mb, cb, we, wr):
    root = math.sqrt(2.0 / math.pi)
    pre = contract(we[...], mb, 0, 0)
    d_hidden = contract(wr[...], cb, 1, 0)
    square = pre * pre
    inner = pre * (root + (root * 0.044715) * square)
    half = 0.5 + 0.5 * jnp.tanh(inner)
    hidden = pre * half
    slope = half + hidden * (1.0 - half) * (2.0 * root + (6.0 * root * 0.044715) * square)
    return hidden, (d_hidden * slope).astype(BF16)


def middle(m_ref, c_ref, we, wr, out_ref, stage, stage_c, mix, cot):
    by_site(m_ref, stage, mix)
    by_site(c_ref, stage_c, cot)
    for b in range(2 * L * L // BLOCK):
        cols = slice(b * BLOCK, (b + 1) * BLOCK)
        _, d_pre = activation(mix[:, cols], cot[:, cols], we, wr)
        out = contract(we[...], d_pre, 1, 0)
        for i in range(BLOCK // 128):
            k = b * (BLOCK // 128) + i
            stage[pl.ds(k, C, stride=STRIDE), :] = out[:, i * 128:(i + 1) * 128]
    out_ref[...] = stage[...].astype(BF16)


def weight_terms(core, m_ref, c_ref, we, wr, keep_ref, send_ref, stage, stage_c, mix, cot,
                 expand_ref, reduce_ref):
    by_site(m_ref, stage, mix)
    by_site(c_ref, stage_c, cot)
    expand_ref[...] = jnp.zeros_like(expand_ref)
    reduce_ref[...] = jnp.zeros_like(reduce_ref)
    for b in range(2 * L * L // BLOCK):
        cols = slice(b * BLOCK, (b + 1) * BLOCK)
        mb, cb = mix[:, cols], cot[:, cols]
        hidden, d_pre = activation(mb, cb, we, wr)
        reduce_ref[...] += contract(hidden.astype(BF16), cb, 1, 1)
        expand_ref[...] += contract(d_pre, mb, 1, 1)
    expand, reduce = expand_ref[...], reduce_ref[...]
    keep_ref[...] = jnp.where(core[0] == 0, expand, reduce)
    send_ref[...] = jnp.where(core[0] == 0, reduce, expand)


VMEM = pl.BlockSpec(memory_space=pltpu.VMEM)
SMEM = pl.BlockSpec(memory_space=pltpu.SMEM)
PARAMS = pltpu.CompilerParams(vmem_limit_bytes=28 * 1024 * 1024)


def shape(*dims, dtype=BF16):
    return jax.ShapeDtypeStruct(dims, dtype)


def estimate(flops):
    return pl.CostEstimate(flops=flops, bytes_accessed=4 * 10**6, transcendentals=0)


def run_prepare(scalars, coef, delta):
    return pl.pallas_call(
        prepare,
        out_shape=(shape(256, 256),) * 4,
        in_specs=[SMEM] + [VMEM] * 2,
        out_specs=(VMEM,) * 4,
        compiler_params=PARAMS,
        cost_estimate=estimate(10**8),
        name="prepare",
    )(scalars, coef, delta)


def run_conv_fwd(scalars, rows, coef, hi, lo, eye):
    return pl.pallas_call(
        conv_fwd,
        out_shape=(shape(ROWS, 128), shape(2, 1024, 128), shape(2, 1024, 128), shape(256, 1024)),
        in_specs=[SMEM] + [VMEM] * 5,
        out_specs=(VMEM,) * 4,
        scratch_shapes=[pltpu.VMEM((ROWS, 128), F32), pltpu.VMEM((2, L, L, 128), F32),
                        pltpu.VMEM((2, L, L + 2 * HALO, 128), F32), pltpu.VMEM((1024, 256), BF16)],
        compiler_params=PARAMS,
        cost_estimate=estimate(10**9),
        name="conv_fwd",
    )(scalars, rows, coef, hi, lo, eye)


def run_conv_bwd(scalars, *arrays):
    return pl.pallas_call(
        conv_bwd,
        out_shape=shape(GROUPS, PIECE + BH + 8, 128),
        in_specs=[SMEM] + [VMEM] * len(arrays),
        out_specs=VMEM,
        scratch_shapes=[pltpu.VMEM((ROWS, 128), F32),
                        pltpu.VMEM((2, L, L + 2 * HALO, 128), F32),
                        pltpu.VMEM((2, L, L, 128), F32), pltpu.VMEM((1024, 256), BF16),
                        pltpu.VMEM((32, 8, 128), F32)],
        compiler_params=PARAMS,
        cost_estimate=estimate(10**9),
        name="conv_bwd",
    )(scalars, *arrays)


def site_scratch():
    return [pltpu.VMEM((ROWS, 128), F32), pltpu.VMEM((ROWS, 128), F32),
            pltpu.VMEM((C, 2048), BF16), pltpu.VMEM((C, 2048), BF16)]


def run_middle(*arrays):
    return pl.pallas_call(
        middle,
        out_shape=shape(ROWS, 128),
        in_specs=[VMEM] * 4,
        out_specs=VMEM,
        scratch_shapes=site_scratch(),
        compiler_params=PARAMS,
        cost_estimate=estimate(10**9),
        name="middle",
    )(*arrays)


def run_weight_terms(core, *arrays):
    return pl.pallas_call(
        weight_terms,
        out_shape=(shape(H, C, dtype=F32),) * 2,
        in_specs=[SMEM] + [VMEM] * 4,
        out_specs=(VMEM,) * 2,
        scratch_shapes=site_scratch() + [pltpu.VMEM((H, C), F32)] * 2,
        compiler_params=PARAMS,
        cost_estimate=estimate(10**9),
        name="weight_terms",
    )(core, *arrays)


def to_rows(field):
    return field.reshape(C, 2, 8, 128).transpose(0, 2, 1, 3).reshape(ROWS, 128)


def from_rows(rows):
    return rows.reshape(C, 8, 2, 128).transpose(0, 2, 1, 3).reshape(1, C, 2, 1024)


def swap(parts):
    return lax.all_to_all(parts, "pen", 0, 0, tiled=True)


def from_other_core(terms):
    return lax.ppermute(terms, "core", [(0, 1), (1, 0)])


def sum_over_chips(terms):
    size = lax.axis_size("zh") * lax.axis_size("y")
    parts = jnp.broadcast_to(terms.astype(BF16)[None], (size,) + terms.shape)
    return jnp.sum(lax.all_to_all(parts, ("zh", "y"), 0, 0, tiled=True).astype(F32), axis=0)


def per_device(activations, cotangent, depth_kernels, dilations, expand_weight, reduce_weight):
    delta = jnp.asarray(delta_table())
    own = lax.dynamic_slice_in_dim(depth_kernels, lax.axis_index("pen") * CH, CH, 1)
    coef = jnp.tile(own.transpose(0, 2, 1), (1, 1, GROUPS))
    coef = jnp.pad(coef, ((0, 0), (0, 16 - TAPS), (0, 128 - C))).reshape(48, 128)
    group = lax.axis_index("pen").astype(jnp.int32)
    core = lax.axis_index("core").astype(jnp.int32)
    scalars = jnp.concatenate([dilations, jnp.mod(group, 4)[None]])

    start = activations.reshape(GROUPS, CH, 2, 8, 128).transpose(0, 1, 3, 2, 4)
    lines = swap(start).reshape(ROWS, 128)
    hi, lo, eye, which = run_prepare(scalars, coef, delta)
    mixed, first, second, field = run_conv_fwd(scalars, lines, coef, hi, lo, eye)
    cot_rows = to_rows(cotangent)
    mixed = swap(mixed.reshape(GROUPS, PIECE, 128)).reshape(ROWS, 128)
    d_mixed = run_middle(mixed, cot_rows, expand_weight, reduce_weight)
    d_lines = swap(d_mixed.reshape(GROUPS, PIECE, 128)).reshape(ROWS, 128)
    keep, send = run_weight_terms(core[None], mixed, cot_rows, expand_weight, reduce_weight)
    terms = keep + from_other_core(send)
    d_conv = run_conv_bwd(scalars, d_lines, coef, hi, lo, which, first, second, field, terms)
    arrived = swap(d_conv)

    weights = jnp.sum(arrived[:, PIECE:PIECE + BH, :].astype(F32), axis=0)
    kern = arrived[:, PIECE + BH:, :].astype(F32).reshape(4, 4, 8, 128)
    kern = jnp.sum(kern, axis=1)[:, :CH, :].reshape(4 * CH, 128)
    mine = sum_over_chips(jnp.concatenate([weights, kern], axis=0))
    d_input = arrived[:, :PIECE, :].reshape(ROWS, 128)
    grad_input = from_rows((cot_rows.astype(F32) + d_input.astype(F32)).astype(BF16))

    samples = lax.axis_size("zh") * lax.axis_size("y") * lax.axis_size("core")
    mine = mine * (1.0 / math.sqrt(samples * L * L * L))
    other = from_other_core(mine)
    own_expand = jnp.where(core == 0, mine, other)[0:BH, 0:C].T
    own_reduce = jnp.where(core == 0, other, mine)[0:BH, 0:C]
    kern = (mine + other)[BH:].reshape(4, CH, 4, 32)[:, :, :, :3 * TAPS]
    kern = kern.transpose(0, 2, 1, 3).reshape(C, 3, TAPS).transpose(1, 0, 2)
    return grad_input, own_expand, own_reduce, kern


def solution(mesh):
    samp = mesh.devices.shape[0]
    split = (2, samp // 4, 2)
    fine = Mesh(mesh.devices.reshape(*split, GROUPS), (*SAMP, "pen"))
    field = P(SAMP, None, "pen", None)
    return jax.shard_map(
        per_device,
        mesh=fine,
        in_specs=(field, field, P(), P(), P(), P()),
        out_specs=(field, P(None, "pen"), P("pen", None), P()),
        check_vma=False,
    )
```

```python
import math

import jax
import jax.numpy as jnp
import numpy as np
from jax import lax
from jax.experimental import pallas as pl
from jax.experimental.pallas import tpu as pltpu
from jax.sharding import Mesh
from jax.sharding import PartitionSpec as P

C = 96
H = 384
L = 32
TAPS = 9
GROUPS = 16
CH = C // GROUPS
ROWS = C * L * L * 2 // 128
STRIDE = 16
PIECE = ROWS // GROUPS
BH = H // GROUPS
HALO = 16
F32 = jnp.float32
BF16 = jnp.bfloat16
SAMP = ("zh", "y", "core")


def delta_table():
    r = np.arange(256)
    plane, rest = r // 128, r % 128
    x, c = 2 * (rest // CH) + plane, rest % CH
    valid = rest < C
    delta = (x[:, None] - x[None, :]) % L
    same = (c[:, None] == c[None, :]) & valid[:, None] & valid[None, :]
    return np.where(same, delta, -1).astype(np.int32)


def contract(a, b, da, db):
    return lax.dot_general(a, b, (((da,), (db,)), ((), ())), preferred_element_type=F32)


def pieces(stage, j, p):
    return stage[pl.ds(2 * j + p, C, stride=STRIDE), :]


def spread(coef, base):
    return [jnp.broadcast_to(coef[base + t:base + t + 1, :], (8, 128)) for t in range(TAPS)]


def tiles(v):
    return v.reshape(4, 8, 128)


def load_field(stage, j):
    gap = jnp.zeros((128 - C, 128), F32)
    parts = []
    for p in range(2):
        parts += [pieces(stage, j, p), gap]
    return jnp.concatenate(parts, axis=0).astype(BF16)


def put_halo(ref, p, y, v):
    ref[p, y, HALO:HALO + L, :] = v
    ref[p, y, 0:HALO, :] = v[L - HALO:, :]
    ref[p, y, HALO + L:, :] = v[:HALO, :]


def prepare(dil, coef, delta, hi_ref, lo_ref, eye_ref, which_ref):
    spacing = dil[0]
    for half in range(2):
        cols = slice(half * 128, (half + 1) * 128)
        table = delta[:, cols]
        m = jnp.zeros((256, 128), F32)
        which = jnp.full((256, 128), -1.0, F32)
        for t in range(TAPS):
            here = table == (((t - 4) * spacing) & (L - 1))
            m = m + jnp.where(here, coef[t:t + 1, :], 0.0)
            which = jnp.where(here, float(t), which)
        which_ref[:, cols] = which.astype(BF16)
        hi = m.astype(BF16)
        hi_ref[:, cols] = hi
        lo_ref[:, cols] = (m - hi.astype(F32)).astype(BF16)
        eye_ref[:, cols] = jnp.where(table == 0, 1.0, 0.0).astype(BF16)


def conv_fwd(dil, a_ref, coef, hi_ref, lo_ref, eye_ref, mixed_ref, first_ref, second_ref,
             field_ref, stage, fir, sec, mix):
    d1, d2 = dil[1], dil[2]
    stage[...] = a_ref[...].astype(F32)
    hi, lo, eye = hi_ref[...], lo_ref[...], eye_ref[...]
    for j in range(8):
        f = load_field(stage, j)
        field_ref[:, j * 128:(j + 1) * 128] = f
        out = (contract(f, hi, 0, 0) + contract(f, lo, 0, 0)).astype(BF16)
        for p in range(2):
            half = out[:, p * 128:(p + 1) * 128]
            first_ref[p, j * 128:(j + 1) * 128, :] = half
            fir[p, 4 * j:4 * j + 4] = half.astype(F32).reshape(4, L, 128)

    taps = spread(coef, 16)

    @pl.loop(0, L, unroll=4)
    def _(y):
        row = pl.ds(pl.multiple_of(y * L, L), L)
        for p in range(2):
            acc = jnp.zeros((4, 8, 128), F32)
            for t in range(TAPS):
                acc = acc + taps[t] * tiles(fir[p, (y + (t - 4) * d1) & (L - 1)])
            acc = acc.reshape(L, 128).astype(BF16)
            second_ref[p, row, :] = acc
            put_halo(sec, p, y, acc.astype(F32))

    taps_z = spread(coef, 32)

    @pl.loop(0, L, unroll=4)
    def _(y):
        row = pl.ds(pl.multiple_of(y * L, L), L)
        for p in range(2):
            acc = jnp.zeros((4, 8, 128), F32)
            for t in range(TAPS):
                acc = acc + taps_z[t] * tiles(sec[p, y, pl.ds(HALO + (t - 4) * d2, L), :])
            mix[row, p * 128:(p + 1) * 128] = acc.reshape(L, 128).astype(BF16)

    for j in range(8):
        turned = contract(eye, mix[j * 128:(j + 1) * 128, :], 1, 1)
        for p in range(2):
            stage[pl.ds(2 * j + p, C, stride=STRIDE), :] = turned[p * 128:p * 128 + C, :]
    mixed_ref[...] = stage[...].astype(BF16)


def conv_bwd(dil, d_ref, coef, hi_ref, lo_ref, which, first_ref, second_ref, field_ref,
             terms, out_ref, stage, dmh, dse, dfi, acc_ref):
    d1, d2 = dil[1], dil[2]
    stage[...] = d_ref[...].astype(F32)
    eye = jnp.where(which[...].astype(F32) == 4.0, 1.0, 0.0).astype(BF16)
    for j in range(8):
        out = contract(load_field(stage, j), eye, 0, 0)
        for p in range(2):
            for i in range(4):
                put_halo(dmh, p, 4 * j + i, out[i * L:(i + 1) * L, p * 128:(p + 1) * 128])

    def fold(v):
        return (v[0] + v[1]) + (v[2] + v[3])

    taps_z = spread(coef, 32)
    empty = (jnp.zeros((8, 128), F32),) * TAPS

    def along_z(y, sums):
        row = pl.ds(pl.multiple_of(y * L, L), L)
        sums = list(sums)
        for p in range(2):
            field = tiles(second_ref[p, row, :].astype(F32))
            acc = jnp.zeros((4, 8, 128), F32)
            for t in range(TAPS):
                moved = tiles(dmh[p, y, pl.ds(HALO - (t - 4) * d2, L), :])
                acc = acc + taps_z[t] * moved
                sums[t] = sums[t] + fold(moved * field)
            dse[p, y] = acc.reshape(L, 128).astype(BF16).astype(F32)
        return tuple(sums)

    sums = lax.fori_loop(0, L, along_z, empty, unroll=4)
    for t in range(TAPS):
        acc_ref[18 + t] = sums[t]
    taps = spread(coef, 16)

    def along_y(y, sums):
        row = pl.ds(pl.multiple_of(y * L, L), L)
        sums = list(sums)
        for p in range(2):
            field = tiles(first_ref[p, row, :].astype(F32))
            acc = jnp.zeros((4, 8, 128), F32)
            for t in range(TAPS):
                moved = tiles(dse[p, (y - (t - 4) * d1) & (L - 1)])
                acc = acc + taps[t] * moved
                sums[t] = sums[t] + fold(moved * field)
            dfi[row, p * 128:(p + 1) * 128] = acc.reshape(L, 128).astype(BF16)
        return tuple(sums)

    sums = lax.fori_loop(0, L, along_y, empty, unroll=4)
    for t in range(TAPS):
        acc_ref[9 + t] = sums[t]
    for t in range(27, 32):
        acc_ref[t] = jnp.zeros((8, 128), F32)

    cross = contract(field_ref[...], dfi[...], 1, 0)
    tap_of = which[...].astype(F32)
    for t in range(TAPS):
        keep = jnp.where(tap_of == float(t), cross, 0.0)
        keep = jnp.sum(keep.reshape(32, 8, 256), axis=0)
        acc_ref[t] = keep[:, :128] + keep[:, 128:]
    lane = lax.broadcasted_iota(jnp.int32, (8, 128), 1)
    channel = lax.broadcasted_iota(jnp.int32, (8, 128), 0)
    table = jnp.where((lax.rem(lane, CH) == channel) & (lane < C), 1.0, 0.0)
    kern = lax.dot_general(
        table, jnp.sum(acc_ref[...], axis=1), (((1,), (1,)), ((), ())),
        precision=lax.Precision.HIGHEST, preferred_element_type=F32)
    kern = jnp.concatenate([kern] * 4, axis=1)
    kern = jnp.where(lane // 32 == dil[3], kern, 0.0)
    hi, lo = hi_ref[...], lo_ref[...]
    for j in range(8):
        block = dfi[j * 128:(j + 1) * 128, :]
        out = contract(hi, block, 1, 1) + contract(lo, block, 1, 1)
        for p in range(2):
            stage[pl.ds(2 * j + p, C, stride=STRIDE), :] = out[p * 128:p * 128 + C, :]
    gap = jnp.zeros((BH, 128 - C), F32)
    for g in range(GROUPS):
        out_ref[g, 0:PIECE, :] = stage[g * PIECE:(g + 1) * PIECE, :].astype(BF16)
        own = slice(g * BH, (g + 1) * BH)
        weights = jnp.concatenate([terms[own, :], gap], axis=1)
        out_ref[g, PIECE:, :] = jnp.concatenate([weights, kern], axis=0).astype(BF16)


BLOCK = 512


def by_site(rows_ref, stage, out):
    stage[...] = rows_ref[...].astype(F32)
    for j in range(8):
        for p in range(2):
            cols = slice((2 * j + p) * 128, (2 * j + p + 1) * 128)
            out[:, cols] = pieces(stage, j, p).astype(BF16)


def activation(mb, cb, we, wr):
    root = math.sqrt(2.0 / math.pi)
    pre = contract(we[...], mb, 0, 0)
    d_hidden = contract(wr[...], cb, 0, 0)
    square = pre * pre
    inner = pre * (root + (root * 0.044715) * square)
    half = 0.5 + 0.5 * jnp.tanh(inner)
    hidden = pre * half
    slope = half + hidden * (1.0 - half) * (2.0 * root + (6.0 * root * 0.044715) * square)
    return hidden, (d_hidden * slope).astype(BF16)


def middle(m_ref, c_ref, we, wr, out_ref, stage, stage_c, mix, cot):
    by_site(m_ref, stage, mix)
    by_site(c_ref, stage_c, cot)
    for b in range(2 * L * L // BLOCK):
        cols = slice(b * BLOCK, (b + 1) * BLOCK)
        _, d_pre = activation(mix[:, cols], cot[:, cols], we, wr)
        out = contract(we[...], d_pre, 1, 0)
        for i in range(BLOCK // 128):
            k = b * (BLOCK // 128) + i
            stage[pl.ds(k, C, stride=STRIDE), :] = out[:, i * 128:(i + 1) * 128]
    out_ref[...] = stage[...].astype(BF16)


def weight_terms(core, m_ref, c_ref, we, wr, keep_ref, send_ref, stage, stage_c, mix, cot,
                 expand_ref, reduce_ref):
    by_site(m_ref, stage, mix)
    by_site(c_ref, stage_c, cot)
    expand_ref[...] = jnp.zeros_like(expand_ref)
    reduce_ref[...] = jnp.zeros_like(reduce_ref)
    for b in range(2 * L * L // BLOCK):
        cols = slice(b * BLOCK, (b + 1) * BLOCK)
        mb, cb = mix[:, cols], cot[:, cols]
        hidden, d_pre = activation(mb, cb, we, wr)
        reduce_ref[...] += contract(hidden.astype(BF16), cb, 1, 1)
        expand_ref[...] += contract(d_pre, mb, 1, 1)
    expand, reduce = expand_ref[...], reduce_ref[...]
    keep_ref[...] = jnp.where(core[0] == 0, expand, reduce)
    send_ref[...] = jnp.where(core[0] == 0, reduce, expand)


VMEM = pl.BlockSpec(memory_space=pltpu.VMEM)
SMEM = pl.BlockSpec(memory_space=pltpu.SMEM)
PARAMS = pltpu.CompilerParams(vmem_limit_bytes=28 * 1024 * 1024)


def shape(*dims, dtype=BF16):
    return jax.ShapeDtypeStruct(dims, dtype)


def estimate(flops):
    return pl.CostEstimate(flops=flops, bytes_accessed=4 * 10**6, transcendentals=0)


def run_prepare(scalars, coef, delta):
    return pl.pallas_call(
        prepare,
        out_shape=(shape(256, 256),) * 4,
        in_specs=[SMEM] + [VMEM] * 2,
        out_specs=(VMEM,) * 4,
        compiler_params=PARAMS,
        cost_estimate=estimate(10**8),
        name="prepare",
    )(scalars, coef, delta)


def run_conv_fwd(scalars, rows, coef, hi, lo, eye):
    return pl.pallas_call(
        conv_fwd,
        out_shape=(shape(ROWS, 128), shape(2, 1024, 128), shape(2, 1024, 128), shape(256, 1024)),
        in_specs=[SMEM] + [VMEM] * 5,
        out_specs=(VMEM,) * 4,
        scratch_shapes=[pltpu.VMEM((ROWS, 128), F32), pltpu.VMEM((2, L, L, 128), F32),
                        pltpu.VMEM((2, L, L + 2 * HALO, 128), F32), pltpu.VMEM((1024, 256), BF16)],
        compiler_params=PARAMS,
        cost_estimate=estimate(10**9),
        name="conv_fwd",
    )(scalars, rows, coef, hi, lo, eye)


def run_conv_bwd(scalars, *arrays):
    return pl.pallas_call(
        conv_bwd,
        out_shape=shape(GROUPS, PIECE + BH + 8, 128),
        in_specs=[SMEM] + [VMEM] * len(arrays),
        out_specs=VMEM,
        scratch_shapes=[pltpu.VMEM((ROWS, 128), F32),
                        pltpu.VMEM((2, L, L + 2 * HALO, 128), F32),
                        pltpu.VMEM((2, L, L, 128), F32), pltpu.VMEM((1024, 256), BF16),
                        pltpu.VMEM((32, 8, 128), F32)],
        compiler_params=PARAMS,
        cost_estimate=estimate(10**9),
        name="conv_bwd",
    )(scalars, *arrays)


def site_scratch():
    return [pltpu.VMEM((ROWS, 128), F32), pltpu.VMEM((ROWS, 128), F32),
            pltpu.VMEM((C, 2048), BF16), pltpu.VMEM((C, 2048), BF16)]


def run_middle(*arrays):
    return pl.pallas_call(
        middle,
        out_shape=shape(ROWS, 128),
        in_specs=[VMEM] * 4,
        out_specs=VMEM,
        scratch_shapes=site_scratch(),
        compiler_params=PARAMS,
        cost_estimate=estimate(10**9),
        name="middle",
    )(*arrays)


def run_weight_terms(core, *arrays):
    return pl.pallas_call(
        weight_terms,
        out_shape=(shape(H, C, dtype=F32),) * 2,
        in_specs=[SMEM] + [VMEM] * 4,
        out_specs=(VMEM,) * 2,
        scratch_shapes=site_scratch() + [pltpu.VMEM((H, C), F32)] * 2,
        compiler_params=PARAMS,
        cost_estimate=estimate(10**9),
        name="weight_terms",
    )(core, *arrays)


def to_rows(field):
    return field.reshape(C, 2, 8, 128).transpose(0, 2, 1, 3).reshape(ROWS, 128)


def from_rows(rows):
    return rows.reshape(C, 8, 2, 128).transpose(0, 2, 1, 3).reshape(1, C, 2, 1024)


def swap(parts):
    return lax.all_to_all(parts, "pen", 0, 0, tiled=True)


def from_other_core(terms):
    return lax.ppermute(terms, "core", [(0, 1), (1, 0)])


def sum_over_chips(terms):
    size = lax.axis_size("zh") * lax.axis_size("y")
    parts = jnp.broadcast_to(terms.astype(BF16)[None], (size,) + terms.shape)
    return jnp.sum(lax.all_to_all(parts, ("zh", "y"), 0, 0, tiled=True).astype(F32), axis=0)


def per_device(activations, cotangent, depth_kernels, dilations, expand_weight, reduce_weight):
    delta = jnp.asarray(delta_table())
    own = lax.dynamic_slice_in_dim(depth_kernels, lax.axis_index("pen") * CH, CH, 1)
    coef = jnp.tile(own.transpose(0, 2, 1), (1, 1, GROUPS))
    coef = jnp.pad(coef, ((0, 0), (0, 16 - TAPS), (0, 128 - C))).reshape(48, 128)
    group = lax.axis_index("pen").astype(jnp.int32)
    core = lax.axis_index("core").astype(jnp.int32)
    reduce_columns = reduce_weight.T
    scalars = jnp.concatenate([dilations, jnp.mod(group, 4)[None]])

    start = activations.reshape(GROUPS, CH, 2, 8, 128).transpose(0, 1, 3, 2, 4)
    lines = swap(start).reshape(ROWS, 128)
    hi, lo, eye, which = run_prepare(scalars, coef, delta)
    mixed, first, second, field = run_conv_fwd(scalars, lines, coef, hi, lo, eye)
    cot_rows = to_rows(cotangent)
    mixed = swap(mixed.reshape(GROUPS, PIECE, 128)).reshape(ROWS, 128)
    d_mixed = run_middle(mixed, cot_rows, expand_weight, reduce_columns)
    d_lines = swap(d_mixed.reshape(GROUPS, PIECE, 128)).reshape(ROWS, 128)
    keep, send = run_weight_terms(core[None], mixed, cot_rows, expand_weight, reduce_columns)
    terms = keep + from_other_core(send)
    d_conv = run_conv_bwd(scalars, d_lines, coef, hi, lo, which, first, second, field, terms)
    arrived = swap(d_conv)

    weights = jnp.sum(arrived[:, PIECE:PIECE + BH, :].astype(F32), axis=0)
    kern = arrived[:, PIECE + BH:, :].astype(F32).reshape(4, 4, 8, 128)
    kern = jnp.sum(kern, axis=1)[:, :CH, :].reshape(4 * CH, 128)
    mine = sum_over_chips(jnp.concatenate([weights, kern], axis=0))
    d_input = arrived[:, :PIECE, :].reshape(ROWS, 128)
    grad_input = from_rows((cot_rows.astype(F32) + d_input.astype(F32)).astype(BF16))

    samples = lax.axis_size("zh") * lax.axis_size("y") * lax.axis_size("core")
    mine = mine * (1.0 / math.sqrt(samples * L * L * L))
    other = from_other_core(mine)
    own_expand = jnp.where(core == 0, mine, other)[0:BH, 0:C].T
    own_reduce = jnp.where(core == 0, other, mine)[0:BH, 0:C]
    kern = (mine + other)[BH:].reshape(4, CH, 4, 32)[:, :, :, :3 * TAPS]
    kern = kern.transpose(0, 2, 1, 3).reshape(C, 3, TAPS).transpose(1, 0, 2)
    return grad_input, own_expand, own_reduce, kern


def solution(mesh):
    samp = mesh.devices.shape[0]
    split = (2, samp // 4, 2)
    fine = Mesh(mesh.devices.reshape(*split, GROUPS), (*SAMP, "pen"))
    field = P(SAMP, None, "pen", None)
    return jax.shard_map(
        per_device,
        mesh=fine,
        in_specs=(field, field, P(), P(), P(), P()),
        out_specs=(field, P(None, "pen"), P("pen", None), P()),
        check_vma=False,
    )
```

```python
import math

import jax
import jax.numpy as jnp
import numpy as np
from jax import lax
from jax.experimental import pallas as pl
from jax.experimental.pallas import tpu as pltpu
from jax.sharding import Mesh
from jax.sharding import PartitionSpec as P

C = 96
H = 384
L = 32
TAPS = 9
GROUPS = 16
CH = C // GROUPS
ROWS = C * L * L * 2 // 128
STRIDE = 16
PIECE = ROWS // GROUPS
BH = H // GROUPS
HALO = 16
F32 = jnp.float32
BF16 = jnp.bfloat16
SAMP = ("zh", "y", "core")


def delta_table():
    r = np.arange(256)
    plane, rest = r // 128, r % 128
    x, c = 2 * (rest // CH) + plane, rest % CH
    valid = rest < C
    delta = (x[:, None] - x[None, :]) % L
    same = (c[:, None] == c[None, :]) & valid[:, None] & valid[None, :]
    return np.where(same, delta, -1).astype(np.int32)


def contract(a, b, da, db):
    return lax.dot_general(a, b, (((da,), (db,)), ((), ())), preferred_element_type=F32)


def pieces(stage, j, p):
    return stage[pl.ds(2 * j + p, C, stride=STRIDE), :]


def spread(coef, base):
    return [jnp.broadcast_to(coef[base + t:base + t + 1, :], (8, 128)) for t in range(TAPS)]


def tiles(v):
    return v.reshape(4, 8, 128)


def load_field(stage, j):
    gap = jnp.zeros((128 - C, 128), F32)
    parts = []
    for p in range(2):
        parts += [pieces(stage, j, p), gap]
    return jnp.concatenate(parts, axis=0).astype(BF16)


def put_halo(ref, p, y, v):
    ref[p, y, HALO:HALO + L, :] = v
    ref[p, y, 0:HALO, :] = v[L - HALO:, :]
    ref[p, y, HALO + L:, :] = v[:HALO, :]


def prepare(dil, coef, delta, hi_ref, lo_ref, eye_ref, which_ref):
    spacing = dil[0]
    for half in range(2):
        cols = slice(half * 128, (half + 1) * 128)
        table = delta[:, cols]
        m = jnp.zeros((256, 128), F32)
        which = jnp.full((256, 128), -1.0, F32)
        for t in range(TAPS):
            here = table == (((t - 4) * spacing) & (L - 1))
            m = m + jnp.where(here, coef[t:t + 1, :], 0.0)
            which = jnp.where(here, float(t), which)
        which_ref[:, cols] = which.astype(BF16)
        hi = m.astype(BF16)
        hi_ref[:, cols] = hi
        lo_ref[:, cols] = (m - hi.astype(F32)).astype(BF16)
        eye_ref[:, cols] = jnp.where(table == 0, 1.0, 0.0).astype(BF16)


def conv_fwd(dil, a_ref, coef, hi_ref, lo_ref, eye_ref, mixed_ref, first_ref, second_ref,
             field_ref, stage, fir, sec, mix):
    d1, d2 = dil[1], dil[2]
    stage[...] = a_ref[...].astype(F32)
    hi, lo, eye = hi_ref[...], lo_ref[...], eye_ref[...]
    for j in range(8):
        f = load_field(stage, j)
        field_ref[:, j * 128:(j + 1) * 128] = f
        out = (contract(f, hi, 0, 0) + contract(f, lo, 0, 0)).astype(BF16)
        for p in range(2):
            half = out[:, p * 128:(p + 1) * 128]
            first_ref[p, j * 128:(j + 1) * 128, :] = half
            fir[p, 4 * j:4 * j + 4] = half.astype(F32).reshape(4, L, 128)

    taps = spread(coef, 16)

    @pl.loop(0, L, unroll=4)
    def _(y):
        row = pl.ds(pl.multiple_of(y * L, L), L)
        for p in range(2):
            acc = jnp.zeros((4, 8, 128), F32)
            for t in range(TAPS):
                acc = acc + taps[t] * tiles(fir[p, (y + (t - 4) * d1) & (L - 1)])
            acc = acc.reshape(L, 128).astype(BF16)
            second_ref[p, row, :] = acc
            put_halo(sec, p, y, acc.astype(F32))

    taps_z = spread(coef, 32)

    @pl.loop(0, L, unroll=4)
    def _(y):
        row = pl.ds(pl.multiple_of(y * L, L), L)
        for p in range(2):
            acc = jnp.zeros((4, 8, 128), F32)
            for t in range(TAPS):
                acc = acc + taps_z[t] * tiles(sec[p, y, pl.ds(HALO + (t - 4) * d2, L), :])
            mix[row, p * 128:(p + 1) * 128] = acc.reshape(L, 128).astype(BF16)

    for j in range(8):
        turned = contract(eye, mix[j * 128:(j + 1) * 128, :], 1, 1)
        for p in range(2):
            stage[pl.ds(2 * j + p, C, stride=STRIDE), :] = turned[p * 128:p * 128 + C, :]
    mixed_ref[...] = stage[...].astype(BF16)


def conv_bwd(dil, d_ref, coef, hi_ref, lo_ref, which, first_ref, second_ref, field_ref,
             terms, out_ref, stage, dmh, dse, dfi, acc_ref):
    d1, d2 = dil[1], dil[2]
    stage[...] = d_ref[...].astype(F32)
    eye = jnp.where(which[...].astype(F32) == 4.0, 1.0, 0.0).astype(BF16)
    for j in range(8):
        out = contract(load_field(stage, j), eye, 0, 0)
        for p in range(2):
            for i in range(4):
                put_halo(dmh, p, 4 * j + i, out[i * L:(i + 1) * L, p * 128:(p + 1) * 128])

    def fold(v):
        return (v[0] + v[1]) + (v[2] + v[3])

    taps_z = spread(coef, 32)
    empty = (jnp.zeros((8, 128), F32),) * TAPS

    def along_z(y, sums):
        row = pl.ds(pl.multiple_of(y * L, L), L)
        sums = list(sums)
        for p in range(2):
            field = tiles(second_ref[p, row, :].astype(F32))
            acc = jnp.zeros((4, 8, 128), F32)
            for t in range(TAPS):
                moved = tiles(dmh[p, y, pl.ds(HALO - (t - 4) * d2, L), :])
                acc = acc + taps_z[t] * moved
                sums[t] = sums[t] + fold(moved * field)
            dse[p, y] = acc.reshape(L, 128).astype(BF16).astype(F32)
        return tuple(sums)

    sums = lax.fori_loop(0, L, along_z, empty, unroll=4)
    for t in range(TAPS):
        acc_ref[3 * t + 2] = sums[t]
    taps = spread(coef, 16)

    def along_y(y, sums):
        row = pl.ds(pl.multiple_of(y * L, L), L)
        sums = list(sums)
        for p in range(2):
            field = tiles(first_ref[p, row, :].astype(F32))
            acc = jnp.zeros((4, 8, 128), F32)
            for t in range(TAPS):
                moved = tiles(dse[p, (y - (t - 4) * d1) & (L - 1)])
                acc = acc + taps[t] * moved
                sums[t] = sums[t] + fold(moved * field)
            dfi[row, p * 128:(p + 1) * 128] = acc.reshape(L, 128).astype(BF16)
        return tuple(sums)

    sums = lax.fori_loop(0, L, along_y, empty, unroll=4)
    for t in range(TAPS):
        acc_ref[3 * t + 1] = sums[t]
    for t in range(27, 32):
        acc_ref[t] = jnp.zeros((8, 128), F32)

    cross = contract(field_ref[...], dfi[...], 1, 0)
    tap_of = which[...].astype(F32)
    for t in range(TAPS):
        keep = jnp.where(tap_of == float(t), cross, 0.0)
        keep = jnp.sum(keep.reshape(32, 8, 256), axis=0)
        acc_ref[3 * t] = keep[:, :128] + keep[:, 128:]
    lane = lax.broadcasted_iota(jnp.int32, (8, 128), 1)
    channel = lax.broadcasted_iota(jnp.int32, (8, 128), 0)
    table = jnp.where((lax.rem(lane, CH) == channel) & (lane < C), 1.0, 0.0)
    kern = lax.dot_general(
        table, jnp.sum(acc_ref[...], axis=1), (((1,), (1,)), ((), ())),
        precision=lax.Precision.HIGHEST, preferred_element_type=F32)
    kern = jnp.concatenate([kern] * 4, axis=1)
    kern = jnp.where(lane // 32 == dil[3], kern, 0.0)
    hi, lo = hi_ref[...], lo_ref[...]
    for j in range(8):
        block = dfi[j * 128:(j + 1) * 128, :]
        out = contract(hi, block, 1, 1) + contract(lo, block, 1, 1)
        for p in range(2):
            stage[pl.ds(2 * j + p, C, stride=STRIDE), :] = out[p * 128:p * 128 + C, :]
    gap = jnp.zeros((BH, 128 - C), F32)
    for g in range(GROUPS):
        out_ref[g, 0:PIECE, :] = stage[g * PIECE:(g + 1) * PIECE, :].astype(BF16)
        own = slice(g * BH, (g + 1) * BH)
        weights = jnp.concatenate([terms[own, :], gap], axis=1)
        out_ref[g, PIECE:, :] = jnp.concatenate([weights, kern], axis=0).astype(BF16)


BLOCK = 512


def by_site(rows_ref, stage, out):
    stage[...] = rows_ref[...].astype(F32)
    for j in range(8):
        for p in range(2):
            cols = slice((2 * j + p) * 128, (2 * j + p + 1) * 128)
            out[:, cols] = pieces(stage, j, p).astype(BF16)


def activation(mb, cb, we, wr):
    root = math.sqrt(2.0 / math.pi)
    pre = contract(we[...], mb, 0, 0)
    d_hidden = contract(wr[...], cb, 0, 0)
    square = pre * pre
    inner = pre * (root + (root * 0.044715) * square)
    half = 0.5 + 0.5 * jnp.tanh(inner)
    hidden = pre * half
    slope = half + hidden * (1.0 - half) * (2.0 * root + (6.0 * root * 0.044715) * square)
    return hidden, (d_hidden * slope).astype(BF16)


def middle(m_ref, c_ref, we, wr, out_ref, stage, stage_c, mix, cot):
    by_site(m_ref, stage, mix)
    by_site(c_ref, stage_c, cot)
    for b in range(2 * L * L // BLOCK):
        cols = slice(b * BLOCK, (b + 1) * BLOCK)
        _, d_pre = activation(mix[:, cols], cot[:, cols], we, wr)
        out = contract(we[...], d_pre, 1, 0)
        for i in range(BLOCK // 128):
            k = b * (BLOCK // 128) + i
            stage[pl.ds(k, C, stride=STRIDE), :] = out[:, i * 128:(i + 1) * 128]
    out_ref[...] = stage[...].astype(BF16)


def weight_terms(core, m_ref, c_ref, we, wr, keep_ref, send_ref, stage, stage_c, mix, cot,
                 expand_ref, reduce_ref):
    by_site(m_ref, stage, mix)
    by_site(c_ref, stage_c, cot)
    expand_ref[...] = jnp.zeros_like(expand_ref)
    reduce_ref[...] = jnp.zeros_like(reduce_ref)
    for b in range(2 * L * L // BLOCK):
        cols = slice(b * BLOCK, (b + 1) * BLOCK)
        mb, cb = mix[:, cols], cot[:, cols]
        hidden, d_pre = activation(mb, cb, we, wr)
        reduce_ref[...] += contract(hidden.astype(BF16), cb, 1, 1)
        expand_ref[...] += contract(d_pre, mb, 1, 1)
    expand, reduce = expand_ref[...], reduce_ref[...]
    keep_ref[...] = jnp.where(core[0] == 0, expand, reduce)
    send_ref[...] = jnp.where(core[0] == 0, reduce, expand)


def finish(core, mine_ref, other_ref, expand_ref, reduce_ref, kern_ref):
    mine, other = mine_ref[...], other_ref[...]
    is_first = core[0] == 0
    expand_ref[...] = jnp.where(is_first, mine, other)[0:BH, 0:C]
    reduce_ref[...] = jnp.where(is_first, other, mine)[0:BH, 0:C]
    kern = (mine + other)[BH:, :]
    row = lax.broadcasted_iota(jnp.int32, (4 * CH, C), 0)
    lane = lax.broadcasted_iota(jnp.int32, (4 * CH, C), 1)
    total = jnp.zeros((32, C), F32)
    for i in range(4):
        target = lax.div(row, CH) * (4 * CH) + i * CH + lax.rem(row, CH)
        place = jnp.where(lane == target, 1.0, 0.0)
        total = total + lax.dot_general(
            kern[:, 32 * i:32 * i + 32], place, (((0,), (0,)), ((), ())),
            precision=lax.Precision.HIGHEST, preferred_element_type=F32)
    for t in range(TAPS):
        kern_ref[t] = total[3 * t:3 * t + 3, :]


VMEM = pl.BlockSpec(memory_space=pltpu.VMEM)
SMEM = pl.BlockSpec(memory_space=pltpu.SMEM)
PARAMS = pltpu.CompilerParams(vmem_limit_bytes=28 * 1024 * 1024)


def shape(*dims, dtype=BF16):
    return jax.ShapeDtypeStruct(dims, dtype)


def estimate(flops):
    return pl.CostEstimate(flops=flops, bytes_accessed=4 * 10**6, transcendentals=0)


def run_prepare(scalars, coef, delta):
    return pl.pallas_call(
        prepare,
        out_shape=(shape(256, 256),) * 4,
        in_specs=[SMEM] + [VMEM] * 2,
        out_specs=(VMEM,) * 4,
        compiler_params=PARAMS,
        cost_estimate=estimate(10**8),
        name="prepare",
    )(scalars, coef, delta)


def run_conv_fwd(scalars, rows, coef, hi, lo, eye):
    return pl.pallas_call(
        conv_fwd,
        out_shape=(shape(ROWS, 128), shape(2, 1024, 128), shape(2, 1024, 128), shape(256, 1024)),
        in_specs=[SMEM] + [VMEM] * 5,
        out_specs=(VMEM,) * 4,
        scratch_shapes=[pltpu.VMEM((ROWS, 128), F32), pltpu.VMEM((2, L, L, 128), F32),
                        pltpu.VMEM((2, L, L + 2 * HALO, 128), F32), pltpu.VMEM((1024, 256), BF16)],
        compiler_params=PARAMS,
        cost_estimate=estimate(10**9),
        name="conv_fwd",
    )(scalars, rows, coef, hi, lo, eye)


def run_conv_bwd(scalars, *arrays):
    return pl.pallas_call(
        conv_bwd,
        out_shape=shape(GROUPS, PIECE + BH + 8, 128),
        in_specs=[SMEM] + [VMEM] * len(arrays),
        out_specs=VMEM,
        scratch_shapes=[pltpu.VMEM((ROWS, 128), F32),
                        pltpu.VMEM((2, L, L + 2 * HALO, 128), F32),
                        pltpu.VMEM((2, L, L, 128), F32), pltpu.VMEM((1024, 256), BF16),
                        pltpu.VMEM((32, 8, 128), F32)],
        compiler_params=PARAMS,
        cost_estimate=estimate(10**9),
        name="conv_bwd",
    )(scalars, *arrays)


def site_scratch():
    return [pltpu.VMEM((ROWS, 128), F32), pltpu.VMEM((ROWS, 128), F32),
            pltpu.VMEM((C, 2048), BF16), pltpu.VMEM((C, 2048), BF16)]


def run_middle(*arrays):
    return pl.pallas_call(
        middle,
        out_shape=shape(ROWS, 128),
        in_specs=[VMEM] * 4,
        out_specs=VMEM,
        scratch_shapes=site_scratch(),
        compiler_params=PARAMS,
        cost_estimate=estimate(10**9),
        name="middle",
    )(*arrays)


def run_weight_terms(core, *arrays):
    return pl.pallas_call(
        weight_terms,
        out_shape=(shape(H, C, dtype=F32),) * 2,
        in_specs=[SMEM] + [VMEM] * 4,
        out_specs=(VMEM,) * 2,
        scratch_shapes=site_scratch() + [pltpu.VMEM((H, C), F32)] * 2,
        compiler_params=PARAMS,
        cost_estimate=estimate(10**9),
        name="weight_terms",
    )(core, *arrays)


def run_finish(core, mine, other):
    return pl.pallas_call(
        finish,
        out_shape=(shape(BH, C, dtype=F32), shape(BH, C, dtype=F32), shape(TAPS, 3, C, dtype=F32)),
        in_specs=[SMEM] + [VMEM] * 2,
        out_specs=(VMEM,) * 3,
        compiler_params=PARAMS,
        cost_estimate=estimate(10**7),
        name="finish",
    )(core, mine, other)


def to_rows(field):
    return field.reshape(C, 2, 8, 128).transpose(0, 2, 1, 3).reshape(ROWS, 128)


def from_rows(rows):
    return rows.reshape(C, 8, 2, 128).transpose(0, 2, 1, 3).reshape(1, C, 2, 1024)


def swap(parts):
    return lax.all_to_all(parts, "pen", 0, 0, tiled=True)


def from_other_core(terms):
    return lax.ppermute(terms, "core", [(0, 1), (1, 0)])


def sum_over_chips(terms):
    size = lax.axis_size("zh") * lax.axis_size("y")
    parts = jnp.broadcast_to(terms.astype(BF16)[None], (size,) + terms.shape)
    return jnp.sum(lax.all_to_all(parts, ("zh", "y"), 0, 0, tiled=True).astype(F32), axis=0)


def per_device(activations, cotangent, depth_kernels, dilations, expand_weight, reduce_weight):
    delta = jnp.asarray(delta_table())
    own = lax.dynamic_slice_in_dim(depth_kernels, lax.axis_index("pen") * CH, CH, 1)
    coef = jnp.tile(own.transpose(0, 2, 1), (1, 1, GROUPS))
    coef = jnp.pad(coef, ((0, 0), (0, 16 - TAPS), (0, 128 - C))).reshape(48, 128)
    group = lax.axis_index("pen").astype(jnp.int32)
    core = lax.axis_index("core").astype(jnp.int32)
    reduce_columns = reduce_weight.T
    scalars = jnp.concatenate([dilations, jnp.mod(group, 4)[None]])

    start = activations.reshape(GROUPS, CH, 2, 8, 128).transpose(0, 1, 3, 2, 4)
    lines = swap(start).reshape(ROWS, 128)
    hi, lo, eye, which = run_prepare(scalars, coef, delta)
    mixed, first, second, field = run_conv_fwd(scalars, lines, coef, hi, lo, eye)
    cot_rows = to_rows(cotangent)
    mixed = swap(mixed.reshape(GROUPS, PIECE, 128)).reshape(ROWS, 128)
    d_mixed = run_middle(mixed, cot_rows, expand_weight, reduce_columns)
    d_lines = swap(d_mixed.reshape(GROUPS, PIECE, 128)).reshape(ROWS, 128)
    keep, send = run_weight_terms(core[None], mixed, cot_rows, expand_weight, reduce_columns)
    terms = keep + from_other_core(send)
    d_conv = run_conv_bwd(scalars, d_lines, coef, hi, lo, which, first, second, field, terms)
    arrived = swap(d_conv)

    weights = jnp.sum(arrived[:, PIECE:PIECE + BH, :].astype(F32), axis=0)
    kern = arrived[:, PIECE + BH:, :].astype(F32).reshape(4, 4, 8, 128)
    kern = jnp.sum(kern, axis=1)[:, :CH, :].reshape(4 * CH, 128)
    mine = sum_over_chips(jnp.concatenate([weights, kern], axis=0))
    d_input = arrived[:, :PIECE, :].reshape(ROWS, 128)
    grad_input = from_rows((cot_rows.astype(F32) + d_input.astype(F32)).astype(BF16))

    samples = lax.axis_size("zh") * lax.axis_size("y") * lax.axis_size("core")
    mine = mine * (1.0 / math.sqrt(samples * L * L * L))
    expand, reduce, kern = run_finish(core[None], mine, from_other_core(mine))
    return grad_input, expand.T, reduce, kern.transpose(1, 2, 0)


def solution(mesh):
    samp = mesh.devices.shape[0]
    split = (2, samp // 4, 2)
    fine = Mesh(mesh.devices.reshape(*split, GROUPS), (*SAMP, "pen"))
    field = P(SAMP, None, "pen", None)
    return jax.shard_map(
        per_device,
        mesh=fine,
        in_specs=(field, field, P(), P(), P(), P()),
        out_specs=(field, P(None, "pen"), P("pen", None), P()),
        check_vma=False,
    )
```

```python
import functools
import math

import jax
import jax.numpy as jnp
import numpy as np
from jax import lax
from jax.experimental import pallas as pl
from jax.experimental.pallas import tpu as pltpu
from jax.sharding import Mesh
from jax.sharding import PartitionSpec as P

C = 96
H = 384
L = 32
TAPS = 9
GROUPS = 16
CH = C // GROUPS
ROWS = C * L * L * 2 // 128
STRIDE = 16
PIECE = ROWS // GROUPS
BH = H // GROUPS
HALO = 16
F32 = jnp.float32
BF16 = jnp.bfloat16
SAMP = ("zh", "y", "core")


def delta_table():
    r = np.arange(256)
    plane, rest = r // 128, r % 128
    x, c = 2 * (rest // CH) + plane, rest % CH
    valid = rest < C
    delta = (x[:, None] - x[None, :]) % L
    same = (c[:, None] == c[None, :]) & valid[:, None] & valid[None, :]
    return np.where(same, delta, -1).astype(np.int32)


def contract(a, b, da, db):
    return lax.dot_general(a, b, (((da,), (db,)), ((), ())), preferred_element_type=F32)


def pieces(stage, j, p):
    return stage[pl.ds(2 * j + p, C, stride=STRIDE), :]


def spread(coef, base):
    return [jnp.broadcast_to(coef[base + t:base + t + 1, :], (8, 128)) for t in range(TAPS)]


def tiles(v):
    return v.reshape(4, 8, 128)


def load_field(stage, j):
    gap = jnp.zeros((128 - C, 128), F32)
    parts = []
    for p in range(2):
        parts += [pieces(stage, j, p), gap]
    return jnp.concatenate(parts, axis=0).astype(BF16)


def put_halo(ref, p, y, v):
    ref[p, y, HALO:HALO + L, :] = v
    ref[p, y, 0:HALO, :] = v[L - HALO:, :]
    ref[p, y, HALO + L:, :] = v[:HALO, :]


def prepare(dil, coef, delta, hi_ref, lo_ref, eye_ref, which_ref):
    spacing = dil[0]
    for half in range(2):
        cols = slice(half * 128, (half + 1) * 128)
        table = delta[:, cols]
        m = jnp.zeros((256, 128), F32)
        which = jnp.full((256, 128), -1.0, F32)
        for t in range(TAPS):
            here = table == (((t - 4) * spacing) & (L - 1))
            m = m + jnp.where(here, coef[t:t + 1, :], 0.0)
            which = jnp.where(here, float(t), which)
        which_ref[:, cols] = which.astype(BF16)
        hi = m.astype(BF16)
        hi_ref[:, cols] = hi
        lo_ref[:, cols] = (m - hi.astype(F32)).astype(BF16)
        eye_ref[:, cols] = jnp.where(table == 0, 1.0, 0.0).astype(BF16)


def conv_fwd(dil, a_ref, coef, hi_ref, lo_ref, eye_ref, mixed_ref, first_ref, second_ref,
             field_ref, stage, fir, sec, mix):
    d1, d2 = dil[1], dil[2]
    stage[...] = a_ref[...].astype(F32)
    hi, lo, eye = hi_ref[...], lo_ref[...], eye_ref[...]
    for j in range(8):
        f = load_field(stage, j)
        field_ref[:, j * 128:(j + 1) * 128] = f
        out = (contract(f, hi, 0, 0) + contract(f, lo, 0, 0)).astype(BF16)
        for p in range(2):
            half = out[:, p * 128:(p + 1) * 128]
            first_ref[p, j * 128:(j + 1) * 128, :] = half
            fir[p, 4 * j:4 * j + 4] = half.astype(F32).reshape(4, L, 128)

    taps = spread(coef, 16)

    @pl.loop(0, L, unroll=4)
    def _(y):
        row = pl.ds(pl.multiple_of(y * L, L), L)
        for p in range(2):
            acc = jnp.zeros((4, 8, 128), F32)
            for t in range(TAPS):
                acc = acc + taps[t] * tiles(fir[p, (y + (t - 4) * d1) & (L - 1)])
            acc = acc.reshape(L, 128).astype(BF16)
            second_ref[p, row, :] = acc
            put_halo(sec, p, y, acc.astype(F32))

    taps_z = spread(coef, 32)

    @pl.loop(0, L, unroll=4)
    def _(y):
        row = pl.ds(pl.multiple_of(y * L, L), L)
        for p in range(2):
            acc = jnp.zeros((4, 8, 128), F32)
            for t in range(TAPS):
                acc = acc + taps_z[t] * tiles(sec[p, y, pl.ds(HALO + (t - 4) * d2, L), :])
            mix[row, p * 128:(p + 1) * 128] = acc.reshape(L, 128).astype(BF16)

    for j in range(8):
        turned = contract(eye, mix[j * 128:(j + 1) * 128, :], 1, 1)
        for p in range(2):
            stage[pl.ds(2 * j + p, C, stride=STRIDE), :] = turned[p * 128:p * 128 + C, :]
    mixed_ref[...] = stage[...].astype(BF16)


def conv_bwd(dil, d_ref, coef, hi_ref, lo_ref, which, first_ref, second_ref, field_ref,
             terms, out_ref, stage, dmh, dse, dfi, acc_ref):
    d1, d2 = dil[1], dil[2]
    stage[...] = d_ref[...].astype(F32)
    eye = jnp.where(which[...].astype(F32) == 4.0, 1.0, 0.0).astype(BF16)
    for j in range(8):
        out = contract(load_field(stage, j), eye, 0, 0)
        for p in range(2):
            for i in range(4):
                put_halo(dmh, p, 4 * j + i, out[i * L:(i + 1) * L, p * 128:(p + 1) * 128])

    def fold(v):
        return (v[0] + v[1]) + (v[2] + v[3])

    taps_z = spread(coef, 32)
    empty = (jnp.zeros((8, 128), F32),) * TAPS

    def along_z(y, sums):
        row = pl.ds(pl.multiple_of(y * L, L), L)
        sums = list(sums)
        for p in range(2):
            field = tiles(second_ref[p, row, :].astype(F32))
            acc = jnp.zeros((4, 8, 128), F32)
            for t in range(TAPS):
                moved = tiles(dmh[p, y, pl.ds(HALO - (t - 4) * d2, L), :])
                acc = acc + taps_z[t] * moved
                sums[t] = sums[t] + fold(moved * field)
            dse[p, y] = acc.reshape(L, 128).astype(BF16).astype(F32)
        return tuple(sums)

    sums = lax.fori_loop(0, L, along_z, empty, unroll=4)
    for t in range(TAPS):
        acc_ref[3 * t + 2] = sums[t]
    taps = spread(coef, 16)

    def along_y(y, sums):
        row = pl.ds(pl.multiple_of(y * L, L), L)
        sums = list(sums)
        for p in range(2):
            field = tiles(first_ref[p, row, :].astype(F32))
            acc = jnp.zeros((4, 8, 128), F32)
            for t in range(TAPS):
                moved = tiles(dse[p, (y - (t - 4) * d1) & (L - 1)])
                acc = acc + taps[t] * moved
                sums[t] = sums[t] + fold(moved * field)
            dfi[row, p * 128:(p + 1) * 128] = acc.reshape(L, 128).astype(BF16)
        return tuple(sums)

    sums = lax.fori_loop(0, L, along_y, empty, unroll=4)
    for t in range(TAPS):
        acc_ref[3 * t + 1] = sums[t]
    for t in range(27, 32):
        acc_ref[t] = jnp.zeros((8, 128), F32)

    cross = contract(field_ref[...], dfi[...], 1, 0)
    tap_of = which[...].astype(F32)
    for t in range(TAPS):
        keep = jnp.where(tap_of == float(t), cross, 0.0)
        keep = jnp.sum(keep.reshape(32, 8, 256), axis=0)
        acc_ref[3 * t] = keep[:, :128] + keep[:, 128:]
    lane = lax.broadcasted_iota(jnp.int32, (8, 128), 1)
    channel = lax.broadcasted_iota(jnp.int32, (8, 128), 0)
    table = jnp.where((lax.rem(lane, CH) == channel) & (lane < C), 1.0, 0.0)
    kern = lax.dot_general(
        table, jnp.sum(acc_ref[...], axis=1), (((1,), (1,)), ((), ())),
        precision=lax.Precision.HIGHEST, preferred_element_type=F32)
    kern = jnp.concatenate([kern] * 4, axis=1)
    kern = jnp.where(lane // 32 == dil[3], kern, 0.0)
    hi, lo = hi_ref[...], lo_ref[...]
    for j in range(8):
        block = dfi[j * 128:(j + 1) * 128, :]
        out = contract(hi, block, 1, 1) + contract(lo, block, 1, 1)
        for p in range(2):
            stage[pl.ds(2 * j + p, C, stride=STRIDE), :] = out[p * 128:p * 128 + C, :]
    gap = jnp.zeros((BH, 128 - C), F32)
    for g in range(GROUPS):
        out_ref[g, 0:PIECE, :] = stage[g * PIECE:(g + 1) * PIECE, :].astype(BF16)
        own = slice(g * BH, (g + 1) * BH)
        weights = jnp.concatenate([terms[own, :], gap], axis=1)
        out_ref[g, PIECE:, :] = jnp.concatenate([weights, kern], axis=0).astype(BF16)


BLOCK = 512


def by_site(rows_ref, stage, out):
    stage[...] = rows_ref[...].astype(F32)
    for j in range(8):
        for p in range(2):
            cols = slice((2 * j + p) * 128, (2 * j + p + 1) * 128)
            out[:, cols] = pieces(stage, j, p).astype(BF16)


def activation(mb, cb, we, wr):
    root = math.sqrt(2.0 / math.pi)
    pre = contract(we[...], mb, 0, 0)
    d_hidden = contract(wr[...], cb, 0, 0)
    square = pre * pre
    inner = pre * (root + (root * 0.044715) * square)
    half = 0.5 + 0.5 * jnp.tanh(inner)
    hidden = pre * half
    slope = half + hidden * (1.0 - half) * (2.0 * root + (6.0 * root * 0.044715) * square)
    return hidden, (d_hidden * slope).astype(BF16)


def lay_out(c_ref, cot, stage):
    by_site(c_ref, stage, cot)


def middle(m_ref, cot, we, wr, out_ref, stage, mix):
    by_site(m_ref, stage, mix)
    for b in range(2 * L * L // BLOCK):
        cols = slice(b * BLOCK, (b + 1) * BLOCK)
        _, d_pre = activation(mix[:, cols], cot[:, cols], we, wr)
        out = contract(we[...], d_pre, 1, 0)
        for i in range(BLOCK // 128):
            k = b * (BLOCK // 128) + i
            stage[pl.ds(k, C, stride=STRIDE), :] = out[:, i * 128:(i + 1) * 128]
    out_ref[...] = stage[...].astype(BF16)


def weight_terms(core, m_ref, cot, we, wr, keep_ref, send_ref, stage, mix, expand_ref, reduce_ref):
    by_site(m_ref, stage, mix)
    expand_ref[...] = jnp.zeros_like(expand_ref)
    reduce_ref[...] = jnp.zeros_like(reduce_ref)
    for b in range(2 * L * L // BLOCK):
        cols = slice(b * BLOCK, (b + 1) * BLOCK)
        mb, cb = mix[:, cols], cot[:, cols]
        hidden, d_pre = activation(mb, cb, we, wr)
        reduce_ref[...] += contract(hidden.astype(BF16), cb, 1, 1)
        expand_ref[...] += contract(d_pre, mb, 1, 1)
    expand, reduce = expand_ref[...], reduce_ref[...]
    keep_ref[...] = jnp.where(core[0] == 0, expand, reduce)
    send_ref[...] = jnp.where(core[0] == 0, reduce, expand)


def finish(scale, core, mine_ref, other_ref, expand_ref, reduce_ref, kern_ref):
    mine, other = mine_ref[...] * scale, other_ref[...] * scale
    is_first = core[0] == 0
    expand_ref[...] = jnp.where(is_first, mine, other)[0:BH, 0:C]
    reduce_ref[...] = jnp.where(is_first, other, mine)[0:BH, 0:C]
    kern = (mine + other)[BH:, :]
    row = lax.broadcasted_iota(jnp.int32, (4 * CH, C), 0)
    lane = lax.broadcasted_iota(jnp.int32, (4 * CH, C), 1)
    total = jnp.zeros((32, C), F32)
    for i in range(4):
        target = lax.div(row, CH) * (4 * CH) + i * CH + lax.rem(row, CH)
        place = jnp.where(lane == target, 1.0, 0.0)
        total = total + lax.dot_general(
            kern[:, 32 * i:32 * i + 32], place, (((0,), (0,)), ((), ())),
            precision=lax.Precision.HIGHEST, preferred_element_type=F32)
    for t in range(TAPS):
        kern_ref[t] = total[3 * t:3 * t + 3, :]


VMEM = pl.BlockSpec(memory_space=pltpu.VMEM)
SMEM = pl.BlockSpec(memory_space=pltpu.SMEM)
PARAMS = pltpu.CompilerParams(vmem_limit_bytes=28 * 1024 * 1024)


def shape(*dims, dtype=BF16):
    return jax.ShapeDtypeStruct(dims, dtype)


def estimate(flops):
    return pl.CostEstimate(flops=flops, bytes_accessed=4 * 10**6, transcendentals=0)


def run_prepare(scalars, coef, delta):
    return pl.pallas_call(
        prepare,
        out_shape=(shape(256, 256),) * 4,
        in_specs=[SMEM] + [VMEM] * 2,
        out_specs=(VMEM,) * 4,
        compiler_params=PARAMS,
        cost_estimate=estimate(10**8),
        name="prepare",
    )(scalars, coef, delta)


def run_conv_fwd(scalars, rows, coef, hi, lo, eye):
    return pl.pallas_call(
        conv_fwd,
        out_shape=(shape(ROWS, 128), shape(2, 1024, 128), shape(2, 1024, 128), shape(256, 1024)),
        in_specs=[SMEM] + [VMEM] * 5,
        out_specs=(VMEM,) * 4,
        scratch_shapes=[pltpu.VMEM((ROWS, 128), F32), pltpu.VMEM((2, L, L, 128), F32),
                        pltpu.VMEM((2, L, L + 2 * HALO, 128), F32), pltpu.VMEM((1024, 256), BF16)],
        compiler_params=PARAMS,
        cost_estimate=estimate(10**9),
        name="conv_fwd",
    )(scalars, rows, coef, hi, lo, eye)


def run_conv_bwd(scalars, *arrays):
    return pl.pallas_call(
        conv_bwd,
        out_shape=shape(GROUPS, PIECE + BH + 8, 128),
        in_specs=[SMEM] + [VMEM] * len(arrays),
        out_specs=VMEM,
        scratch_shapes=[pltpu.VMEM((ROWS, 128), F32),
                        pltpu.VMEM((2, L, L + 2 * HALO, 128), F32),
                        pltpu.VMEM((2, L, L, 128), F32), pltpu.VMEM((1024, 256), BF16),
                        pltpu.VMEM((32, 8, 128), F32)],
        compiler_params=PARAMS,
        cost_estimate=estimate(10**9),
        name="conv_bwd",
    )(scalars, *arrays)


def site_scratch():
    return [pltpu.VMEM((ROWS, 128), F32), pltpu.VMEM((C, 2048), BF16)]


def run_lay_out(rows):
    return pl.pallas_call(
        lay_out,
        out_shape=shape(C, 2048),
        in_specs=[VMEM],
        out_specs=VMEM,
        scratch_shapes=[pltpu.VMEM((ROWS, 128), F32)],
        compiler_params=PARAMS,
        cost_estimate=estimate(10**8),
        name="lay_out",
    )(rows)


def run_middle(*arrays):
    return pl.pallas_call(
        middle,
        out_shape=shape(ROWS, 128),
        in_specs=[VMEM] * 4,
        out_specs=VMEM,
        scratch_shapes=site_scratch(),
        compiler_params=PARAMS,
        cost_estimate=estimate(10**9),
        name="middle",
    )(*arrays)


def run_weight_terms(core, *arrays):
    return pl.pallas_call(
        weight_terms,
        out_shape=(shape(H, C, dtype=F32),) * 2,
        in_specs=[SMEM] + [VMEM] * 4,
        out_specs=(VMEM,) * 2,
        scratch_shapes=site_scratch() + [pltpu.VMEM((H, C), F32)] * 2,
        compiler_params=PARAMS,
        cost_estimate=estimate(10**9),
        name="weight_terms",
    )(core, *arrays)


def run_finish(scale, core, mine, other):
    return pl.pallas_call(
        functools.partial(finish, scale),
        out_shape=(shape(BH, C, dtype=F32), shape(BH, C, dtype=F32), shape(TAPS, 3, C, dtype=F32)),
        in_specs=[SMEM] + [VMEM] * 2,
        out_specs=(VMEM,) * 3,
        compiler_params=PARAMS,
        cost_estimate=estimate(10**7),
        name="finish",
    )(core, mine, other)


def to_rows(field):
    return field.reshape(C, 2, 8, 128).transpose(0, 2, 1, 3).reshape(ROWS, 128)


def from_rows(rows):
    return rows.reshape(C, 8, 2, 128).transpose(0, 2, 1, 3).reshape(1, C, 2, 1024)


def swap(parts):
    return lax.all_to_all(parts, "pen", 0, 0, tiled=True)


def from_other_core(terms):
    return lax.ppermute(terms, "core", [(0, 1), (1, 0)])


def sum_over_chips(terms):
    size = lax.axis_size("zh") * lax.axis_size("y")
    parts = jnp.broadcast_to(terms.astype(BF16)[None], (size,) + terms.shape)
    return jnp.sum(lax.all_to_all(parts, ("y", "zh"), 0, 0, tiled=True).astype(F32), axis=0)


def per_device(activations, cotangent, depth_kernels, dilations, expand_weight, reduce_weight):
    delta = jnp.asarray(delta_table())
    own = lax.dynamic_slice_in_dim(depth_kernels, lax.axis_index("pen") * CH, CH, 1)
    coef = jnp.tile(own.transpose(0, 2, 1), (1, 1, GROUPS))
    coef = jnp.pad(coef, ((0, 0), (0, 16 - TAPS), (0, 128 - C))).reshape(48, 128)
    group = lax.axis_index("pen").astype(jnp.int32)
    core = lax.axis_index("core").astype(jnp.int32)
    reduce_columns = reduce_weight.T
    scalars = jnp.concatenate([dilations, jnp.mod(group, 4)[None]])

    start = activations.reshape(GROUPS, CH, 2, 8, 128).transpose(0, 1, 3, 2, 4)
    lines = swap(start).reshape(ROWS, 128)
    cot_rows = to_rows(cotangent)
    lines, cot = lax.optimization_barrier((lines, run_lay_out(cot_rows)))
    hi, lo, eye, which = run_prepare(scalars, coef, delta)
    mixed, first, second, field = run_conv_fwd(scalars, lines, coef, hi, lo, eye)
    mixed = swap(mixed.reshape(GROUPS, PIECE, 128)).reshape(ROWS, 128)
    d_mixed = run_middle(mixed, cot, expand_weight, reduce_columns)
    d_lines = swap(d_mixed.reshape(GROUPS, PIECE, 128)).reshape(ROWS, 128)
    keep, send = run_weight_terms(core[None], mixed, cot, expand_weight, reduce_columns)
    terms = keep + from_other_core(send)
    d_conv = run_conv_bwd(scalars, d_lines, coef, hi, lo, which, first, second, field, terms)
    arrived = swap(d_conv)

    weights = jnp.sum(arrived[:, PIECE:PIECE + BH, :].astype(F32), axis=0)
    kern = arrived[:, PIECE + BH:, :].astype(F32).reshape(4, 4, 8, 128)
    kern = jnp.sum(kern, axis=1)[:, :CH, :].reshape(4 * CH, 128)
    mine = sum_over_chips(jnp.concatenate([weights, kern], axis=0))
    d_input = arrived[:, :PIECE, :].reshape(ROWS, 128)
    grad_input = from_rows((cot_rows.astype(F32) + d_input.astype(F32)).astype(BF16))

    samples = lax.axis_size("zh") * lax.axis_size("y") * lax.axis_size("core")
    scale = 1.0 / math.sqrt(samples * L * L * L)
    expand, reduce, kern = run_finish(scale, core[None], mine, from_other_core(mine))
    return grad_input, expand.T, reduce, kern.transpose(1, 2, 0)


def solution(mesh):
    samp = mesh.devices.shape[0]
    split = (2, samp // 4, 2)
    fine = Mesh(mesh.devices.reshape(*split, GROUPS), (*SAMP, "pen"))
    field = P(SAMP, None, "pen", None)
    return jax.shard_map(
        per_device,
        mesh=fine,
        in_specs=(field, field, P(), P(), P(), P()),
        out_specs=(field, P(None, "pen"), P("pen", None), P()),
        check_vma=False,
    )
```

```python
import functools
import math

import jax
import jax.numpy as jnp
import numpy as np
from jax import lax
from jax.experimental import pallas as pl
from jax.experimental.pallas import tpu as pltpu
from jax.sharding import Mesh
from jax.sharding import PartitionSpec as P

C = 96
H = 384
L = 32
TAPS = 9
GROUPS = 16
CH = C // GROUPS
ROWS = C * L * L * 2 // 128
STRIDE = 16
PIECE = ROWS // GROUPS
BH = H // GROUPS
HALO = 16
F32 = jnp.float32
BF16 = jnp.bfloat16
SAMP = ("zh", "y", "core")


def delta_table():
    r = np.arange(256)
    plane, rest = r // 128, r % 128
    x, c = 2 * (rest // CH) + plane, rest % CH
    valid = rest < C
    delta = (x[:, None] - x[None, :]) % L
    same = (c[:, None] == c[None, :]) & valid[:, None] & valid[None, :]
    return np.where(same, delta, -1).astype(np.int32)


def contract(a, b, da, db):
    return lax.dot_general(a, b, (((da,), (db,)), ((), ())), preferred_element_type=F32)


def pieces(stage, j, p):
    return stage[pl.ds(2 * j + p, C, stride=STRIDE), :]


def spread(coef, base):
    return [jnp.broadcast_to(coef[base + t:base + t + 1, :], (8, 128)) for t in range(TAPS)]


def tiles(v):
    return v.reshape(4, 8, 128)


def load_field(stage, j):
    gap = jnp.zeros((128 - C, 128), F32)
    parts = []
    for p in range(2):
        parts += [pieces(stage, j, p), gap]
    return jnp.concatenate(parts, axis=0).astype(BF16)


def put_halo(ref, p, y, v):
    ref[p, y, HALO:HALO + L, :] = v
    ref[p, y, 0:HALO, :] = v[L - HALO:, :]
    ref[p, y, HALO + L:, :] = v[:HALO, :]


def prepare(dil, coef, delta, hi_ref, lo_ref, eye_ref, which_ref):
    spacing = dil[0]
    for half in range(2):
        cols = slice(half * 128, (half + 1) * 128)
        table = delta[:, cols]
        m = jnp.zeros((256, 128), F32)
        which = jnp.full((256, 128), -1.0, F32)
        for t in range(TAPS):
            here = table == (((t - 4) * spacing) & (L - 1))
            m = m + jnp.where(here, coef[t:t + 1, :], 0.0)
            which = jnp.where(here, float(t), which)
        which_ref[:, cols] = which.astype(BF16)
        hi = m.astype(BF16)
        hi_ref[:, cols] = hi
        lo_ref[:, cols] = (m - hi.astype(F32)).astype(BF16)
        eye_ref[:, cols] = jnp.where(table == 0, 1.0, 0.0).astype(BF16)


def conv_fwd(dil, a_ref, coef, hi_ref, lo_ref, eye_ref, mixed_ref, first_ref, second_ref,
             field_ref, stage, fir, sec, mix):
    d1, d2 = dil[1], dil[2]
    stage[...] = a_ref[...].astype(F32)
    hi, lo, eye = hi_ref[...], lo_ref[...], eye_ref[...]
    for j in range(8):
        f = load_field(stage, j)
        field_ref[:, j * 128:(j + 1) * 128] = f
        out = (contract(f, hi, 0, 0) + contract(f, lo, 0, 0)).astype(BF16)
        for p in range(2):
            half = out[:, p * 128:(p + 1) * 128]
            first_ref[p, j * 128:(j + 1) * 128, :] = half
            fir[p, 4 * j:4 * j + 4] = half.astype(F32).reshape(4, L, 128)

    taps = spread(coef, 16)

    @pl.loop(0, L, unroll=4)
    def _(y):
        row = pl.ds(pl.multiple_of(y * L, L), L)
        for p in range(2):
            acc = jnp.zeros((4, 8, 128), F32)
            for t in range(TAPS):
                acc = acc + taps[t] * tiles(fir[p, (y + (t - 4) * d1) & (L - 1)])
            acc = acc.reshape(L, 128).astype(BF16)
            second_ref[p, row, :] = acc
            put_halo(sec, p, y, acc.astype(F32))

    taps_z = spread(coef, 32)

    @pl.loop(0, L, unroll=4)
    def _(y):
        row = pl.ds(pl.multiple_of(y * L, L), L)
        for p in range(2):
            acc = jnp.zeros((4, 8, 128), F32)
            for t in range(TAPS):
                acc = acc + taps_z[t] * tiles(sec[p, y, pl.ds(HALO + (t - 4) * d2, L), :])
            mix[row, p * 128:(p + 1) * 128] = acc.reshape(L, 128).astype(BF16)

    for j in range(8):
        turned = contract(eye, mix[j * 128:(j + 1) * 128, :], 1, 1)
        for p in range(2):
            stage[pl.ds(2 * j + p, C, stride=STRIDE), :] = turned[p * 128:p * 128 + C, :]
    mixed_ref[...] = stage[...].astype(BF16)


def conv_bwd(dil, d_ref, coef, hi_ref, lo_ref, which, first_ref, second_ref, field_ref,
             terms, out_ref, stage, dmh, dse, dfi, acc_ref):
    d1, d2 = dil[1], dil[2]
    stage[...] = d_ref[...].astype(F32)
    eye = jnp.where(which[...].astype(F32) == 4.0, 1.0, 0.0).astype(BF16)
    for j in range(8):
        out = contract(load_field(stage, j), eye, 0, 0)
        for p in range(2):
            for i in range(4):
                put_halo(dmh, p, 4 * j + i, out[i * L:(i + 1) * L, p * 128:(p + 1) * 128])

    def fold(v):
        return (v[0] + v[1]) + (v[2] + v[3])

    taps_z = spread(coef, 32)
    empty = (jnp.zeros((8, 128), F32),) * TAPS

    def along_z(y, sums):
        row = pl.ds(pl.multiple_of(y * L, L), L)
        sums = list(sums)
        for p in range(2):
            field = tiles(second_ref[p, row, :].astype(F32))
            acc = jnp.zeros((4, 8, 128), F32)
            for t in range(TAPS):
                moved = tiles(dmh[p, y, pl.ds(HALO - (t - 4) * d2, L), :])
                acc = acc + taps_z[t] * moved
                sums[t] = sums[t] + fold(moved * field)
            dse[p, y] = acc.reshape(L, 128).astype(BF16).astype(F32)
        return tuple(sums)

    sums = lax.fori_loop(0, L, along_z, empty, unroll=4)
    for t in range(TAPS):
        acc_ref[3 * t + 2] = sums[t]
    taps = spread(coef, 16)

    def along_y(y, sums):
        row = pl.ds(pl.multiple_of(y * L, L), L)
        sums = list(sums)
        for p in range(2):
            field = tiles(first_ref[p, row, :].astype(F32))
            acc = jnp.zeros((4, 8, 128), F32)
            for t in range(TAPS):
                moved = tiles(dse[p, (y - (t - 4) * d1) & (L - 1)])
                acc = acc + taps[t] * moved
                sums[t] = sums[t] + fold(moved * field)
            dfi[row, p * 128:(p + 1) * 128] = acc.reshape(L, 128).astype(BF16)
        return tuple(sums)

    sums = lax.fori_loop(0, L, along_y, empty, unroll=4)
    for t in range(TAPS):
        acc_ref[3 * t + 1] = sums[t]
    for t in range(27, 32):
        acc_ref[t] = jnp.zeros((8, 128), F32)

    cross = contract(field_ref[...], dfi[...], 1, 0)
    tap_of = which[...].astype(F32)
    for t in range(TAPS):
        keep = jnp.where(tap_of == float(t), cross, 0.0)
        keep = jnp.sum(keep.reshape(32, 8, 256), axis=0)
        acc_ref[3 * t] = keep[:, :128] + keep[:, 128:]
    lane = lax.broadcasted_iota(jnp.int32, (8, 128), 1)
    channel = lax.broadcasted_iota(jnp.int32, (8, 128), 0)
    table = jnp.where((lax.rem(lane, CH) == channel) & (lane < C), 1.0, 0.0)
    kern = lax.dot_general(
        table, jnp.sum(acc_ref[...], axis=1), (((1,), (1,)), ((), ())),
        precision=lax.Precision.HIGHEST, preferred_element_type=F32)
    kern = jnp.concatenate([kern] * 4, axis=1)
    kern = jnp.where(lane // 32 == dil[3], kern, 0.0)
    hi, lo = hi_ref[...], lo_ref[...]
    for j in range(8):
        block = dfi[j * 128:(j + 1) * 128, :]
        out = contract(hi, block, 1, 1) + contract(lo, block, 1, 1)
        for p in range(2):
            stage[pl.ds(2 * j + p, C, stride=STRIDE), :] = out[p * 128:p * 128 + C, :]
    gap = jnp.zeros((BH, 128 - C), F32)
    for g in range(GROUPS):
        out_ref[g, 0:PIECE, :] = stage[g * PIECE:(g + 1) * PIECE, :].astype(BF16)
        own = slice(g * BH, (g + 1) * BH)
        weights = jnp.concatenate([terms[own, :], gap], axis=1)
        out_ref[g, PIECE:, :] = jnp.concatenate([weights, kern], axis=0).astype(BF16)


BLOCK = 512


def by_site(rows_ref, stage, out):
    stage[...] = rows_ref[...].astype(F32)
    for j in range(8):
        for p in range(2):
            cols = slice((2 * j + p) * 128, (2 * j + p + 1) * 128)
            out[:, cols] = pieces(stage, j, p).astype(BF16)


def activation(mb, cb, we, wr):
    root = math.sqrt(2.0 / math.pi)
    pre = contract(we[...], mb, 0, 0)
    d_hidden = contract(wr[...], cb, 0, 0)
    square = pre * pre
    inner = pre * (root + (root * 0.044715) * square)
    half = 0.5 + 0.5 * jnp.tanh(inner)
    hidden = pre * half
    slope = half + hidden * (1.0 - half) * (2.0 * root + (6.0 * root * 0.044715) * square)
    return hidden, (d_hidden * slope).astype(BF16)


def lay_out(c_ref, cot, stage):
    by_site(c_ref, stage, cot)


def middle(m_ref, cot, we, wr, out_ref, stage, mix):
    by_site(m_ref, stage, mix)
    for b in range(2 * L * L // BLOCK):
        cols = slice(b * BLOCK, (b + 1) * BLOCK)
        _, d_pre = activation(mix[:, cols], cot[:, cols], we, wr)
        out = contract(we[...], d_pre, 1, 0)
        for i in range(BLOCK // 128):
            k = b * (BLOCK // 128) + i
            stage[pl.ds(k, C, stride=STRIDE), :] = out[:, i * 128:(i + 1) * 128]
    out_ref[...] = stage[...].astype(BF16)


def weight_terms(core, m_ref, cot, we, wr, keep_ref, send_ref, stage, mix, expand_ref, reduce_ref):
    by_site(m_ref, stage, mix)
    expand_ref[...] = jnp.zeros_like(expand_ref)
    reduce_ref[...] = jnp.zeros_like(reduce_ref)
    for b in range(2 * L * L // BLOCK):
        cols = slice(b * BLOCK, (b + 1) * BLOCK)
        mb, cb = mix[:, cols], cot[:, cols]
        hidden, d_pre = activation(mb, cb, we, wr)
        reduce_ref[...] += contract(hidden.astype(BF16), cb, 1, 1)
        expand_ref[...] += contract(d_pre, mb, 1, 1)
    expand, reduce = expand_ref[...], reduce_ref[...]
    keep_ref[...] = jnp.where(core[0] == 0, expand, reduce)
    send_ref[...] = jnp.where(core[0] == 0, reduce, expand)


def finish(scale, core, mine_ref, other_ref, expand_ref, reduce_ref, kern_ref):
    mine, other = mine_ref[...] * scale, other_ref[...] * scale
    is_first = core[0] == 0
    expand_ref[...] = jnp.where(is_first, mine, other)[0:BH, 0:C]
    reduce_ref[...] = jnp.where(is_first, other, mine)[0:BH, 0:C]
    kern = (mine + other)[BH:, :]
    row = lax.broadcasted_iota(jnp.int32, (4 * CH, C), 0)
    lane = lax.broadcasted_iota(jnp.int32, (4 * CH, C), 1)
    total = jnp.zeros((32, C), F32)
    for i in range(4):
        target = lax.div(row, CH) * (4 * CH) + i * CH + lax.rem(row, CH)
        place = jnp.where(lane == target, 1.0, 0.0)
        total = total + lax.dot_general(
            kern[:, 32 * i:32 * i + 32], place, (((0,), (0,)), ((), ())),
            precision=lax.Precision.HIGHEST, preferred_element_type=F32)
    for t in range(TAPS):
        kern_ref[t] = total[3 * t:3 * t + 3, :]


VMEM = pl.BlockSpec(memory_space=pltpu.VMEM)
SMEM = pl.BlockSpec(memory_space=pltpu.SMEM)
PARAMS = pltpu.CompilerParams(vmem_limit_bytes=28 * 1024 * 1024)


def shape(*dims, dtype=BF16):
    return jax.ShapeDtypeStruct(dims, dtype)


def estimate(flops):
    return pl.CostEstimate(flops=flops, bytes_accessed=4 * 10**6, transcendentals=0)


def run_prepare(scalars, coef, delta):
    return pl.pallas_call(
        prepare,
        out_shape=(shape(256, 256),) * 4,
        in_specs=[SMEM] + [VMEM] * 2,
        out_specs=(VMEM,) * 4,
        compiler_params=PARAMS,
        cost_estimate=estimate(10**8),
        name="prepare",
    )(scalars, coef, delta)


def run_conv_fwd(scalars, rows, coef, hi, lo, eye):
    return pl.pallas_call(
        conv_fwd,
        out_shape=(shape(ROWS, 128), shape(2, 1024, 128), shape(2, 1024, 128), shape(256, 1024)),
        in_specs=[SMEM] + [VMEM] * 5,
        out_specs=(VMEM,) * 4,
        scratch_shapes=[pltpu.VMEM((ROWS, 128), F32), pltpu.VMEM((2, L, L, 128), F32),
                        pltpu.VMEM((2, L, L + 2 * HALO, 128), F32), pltpu.VMEM((1024, 256), BF16)],
        compiler_params=PARAMS,
        cost_estimate=estimate(10**9),
        name="conv_fwd",
    )(scalars, rows, coef, hi, lo, eye)


def run_conv_bwd(scalars, *arrays):
    return pl.pallas_call(
        conv_bwd,
        out_shape=shape(GROUPS, PIECE + BH + 8, 128),
        in_specs=[SMEM] + [VMEM] * len(arrays),
        out_specs=VMEM,
        scratch_shapes=[pltpu.VMEM((ROWS, 128), F32),
                        pltpu.VMEM((2, L, L + 2 * HALO, 128), F32),
                        pltpu.VMEM((2, L, L, 128), F32), pltpu.VMEM((1024, 256), BF16),
                        pltpu.VMEM((32, 8, 128), F32)],
        compiler_params=PARAMS,
        cost_estimate=estimate(10**9),
        name="conv_bwd",
    )(scalars, *arrays)


def site_scratch():
    return [pltpu.VMEM((ROWS, 128), F32), pltpu.VMEM((C, 2048), BF16)]


def run_lay_out(rows):
    return pl.pallas_call(
        lay_out,
        out_shape=shape(C, 2048),
        in_specs=[VMEM],
        out_specs=VMEM,
        scratch_shapes=[pltpu.VMEM((ROWS, 128), F32)],
        compiler_params=PARAMS,
        cost_estimate=estimate(10**8),
        name="lay_out",
    )(rows)


def run_middle(*arrays):
    return pl.pallas_call(
        middle,
        out_shape=shape(ROWS, 128),
        in_specs=[VMEM] * 4,
        out_specs=VMEM,
        scratch_shapes=site_scratch(),
        compiler_params=PARAMS,
        cost_estimate=estimate(10**9),
        name="middle",
    )(*arrays)


def run_weight_terms(core, *arrays):
    return pl.pallas_call(
        weight_terms,
        out_shape=(shape(H, C, dtype=F32),) * 2,
        in_specs=[SMEM] + [VMEM] * 4,
        out_specs=(VMEM,) * 2,
        scratch_shapes=site_scratch() + [pltpu.VMEM((H, C), F32)] * 2,
        compiler_params=PARAMS,
        cost_estimate=estimate(10**9),
        name="weight_terms",
    )(core, *arrays)


def run_finish(scale, core, mine, other):
    return pl.pallas_call(
        functools.partial(finish, scale),
        out_shape=(shape(BH, C, dtype=F32), shape(BH, C, dtype=F32), shape(TAPS, 3, C, dtype=F32)),
        in_specs=[SMEM] + [VMEM] * 2,
        out_specs=(VMEM,) * 3,
        compiler_params=PARAMS,
        cost_estimate=estimate(10**7),
        name="finish",
    )(core, mine, other)


def to_rows(field):
    return field.reshape(C, 2, 8, 128).transpose(0, 2, 1, 3).reshape(ROWS, 128)


def from_rows(rows):
    return rows.reshape(C, 8, 2, 128).transpose(0, 2, 1, 3).reshape(1, C, 2, 1024)


def swap(parts):
    return lax.all_to_all(parts, "pen", 0, 0, tiled=True)


def from_other_core(terms):
    return lax.ppermute(terms, "core", [(0, 1), (1, 0)])


def sum_over_chips(terms):
    size = lax.axis_size("zh") * lax.axis_size("y")
    parts = jnp.broadcast_to(terms.astype(BF16)[None], (size,) + terms.shape)
    return jnp.sum(lax.all_to_all(parts, ("zh", "y"), 0, 0, tiled=True).astype(F32), axis=0)


def per_device(activations, cotangent, depth_kernels, dilations, expand_weight, reduce_weight):
    delta = jnp.asarray(delta_table())
    own = lax.dynamic_slice_in_dim(depth_kernels, lax.axis_index("pen") * CH, CH, 1)
    coef = jnp.tile(own.transpose(0, 2, 1), (1, 1, GROUPS))
    coef = jnp.pad(coef, ((0, 0), (0, 16 - TAPS), (0, 128 - C))).reshape(48, 128)
    group = lax.axis_index("pen").astype(jnp.int32)
    core = lax.axis_index("core").astype(jnp.int32)
    reduce_columns = reduce_weight.T
    scalars = jnp.concatenate([dilations, jnp.mod(group, 4)[None]])

    start = activations.reshape(GROUPS, CH, 2, 8, 128).transpose(0, 1, 3, 2, 4)
    lines = swap(start).reshape(ROWS, 128)
    cot_rows = to_rows(cotangent)
    lines, cot = lax.optimization_barrier((lines, run_lay_out(cot_rows)))
    hi, lo, eye, which = run_prepare(scalars, coef, delta)
    mixed, first, second, field = run_conv_fwd(scalars, lines, coef, hi, lo, eye)
    mixed = swap(mixed.reshape(GROUPS, PIECE, 128)).reshape(ROWS, 128)
    d_mixed = run_middle(mixed, cot, expand_weight, reduce_columns)
    d_lines = swap(d_mixed.reshape(GROUPS, PIECE, 128)).reshape(ROWS, 128)
    keep, send = run_weight_terms(core[None], mixed, cot, expand_weight, reduce_columns)
    terms = keep + from_other_core(send)
    d_conv = run_conv_bwd(scalars, d_lines, coef, hi, lo, which, first, second, field, terms)
    arrived = swap(d_conv)

    weights = jnp.sum(arrived[:, PIECE:PIECE + BH, :].astype(F32), axis=0)
    kern = arrived[:, PIECE + BH:, :].astype(F32).reshape(4, 4, 8, 128)
    kern = jnp.sum(kern, axis=1)[:, :CH, :].reshape(4 * CH, 128)
    mine = sum_over_chips(jnp.concatenate([weights, kern], axis=0))
    d_input = arrived[:, :PIECE, :].reshape(ROWS, 128)
    grad_input = from_rows((cot_rows.astype(F32) + d_input.astype(F32)).astype(BF16))

    samples = lax.axis_size("zh") * lax.axis_size("y") * lax.axis_size("core")
    scale = 1.0 / math.sqrt(samples * L * L * L)
    expand, reduce, kern = run_finish(scale, core[None], mine, from_other_core(mine))
    return grad_input, expand.T, reduce, kern.transpose(1, 2, 0)


def solution(mesh):
    samp = mesh.devices.shape[0]
    split = (2, samp // 4, 2)
    fine = Mesh(mesh.devices.reshape(*split, GROUPS), (*SAMP, "pen"))
    field = P(SAMP, None, "pen", None)
    return jax.shard_map(
        per_device,
        mesh=fine,
        in_specs=(field, field, P(), P(), P(), P()),
        out_specs=(field, P(None, "pen"), P("pen", None), P()),
        check_vma=False,
    )
```
